512 devices in a mesh: lon: 64 (over y, z_lo, core), lat: 8 (over x, z_hi).
Axes of the slice: x: 4, y: 4, z: 16 (z_hi: 2, z_lo: 8; z = z_hi * 8 + z_lo), core: 2. Of those that a mesh axis runs over, the one named last changes fastest.
Arguments:
- tokens: bfloat16 [48, 768, 384], P('lat', 'lon'), may hold values from -6 to 6
- kinds: int32 [48, 768, 2], P('lat', 'lon'), may hold values from 0 to 15
- kind_embed: bfloat16 [16, 192], replicated, may hold values from -3 to 3
- pair_index: int32 [144, 144], replicated, may hold values from 0 to 3311
- bias_table: float32 [8, 6, 3312], P('lat'), may hold values from -4 to 4
- attn_gain: float32 [192], replicated, may hold values from 0.3 to 4
- mlp_gain: float32 [192], replicated, may hold values from 0.3 to 4
- mix_weight: bfloat16 [192, 576], replicated, may hold values from -0.4375 to 0.4375
- out_weight: bfloat16 [192, 192], replicated, may hold values from -0.4375 to 0.4375
- up_weight: bfloat16 [192, 768], replicated, may hold values from -0.4375 to 0.4375
- down_weight: bfloat16 [768, 192], replicated, may hold values from -0.21875 to 0.21875
- cotangent: bfloat16 [48, 768, 384], P('lat', 'lon'), may hold values from -8 to 8
Outputs:
- token_grad: bfloat16 [48, 768, 384], P('lat', 'lon')
- mix_grad: float32 [192, 576], P('lon')
- out_grad: float32 [192, 192], P('lon')
- up_grad: float32 [192, 768], P('lon')
- down_grad: float32 [768, 192], P('lon')
- gain_grad: float32 [2, 192], P(None, 'lon')
- embed_grad: float32 [16, 192], P(None, 'lon')
- bias_grad: float32 [8, 6, 3312], P('lat')
The draws below stay inside these ranges and needn't reach their ends.
All inputs are finite; a program needn't handle non-finite values.
Results may differ from the reference program's by a relative error of at most 0.012.
The reference program's roundings to bfloat16 on the way count: a program that leaves them out, or rounds other values in their place, can miss the bound.
Values may be sent and summed in bfloat16 or wider, within the bound.
A program may use at most 64 MiB of HBM per device.

```python
import jax
import jax.numpy as jnp
from jax import lax

C = 192
HEADS = 6
FF = 768
LEVELS = 2
WIN_LAT = 6
WIN_LON = 12
KINDS = 16
WIN = 144
PAIRS = 3312
NLAT = 48
NLON = 768
NLATW = 8


def draw_cotangent(key, part):
    key = jax.random.fold_in(key, 7)
    columns = jnp.arange(NLON, dtype=jnp.float32) / NLON
    base = jax.random.truncated_normal(key, -4.0, 4.0, (NLAT, NLON, LEVELS * C), jnp.float32)
    ramp = 1.0 + columns
    return (base * ramp[None, :, None]).astype(jnp.bfloat16)


def rising_gain(key, start, growth, rough):
    place = jnp.arange(C, dtype=jnp.float32) / max(C - 1, 1)
    factor = jax.random.uniform(key, (C,), jnp.float32, 1.0 - rough, 1.0 + rough)
    return start * jnp.exp(place * jnp.log(growth)) * factor


def draw_attn_gain(key, part):
    key = jax.random.fold_in(key, 11)
    return rising_gain(key, 0.5, 4.0, 0.2)


def draw_mlp_gain(key, part):
    key = jax.random.fold_in(key, 13)
    return rising_gain(key, 0.5, 4.0, 0.2)


def set_ends(array, key, smallest, high):
    index_at = [jax.random.randint(jax.random.fold_in(key, axis), (), 0, length) for axis, length in enumerate(array.shape)]
    main_axis = array.shape.index(max(array.shape))
    beside = index_at[:main_axis] + [(index_at[main_axis] + 1) % array.shape[main_axis]] + index_at[main_axis + 1:]
    return array.at[tuple(index_at)].set(smallest).at[tuple(beside)].set(high)


def level_of(stream_key, shape, pieces, least, largest):
    def one(axis_at, blocks):
        heights = jax.random.uniform(jax.random.fold_in(jax.random.fold_in(stream_key, 6), axis_at), (blocks,), jnp.float32, least / len(pieces), largest / len(pieces))
        return jnp.repeat(jnp.exp(heights), shape[axis_at] // blocks).reshape((-1,) + (1,) * (len(shape) - axis_at - 1))

    factor_of = one(*pieces[0])
    for cut in pieces[1:]:
        factor_of = factor_of * one(*cut)
    return factor_of


def noise(rng, shape, deviation, reach, cuts=(), kind=jnp.bfloat16):
    array = deviation * jax.random.normal(rng, shape, jnp.float32)
    if cuts:
        array = array * level_of(rng, shape, cuts, -0.22, 0.18)
    return jnp.clip(array, -reach, reach).astype(kind)


def setup_inputs(seed: int = 0) -> dict:
    seeds = jax.random.split(jax.random.key(seed), 13)
    tokens = noise(seeds[0], (NLAT, NLON, LEVELS * C), 1.0, 6.0, ((0, 8), (1, 64)))
    kinds = set_ends(jax.random.randint(seeds[1], (NLAT, NLON, LEVELS), 0, KINDS), jax.random.fold_in(seeds[1], 1), 0, KINDS - 1).astype(jnp.int32)
    kind_embed = noise(seeds[2], (KINDS, C), 0.5, 3.0)
    pair_index = set_ends(jax.random.randint(seeds[3], (WIN, WIN), 0, PAIRS), jax.random.fold_in(seeds[3], 1), 0, PAIRS - 1).astype(jnp.int32)
    bias_table = noise(seeds[4], (NLATW, HEADS, PAIRS), 1.0, 4.0, ((0, 8),), jnp.float32)
    attn_gain = draw_attn_gain(jax.random.fold_in(seeds[12], 71), 0)
    mlp_gain = draw_mlp_gain(jax.random.fold_in(seeds[12], 71), 0)
    mix_weight = noise(seeds[7], (C, 3 * C), C ** -0.5, 0.4375)
    out_weight = noise(seeds[8], (C, C), C ** -0.5, 0.4375)
    up_weight = noise(seeds[9], (C, FF), C ** -0.5, 0.4375)
    down_weight = noise(seeds[10], (FF, C), FF ** -0.5, 0.21875)
    cotangent = draw_cotangent(jax.random.fold_in(seeds[12], 71), 0)
    return dict(tokens=tokens, kinds=kinds, kind_embed=kind_embed, pair_index=pair_index, bias_table=bias_table, attn_gain=attn_gain, mlp_gain=mlp_gain, mix_weight=mix_weight, out_weight=out_weight, up_weight=up_weight, down_weight=down_weight, cotangent=cotangent)


NORM_EPS = 1e-05
RMS_EPS = 1e-06
GELU_SQRT = 0.7978845608028654
GELU_CUBE = 0.044715

def layer_norm(values, gain):
    centre_val = lax.optimization_barrier(jnp.mean(values, axis=-1, keepdims=True))
    centred = values - centre_val
    inverse = lax.rsqrt(lax.optimization_barrier(jnp.mean(centred * centred, axis=-1, keepdims=True)) + NORM_EPS)
    normed = centred * inverse
    return (normed * gain, normed, inverse)

def norm_backward(upstream, normed, inverse, gain):
    scaled = upstream * gain
    result = inverse * (scaled - lax.optimization_barrier(jnp.mean(scaled, axis=-1, keepdims=True)) - normed * lax.optimization_barrier(jnp.mean(scaled * normed, axis=-1, keepdims=True)))
    return (result, lax.optimization_barrier(jnp.sum(upstream * normed, axis=(0, 1))))

def gelu_parts(inner):
    tangent = jnp.tanh(GELU_SQRT * (inner + GELU_CUBE * inner * inner * inner))
    activated = 0.5 * inner * (1.0 + tangent)
    derivative = 0.5 * (1.0 + tangent) + 0.5 * inner * (1.0 - tangent * tangent) * GELU_SQRT * (1.0 + 3.0 * GELU_CUBE * inner * inner)
    return (activated, derivative)

def window_backward(stored, upstream, groups, bias_dense, weights):
    mix_weight, out_weight, up_weight, down_weight, attn_gain, mlp_gain = weights
    window_count, win_size, channels = stored.shape
    head_count = bias_dense.shape[1]
    head_size = channels // head_count
    score_scale = head_size ** (-0.5)
    shaped = (window_count, win_size, head_count, head_size)
    residual_in = stored.astype(jnp.float32)
    normed_one, hat_one, inv_one = layer_norm(residual_in, attn_gain)
    first_in = normed_one.astype(jnp.bfloat16)
    mixed = jnp.einsum('nwc,cd->nwd', first_in, mix_weight, preferred_element_type=jnp.float32).astype(jnp.bfloat16)
    queries = mixed[..., :channels].reshape(shaped)
    key_rows = mixed[..., channels:2 * channels].reshape(shaped)
    value_rows = mixed[..., 2 * channels:].reshape(shaped)
    scores = jnp.einsum('nqhd,nkhd->nhqk', queries, key_rows, preferred_element_type=jnp.float32) * score_scale + bias_dense
    allowed = groups[:, None, :, None] == groups[:, None, None, :]
    expon = jnp.where(allowed, jnp.exp(scores), 0.0)
    attend = expon / lax.optimization_barrier(jnp.sum(expon, axis=-1, keepdims=True))
    attend_low = attend.astype(jnp.bfloat16)
    context = jnp.einsum('nhqk,nkhd->nqhd', attend_low, value_rows, preferred_element_type=jnp.float32).astype(jnp.bfloat16).reshape(window_count, win_size, channels)
    residual_mid = residual_in + jnp.einsum('nwc,cd->nwd', context, out_weight, preferred_element_type=jnp.float32)
    normed_two, hat_two, inv_two = layer_norm(residual_mid, mlp_gain)
    second_in = normed_two.astype(jnp.bfloat16)
    hidden_pre = jnp.einsum('nwc,cf->nwf', second_in, up_weight, preferred_element_type=jnp.float32)
    hidden_act, hidden_slope = gelu_parts(hidden_pre)
    hidden_low = hidden_act.astype(jnp.bfloat16)
    down_grad = jnp.einsum('nwf,nwc->fc', hidden_low, upstream, preferred_element_type=jnp.float32)
    hidden_grad = (jnp.einsum('nwc,fc->nwf', upstream, down_weight, preferred_element_type=jnp.float32) * hidden_slope).astype(jnp.bfloat16)
    up_grad = jnp.einsum('nwc,nwf->cf', second_in, hidden_grad, preferred_element_type=jnp.float32)
    second_grad = jnp.einsum('nwf,cf->nwc', hidden_grad, up_weight, preferred_element_type=jnp.float32)
    mid_back, mlp_gain_grad = norm_backward(second_grad, hat_two, inv_two, mlp_gain)
    mid_grad = upstream.astype(jnp.float32) + mid_back
    mid_low = mid_grad.astype(jnp.bfloat16)
    out_grad = jnp.einsum('nwc,nwd->cd', context, mid_low, preferred_element_type=jnp.float32)
    context_grad = jnp.einsum('nwd,cd->nwc', mid_low, out_weight, preferred_element_type=jnp.float32).astype(jnp.bfloat16).reshape(shaped)
    attend_grad = jnp.einsum('nqhd,nkhd->nhqk', context_grad, value_rows, preferred_element_type=jnp.float32)
    value_grad = jnp.einsum('nhqk,nqhd->nkhd', attend_low, context_grad, preferred_element_type=jnp.float32).astype(jnp.bfloat16)
    score_grad = attend * (attend_grad - lax.optimization_barrier(jnp.sum(attend * attend_grad, axis=-1, keepdims=True)))
    score_low = score_grad.astype(jnp.bfloat16)
    query_grad = (jnp.einsum('nhqk,nkhd->nqhd', score_low, key_rows, preferred_element_type=jnp.float32) * score_scale).astype(jnp.bfloat16)
    key_grad = (jnp.einsum('nhqk,nqhd->nkhd', score_low, queries, preferred_element_type=jnp.float32) * score_scale).astype(jnp.bfloat16)
    flat_shape = (window_count, win_size, channels)
    mixed_grad = jnp.concatenate([query_grad.reshape(flat_shape), key_grad.reshape(flat_shape), value_grad.reshape(flat_shape)], axis=-1)
    mix_grad = jnp.einsum('nwc,nwd->cd', first_in, mixed_grad, preferred_element_type=jnp.float32)
    first_grad = jnp.einsum('nwd,cd->nwc', mixed_grad, mix_weight, preferred_element_type=jnp.float32)
    in_back, attn_gain_grad = norm_backward(first_grad, hat_one, inv_one, attn_gain)
    moved_grad = mid_grad + in_back
    return (moved_grad, score_grad, (mix_grad, out_grad, up_grad, down_grad, attn_gain_grad, mlp_gain_grad))

def to_windows(grid, channels):
    lat_rows, lon_cols, flat = grid.shape
    levels = flat // channels
    shaped = grid.reshape(lat_rows // WIN_LAT, WIN_LAT, lon_cols // WIN_LON, WIN_LON, levels, channels)
    return shaped.transpose(0, 2, 1, 3, 4, 5).reshape(lat_rows // WIN_LAT, lon_cols // WIN_LON, WIN_LAT * WIN_LON * levels, channels)

def from_windows(windows, lat_rows, lon_cols, channels):
    levels = windows.shape[-2] // (WIN_LAT * WIN_LON)
    shaped = windows.reshape(lat_rows // WIN_LAT, lon_cols // WIN_LON, WIN_LAT, WIN_LON, levels, channels)
    return shaped.transpose(0, 2, 1, 3, 4, 5).reshape(lat_rows, lon_cols, levels * channels)

def reference(tokens, kinds, kind_embed, pair_index, bias_table, attn_gain, mlp_gain, mix_weight, out_weight, up_weight, down_weight, cotangent):
    lat_total, lon_total, flat = tokens.shape
    channels = mix_weight.shape[0]
    levels = flat // channels
    lat_wins = lat_total // WIN_LAT
    lon_wins = lon_total // WIN_LON
    head_count = bias_table.shape[1]
    embedded = kind_embed[kinds].astype(jnp.float32).reshape(lat_total, lon_total, flat)
    stored = (tokens.astype(jnp.float32) + embedded).astype(jnp.bfloat16)
    offsets = (-(WIN_LAT // 2), -(WIN_LON // 2))
    win_in = to_windows(jnp.roll(stored, offsets, (0, 1)), channels)
    win_up = to_windows(jnp.roll(cotangent, offsets, (0, 1)), channels)
    bias_dense = bias_table[:, :, pair_index]
    weights = (mix_weight, out_weight, up_weight, down_weight, attn_gain, mlp_gain)

    def one_band(band):
        lat_rows = band * WIN_LAT + jnp.arange(WIN_LAT, dtype=jnp.int32) + WIN_LAT // 2
        row_group = (lat_rows >= lat_total).astype(jnp.int32)
        groups = jnp.broadcast_to(row_group[:, None, None], (WIN_LAT, WIN_LON, levels)).reshape(1, WIN_LAT * WIN_LON * levels)
        groups = jnp.broadcast_to(groups, (lon_wins, WIN_LAT * WIN_LON * levels))
        moved_grad, score_grad, grads = window_backward(win_in[band], win_up[band], groups, bias_dense[band][None], weights)
        return (moved_grad, lax.optimization_barrier(jnp.sum(score_grad, axis=0)), grads)
    moved_grad, score_sum, grads = lax.map(one_band, jnp.arange(lat_wins, dtype=jnp.int32))
    grads = tuple((lax.optimization_barrier(jnp.sum(stacked, axis=0)) for stacked in grads))
    grid_grad = jnp.roll(from_windows(moved_grad, lat_total, lon_total, channels), (WIN_LAT // 2, WIN_LON // 2), (0, 1))
    win_size = pair_index.shape[0]
    pair_rows = score_sum.reshape(lat_wins * head_count, win_size * win_size).T
    bias_sum = jax.ops.segment_sum(pair_rows, pair_index.reshape(-1), num_segments=PAIRS)
    bias_part = bias_sum.T.reshape(lat_wins, head_count, PAIRS)
    kind_hot = (kinds[..., None] == jnp.arange(KINDS, dtype=jnp.int32)).astype(jnp.float32)
    embed_part = jnp.einsum('abln,ablc->nc', kind_hot, grid_grad.reshape(lat_total, lon_total, levels, channels), precision=lax.Precision.HIGHEST)
    gain_pair = jnp.stack([grads[4], grads[5]])
    dense = (grads[0], grads[1], grads[2], grads[3], gain_pair, embed_part)
    total_sq = sum((jnp.sum(item * item) for item in dense)) + jnp.sum(bias_part * bias_part)
    param_total = sum((item.size for item in dense)) + bias_part.size
    factor = lax.rsqrt(total_sq / param_total + RMS_EPS)
    return (grid_grad.astype(jnp.bfloat16), grads[0] * factor, grads[1] * factor, grads[2] * factor, grads[3] * factor, gain_pair * factor, embed_part * factor, bias_part * factor)
```

```python
import jax
import jax.numpy as jnp
import numpy as np
from jax import lax
from jax.experimental import pallas as pl
from jax.experimental.pallas import tpu as pltpu
from jax.sharding import PartitionSpec as P

F32 = jnp.float32
BF16 = jnp.bfloat16
MESH = pl.DeviceIdType.MESH

C = 192
HEADS = 6
HEAD = 32
FF = 768
WIN_LAT = 6
WIN_LON = 12
KINDS = 16
PAIRS = 3312
TOK = 144
CELLS = 18
PART = 36
LANES = 128
HI = 26
COLS = 2304
TILES = 18
NORM_EPS = 1e-05
RMS_EPS = 1e-06
GELU_SQRT = 0.7978845608028654
GELU_CUBE = 0.044715
LON, LAT = 64, 8
ZLO = 8
VMEM_LIMIT = 56 * 1024 * 1024


def place():
    lon, lat = lax.axis_index("lon"), lax.axis_index("lat")
    return lat // 2, lon // 16, (lat % 2) * ZLO + (lon // 2) % ZLO, lon % 2


def at(x, y, z, core):
    return {"lon": y * 16 + (z % ZLO) * 2 + core, "lat": x * 2 + z // ZLO}


def dot(a, b):
    return lax.dot_general(a, b, (((1,), (0,)), ((), ())), preferred_element_type=F32)


def dot_nt(a, b):
    return lax.dot_general(a, b, (((1,), (1,)), ((), ())), preferred_element_type=F32)


def dot_tn(a, b):
    return lax.dot_general(a, b, (((0,), (0,)), ((), ())), preferred_element_type=F32)


def two_terms(v):
    high = v.astype(BF16)
    return high, (v - high.astype(F32)).astype(BF16)


def halo_kernel(tok_ref, kind_ref, embed_ref, cot_ref, out_ref, tok_s, kind_s, flat_s, send, recv, send_sem, recv_sem):
    lon, lat = lax.axis_index("lon"), lax.axis_index("lat")
    barrier = pltpu.get_barrier_semaphore()
    for dr, dc in ((1, 0), (0, 1), (1, 1)):
        for sign in (1, -1):
            pl.semaphore_signal(
                barrier,
                inc=1,
                device_id={"lon": (lon + sign * dc + LON) % LON, "lat": (lat + sign * dr + LAT) % LAT},
                device_id_type=MESH,
            )
    embed = embed_ref[...].astype(F32)
    blank = jnp.zeros((KINDS, C), F32)
    wide = jnp.concatenate(
        [jnp.concatenate([embed, blank], axis=1), jnp.concatenate([blank, embed], axis=1)], axis=0
    ).astype(BF16)
    for row in range(WIN_LAT):
        tok = tok_ref[row].astype(F32)
        cot = cot_ref[row].astype(F32)
        kind = kind_ref[row]
        for half in range(2):
            quarter = 2 * (row // 3) + half
            start = 6 * (row % 3)
            cells = slice(6 * half, 6 * half + 6)
            tok_s[quarter, start : start + 6, :] = tok[cells]
            flat_s[quarter, CELLS + start : CELLS + start + 6, :] = cot[cells]
            kind_s[quarter, start : start + 6, :] = kind[cells]
    column = lax.broadcasted_iota(jnp.int32, (24, 32), 1)
    lane = lax.broadcasted_iota(jnp.int32, (24, LANES), 1)
    sub = lax.broadcasted_iota(jnp.int32, (24, LANES), 0)
    for quarter in range(4):
        kinds = kind_s[quarter]
        first, second = kinds[:, 0:1], kinds[:, 1:2]
        hot = jnp.where((column == first) | (column == second + KINDS), 1.0, 0.0).astype(BF16)
        stored = tok_s[quarter] + dot(hot, wide)
        flat_s[quarter, 0:CELLS, :] = stored[0:CELLS]
        valid = sub < CELLS
        row = jnp.where(valid & (lane == sub), first.astype(F32), 0.0) + jnp.where(
            valid & (lane == sub + CELLS), second.astype(F32), 0.0
        )
        flat_s[quarter, 36:48, :] = jnp.zeros((12, 2 * C), F32)
        flat_s[quarter, 36:37, 0:LANES] = jnp.sum(row, axis=0, keepdims=True)
        send[quarter] = flat_s[quarter].astype(BF16)
    pl.semaphore_wait(barrier, 6)
    copies = []
    for slot in (3, 2, 1):
        dr, dc = slot // 2, slot % 2
        copy = pltpu.make_async_remote_copy(
            src_ref=send.at[3 - slot],
            dst_ref=recv.at[slot],
            send_sem=send_sem.at[slot],
            recv_sem=recv_sem.at[slot],
            device_id={"lon": (lon - dc + LON) % LON, "lat": (lat - dr + LAT) % LAT},
            device_id_type=MESH,
        )
        copy.start()
        copies.append(copy)
    out_ref[0] = send[3]
    for slot, copy in zip((3, 2, 1), copies):
        copy.wait_recv()
        out_ref[slot] = recv[slot]
    for copy in copies:
        copy.wait_send()


def halo(tokens, kinds, kind_embed, cotangent):
    return pl.pallas_call(
        halo_kernel,
        out_shape=jax.ShapeDtypeStruct((4, 48, 2 * C), BF16),
        in_specs=[pl.BlockSpec(memory_space=pltpu.VMEM)] * 4,
        out_specs=pl.BlockSpec(memory_space=pltpu.VMEM),
        scratch_shapes=[
            pltpu.VMEM((4, 24, 2 * C), F32),
            pltpu.VMEM((4, 24, 2), jnp.int32),
            pltpu.VMEM((4, 48, 2 * C), F32),
            pltpu.VMEM((4, 48, 2 * C), BF16),
            pltpu.VMEM((4, 48, 2 * C), BF16),
            pltpu.SemaphoreType.DMA((4,)),
            pltpu.SemaphoreType.DMA((4,)),
        ],
        compiler_params=pltpu.CompilerParams(collective_id=0, has_side_effects=True, vmem_limit_bytes=VMEM_LIMIT),
        name="halo_in",
    )(tokens, kinds, kind_embed, cotangent)


def layer_norm(values, gain):
    centred = values - jnp.mean(values, axis=-1, keepdims=True)
    inverse = lax.rsqrt(jnp.mean(centred * centred, axis=-1, keepdims=True) + NORM_EPS)
    normed = centred * inverse
    return normed * gain, normed, inverse


def norm_backward(upstream, normed, inverse, gain):
    scaled = upstream * gain
    return inverse * (
        scaled
        - jnp.mean(scaled, axis=-1, keepdims=True)
        - normed * jnp.mean(scaled * normed, axis=-1, keepdims=True)
    )


def dense_rows(ref, values, base):
    ref[base : base + TOK, :] = values[:, 0:LANES]
    tail = values[:, LANES:TOK]
    tail = jnp.concatenate([tail, jnp.zeros((TOK, LANES - 16), tail.dtype)], axis=1)
    row = tail[0:16]
    for group in range(1, 8):
        row = row + pltpu.roll(tail[16 * group : 16 * group + 16], 16 * group, 1)
    ref[base + TOK : base + TOK + 16, :] = row
    ref[base + TOK + 16 : base + TOK + 32, :] = tail[LANES:TOK]


DENSE = TOK + 32


def window_kernel(
    block_ref, index_ref, table_ref, gain1_ref, gain2_ref, mix_ref, out_ref, up_ref, down_ref, order_ref, spread_ref,
    grads_ref, bias_out_ref, back_ref,
    flat_s, x_s, g_s, hot_s, high_s, low_s, table_s, dense_s, bias_s, acc_s, grad_s, rows_s, ge_s, moved_s,
):
    lane36 = lax.broadcasted_iota(jnp.int32, (PART, LANES), 1)
    sub36 = lax.broadcasted_iota(jnp.int32, (PART, LANES), 0)
    for slot in range(4):
        flat_s[slot] = block_ref[slot].astype(F32)
        toks = flat_s[slot, 0:CELLS, :]
        cots = flat_s[slot, CELLS:PART, :]
        base = PART * slot
        x_s[base : base + CELLS, :] = toks[:, 0:C]
        x_s[base + CELLS : base + PART, :] = toks[:, C : 2 * C]
        g_s[base : base + CELLS, :] = cots[:, 0:C]
        g_s[base + CELLS : base + PART, :] = cots[:, C : 2 * C]
        kind_row = flat_s[slot, PART : PART + 1, 0:LANES]
        kind_col = jnp.sum(jnp.where(lane36 == sub36, kind_row, 0.0), axis=1, keepdims=True)
        hot_s[base : base + PART, :] = jnp.where(lane36.astype(F32) == kind_col, 1.0, 0.0)

    order = order_ref[...]
    index = index_ref[...]
    high = (index // LANES).astype(F32).astype(BF16)
    low = (index % LANES).astype(F32).astype(BF16)
    dense_rows(high_s, dot_nt(dot(order, high).astype(BF16), order), 0)
    dense_rows(low_s, dot_nt(dot(order, low).astype(BF16), order), 0)
    table_s[...] = jnp.zeros((HEADS * 32, LANES), F32)
    for row in range(HI):
        width = min(LANES, PAIRS - row * LANES)
        for head in range(HEADS):
            table_s[32 * head + row : 32 * head + row + 1, 0:width] = table_ref[
                0, head : head + 1, row * LANES : row * LANES + width
            ]

    def gather(step, carry):
        start = pl.multiple_of(step * 16, 16)
        lows = low_s[pl.ds(start, 16), :].astype(jnp.int32)
        highs = high_s[pl.ds(start, 16), :]
        totals = [jnp.zeros((16, LANES), F32) for _ in range(HEADS)]
        for row in range(HI):
            chosen = highs == float(row)
            for head in range(HEADS):
                line = jnp.broadcast_to(table_s[32 * head + row : 32 * head + row + 1, :], (16, LANES))
                found = jnp.take_along_axis(line, lows, axis=1, mode="promise_in_bounds")
                totals[head] = jnp.where(chosen, found, totals[head])
        for head in range(HEADS):
            dense_s[pl.ds(pl.multiple_of(head * DENSE + start, 16), 16), :] = totals[head]
        return carry

    lax.fori_loop(0, DENSE // 16, gather, 0)
    for head in range(HEADS):
        base = head * DENSE
        bias_s[head * TOK : head * TOK + TOK, 0:LANES] = dense_s[base : base + TOK, :]
        row = dense_s[base + TOK : base + TOK + 16, :]
        for group in range(8):
            turned = row if group == 0 else pltpu.roll(row, LANES - 16 * group, 1)
            bias_s[head * TOK + 16 * group : head * TOK + 16 * group + 16, LANES:TOK] = turned[:, 0:16]
        bias_s[head * TOK + LANES : head * TOK + TOK, LANES:TOK] = dense_s[base + TOK + 16 : base + TOK + 32, 0:16]

    gain1, gain2 = gain1_ref[...], gain2_ref[...]
    mix_weight, out_weight = mix_ref[...], out_ref[...]
    up_weight, down_weight = up_ref[...], down_ref[...]
    residual = x_s[...]
    upstream = g_s[...]
    upstream_low = upstream.astype(BF16)
    first, hat1, inv1 = layer_norm(residual, gain1)
    first_in = first.astype(BF16)
    mixed = dot(first_in, mix_weight)
    queries = mixed[:, 0:C].astype(BF16).astype(F32)
    keys = mixed[:, C : 2 * C].astype(BF16)
    values = mixed[:, 2 * C : 3 * C].astype(BF16)
    channel = lax.broadcasted_iota(jnp.int32, (TOK, C), 1)
    of_head = [(channel >= HEAD * n) & (channel < HEAD * n + HEAD) for n in range(HEADS)]
    q_stack = jnp.concatenate([jnp.where(m, queries, 0.0) for m in of_head], axis=0).astype(BF16)
    scores = dot_nt(q_stack, keys) * (HEAD**-0.5) + bias_s[...]
    last = lax.axis_index("lat") == LAT - 1
    group_q = ((lax.broadcasted_iota(jnp.int32, (HEADS * TOK, TOK), 0) // 72) % 2).astype(F32)
    group_k = (lax.broadcasted_iota(jnp.int32, (HEADS * TOK, TOK), 1) >= 72).astype(F32)
    allowed = jnp.abs(group_q - group_k) * jnp.where(last, 1.0, 0.0) < 0.5
    expon = jnp.where(allowed, jnp.exp(scores), 0.0)
    attend = expon / jnp.sum(expon, axis=-1, keepdims=True)
    attend_low = attend.astype(BF16)
    context = jnp.zeros((TOK, C), F32)
    for n in range(HEADS):
        context += jnp.where(of_head[n], dot(attend_low[n * TOK : (n + 1) * TOK], values), 0.0)
    context = context.astype(BF16)
    mid = residual + dot(context, out_weight)
    second, hat2, inv2 = layer_norm(mid, gain2)
    second_in = second.astype(BF16)
    inner = dot(second_in, up_weight)
    tangent = jnp.tanh(GELU_SQRT * (inner + GELU_CUBE * inner * inner * inner))
    hidden_low = (0.5 * inner * (1.0 + tangent)).astype(BF16)
    slope = 0.5 * (1.0 + tangent) + 0.5 * inner * (1.0 - tangent * tangent) * GELU_SQRT * (
        1.0 + 3.0 * GELU_CUBE * inner * inner
    )
    hidden_grad = (dot_nt(upstream_low, down_weight) * slope).astype(BF16)
    second_grad = dot_nt(hidden_grad, up_weight)
    mid_grad = upstream + norm_backward(second_grad, hat2, inv2, gain2)
    mid_low = mid_grad.astype(BF16)
    context_grad = dot_nt(mid_low, out_weight).astype(BF16).astype(F32)
    c_stack = jnp.concatenate([jnp.where(m, context_grad, 0.0) for m in of_head], axis=0).astype(BF16)
    attend_grad = dot_nt(c_stack, values)
    value_grad = dot_tn(attend_low, c_stack).astype(BF16)
    score_grad = attend * (attend_grad - jnp.sum(attend * attend_grad, axis=-1, keepdims=True))
    score_low = score_grad.astype(BF16)
    query_grad = jnp.zeros((TOK, C), F32)
    for n in range(HEADS):
        query_grad += jnp.where(of_head[n], dot(score_low[n * TOK : (n + 1) * TOK], keys), 0.0)
        dense_rows(dense_s, score_grad[n * TOK : (n + 1) * TOK], n * DENSE)
    query_grad = (query_grad * (HEAD**-0.5)).astype(BF16)
    key_grad = (dot_tn(score_low, q_stack) * (HEAD**-0.5)).astype(BF16)
    first_grad = (
        dot_nt(query_grad, mix_weight[:, 0:C])
        + dot_nt(key_grad, mix_weight[:, C : 2 * C])
        + dot_nt(value_grad, mix_weight[:, 2 * C : 3 * C])
    )
    moved = mid_grad + norm_backward(first_grad, hat1, inv1, gain1)

    moved_s[...] = moved
    for slot in range(4):
        base = PART * slot
        flat_s[slot, 0:CELLS, 0:C] = moved_s[base : base + CELLS, :]
        flat_s[slot, 0:CELLS, C : 2 * C] = moved_s[base + CELLS : base + PART, :]
        back_ref[slot] = flat_s[slot, 0:32, :].astype(BF16)

    grad_s[:, 0:C] = dot_tn(first_in, query_grad)
    grad_s[:, C : 2 * C] = dot_tn(first_in, key_grad)
    grad_s[:, 2 * C : 3 * C] = dot_tn(first_in, value_grad)
    grad_s[:, 3 * C : 4 * C] = dot_tn(context, mid_low)
    grad_s[:, 4 * C : 8 * C] = dot_tn(second_in, hidden_grad)
    spread = dot(hidden_low, spread_ref[...]).astype(BF16)
    for part in range(4):
        grad_s[:, (8 + part) * C : (9 + part) * C] = dot_tn(spread[:, part * C : (part + 1) * C], upstream_low)
    lane = lax.broadcasted_iota(jnp.int32, (TOK, LANES), 1)
    small = jnp.zeros((C, LANES), F32)
    for left, right in (
        (moved, hot_s[...]),
        (first_grad * hat1, jnp.where(lane == KINDS, 1.0, 0.0)),
        (second_grad * hat2, jnp.where(lane == KINDS + 1, 1.0, 0.0)),
    ):
        for term in two_terms(left):
            small += dot_tn(term, right.astype(BF16))
    ge_s[...] = small
    for tile in range(TILES):
        rows_s[tile // 9, pl.ds(tile % 9, C, stride=9), :] = grad_s[:, tile * LANES : (tile + 1) * LANES]
    extra = jnp.zeros((32, LANES), F32)
    for k in range(6):
        line = ge_s[pl.ds(k, 32, stride=6), :]
        extra += pltpu.roll(line, 18 * k, 1) if k else line
    sub64 = lax.broadcasted_iota(jnp.int32, (64, LANES), 0)
    for half in range(2):
        for block in range(32):
            got = rows_s[half, 54 * block : 54 * block + 64, :]
            tail = jnp.where(sub64 == 54, extra[block : block + 1], 0.0) if half == 0 else jnp.zeros_like(got)
            got = jnp.where(sub64 < 54, got, tail).astype(BF16)
            for part in range(4):
                grads_ref[half, block // 8, part, block % 8] = got[16 * part : 16 * part + 16]

    acc_s[...] = jnp.zeros((208, LANES), F32)
    row32 = lax.broadcasted_iota(jnp.int32, (32, 2 * LANES), 0).astype(F32)
    row128 = lax.broadcasted_iota(jnp.int32, (LANES, 2 * LANES), 0).astype(F32)

    def pair(ref, row):
        return jnp.concatenate([ref[pl.ds(row, 1), :], ref[pl.ds(row + DENSE // 2, 1), :]], axis=1)

    def scatter(step, carry):
        chosen = row32 == pair(high_s, step)
        hot = jnp.where(row128 == pair(low_s, step), 1.0, 0.0).astype(BF16)
        spread_out = [jnp.where(chosen, pair(dense_s, n * DENSE + step), 0.0) for n in range(HEADS)]
        acc_s[0 : 32 * HEADS, :] += dot_nt(jnp.concatenate(spread_out, axis=0).astype(BF16), hot)
        return carry

    lax.fori_loop(0, DENSE // 2, scatter, 0)
    sub16 = lax.broadcasted_iota(jnp.int32, (16, LANES), 0)
    for block in range(16):
        bias_out_ref[block // 8, block % 8] = jnp.where(sub16 < 12, acc_s[12 * block : 12 * block + 16, :], 0.0)


def window(block, pair_index, bias_table, gain1, gain2, mix_weight, out_weight, up_weight, down_weight):
    token = np.arange(TOK)
    slot, level, cell = token // PART, (token % PART) // CELLS, token % CELLS
    row, col = 3 * (slot // 2) + cell // 6, 6 * (slot % 2) + cell % 6
    order = np.zeros((TOK, TOK), np.float32)
    order[token, (row * WIN_LON + col) * 2 + level] = 1.0
    column = np.arange(FF)
    spread = np.zeros((FF, FF), np.float32)
    spread[4 * (column % C) + column // C, column] = 1.0
    vmem = pl.BlockSpec(memory_space=pltpu.VMEM)
    return pl.pallas_call(
        window_kernel,
        out_shape=(
            jax.ShapeDtypeStruct((2, 4, 4, ZLO, 16, LANES), BF16),
            jax.ShapeDtypeStruct((2, ZLO, 16, LANES), F32),
            jax.ShapeDtypeStruct((4, 32, 2 * C), BF16),
        ),
        in_specs=[vmem] * 11,
        out_specs=(vmem, vmem, vmem),
        scratch_shapes=[
            pltpu.VMEM((4, 48, 2 * C), F32),
            pltpu.VMEM((TOK, C), F32),
            pltpu.VMEM((TOK, C), F32),
            pltpu.VMEM((TOK, LANES), F32),
            pltpu.VMEM((DENSE, LANES), F32),
            pltpu.VMEM((DENSE, LANES), F32),
            pltpu.VMEM((HEADS * 32, LANES), F32),
            pltpu.VMEM((HEADS * DENSE, LANES), F32),
            pltpu.VMEM((HEADS * TOK, TOK), F32),
            pltpu.VMEM((208, LANES), F32),
            pltpu.VMEM((C, COLS), F32),
            pltpu.VMEM((2, 9 * C + 16, LANES), F32),
            pltpu.VMEM((C, LANES), F32),
            pltpu.VMEM((TOK, C), F32),
        ],
        compiler_params=pltpu.CompilerParams(vmem_limit_bytes=VMEM_LIMIT),
        name="window",
    )(
        block, pair_index, bias_table, gain1, gain2, mix_weight, out_weight, up_weight, down_weight,
        jnp.asarray(order, BF16), jnp.asarray(spread, BF16),
    )


def reduce_kernel(
    grads_ref, bias_ref, back_ref,
    dense_out, bias_out, back_out, total_out,
    core_r, plane_s, plane_r, line_s, line_r, share, bcore_r, bline_s, bline_r, brow_r, ball, back_r, squares_z, squares_y,
    core_ss, core_rs, plane_ss, plane_rs, line_ss, line_rs, share_ss, share_rs, bcore_ss, bcore_rs, bline_ss, bline_rs,
    brow_ss, brow_rs, ball_ss, ball_rs, bpair_ss, bpair_rs, back_ss, back_rs, sz_ss, sz_rs, sy_ss, sy_rs,
):
    lon, lat = lax.axis_index("lon"), lax.axis_index("lat")
    x, y, z, core = place()
    z_lo, z_hi = z % ZLO, z // ZLO
    other = 1 - core

    def remote(src, dst, send_sem, recv_sem, target):
        return pltpu.make_async_remote_copy(
            src_ref=src, dst_ref=dst, send_sem=send_sem, recv_sem=recv_sem, device_id=target, device_id_type=MESH
        )

    barrier = pltpu.get_barrier_semaphore()
    peers = [at(x, y, z, other)]
    peers += [at((x + d // 4) % 4, (y + d % 4) % 4, z, core) for d in range(1, 16)]
    peers += [at(x, y, (z + d) % 16, core) for d in range(1, 16)]
    peers += [at((x + d) % 4, y, z, other) for d in range(1, 4)]
    for dr, dc in ((1, 0), (0, 1), (1, 1)):
        for sign in (1, -1):
            peers.append({"lon": (lon + sign * dc + LON) % LON, "lat": (lat + sign * dr + LAT) % LAT})
    for peer in peers:
        pl.semaphore_signal(barrier, inc=1, device_id=peer, device_id_type=MESH)
    pl.semaphore_wait(barrier, len(peers))

    sends = []

    bcore = remote(bias_ref.at[other], bcore_r, bcore_ss, bcore_rs, at(x, y, z, other))
    bcore.start()
    sends.append(bcore)
    core_copies = []
    for j in range(4):
        to = (y + 1 + j) % 4
        copy = remote(grads_ref.at[other, to], core_r.at[to], core_ss.at[j], core_rs.at[j], at(x, y, z, other))
        copy.start()
        core_copies.append(copy)
    sends += core_copies
    back_copies = []
    for slot in (3, 2, 1):
        dr, dc = slot // 2, slot % 2
        copy = remote(
            back_ref.at[slot],
            back_r.at[3 - slot],
            back_ss.at[slot],
            back_rs.at[slot],
            {"lon": (lon + dc) % LON, "lat": (lat + dr) % LAT},
        )
        copy.start()
        back_copies.append((slot, copy))
    sends += [copy for _, copy in back_copies]

    bcore.wait_recv()
    for part in range(ZLO):
        bline_s[part] = bias_ref[core, part] + bcore_r[part]
    bline_r[z_lo] = bline_s[z_lo]
    bline_copies = []
    for d in range(1, ZLO):
        to = (z_lo + d) % ZLO
        copy = remote(
            bline_s.at[to], bline_r.at[z_lo], bline_ss.at[d], bline_rs.at[d], at(x, y, z_hi * ZLO + to, core)
        )
        copy.start()
        bline_copies.append(copy)
    sends += bline_copies

    plane_copies = {}
    for j in range(4):
        to_y = (y + 1 + j) % 4
        core_copies[j].wait_recv()
        for part in range(4):
            plane_s[to_y, part] = (grads_ref[core, to_y, part].astype(F32) + core_r[to_y, part].astype(F32)).astype(BF16)
        for i in range(4):
            dx, dy = (i + 1) % 4, (j + 1) % 4
            d = dx * 4 + dy
            to_x = (x + dx) % 4
            if d == 0:
                plane_r[x * 4 + y] = plane_s[y, x]
                continue
            copy = remote(
                plane_s.at[to_y, to_x],
                plane_r.at[x * 4 + y],
                plane_ss.at[d],
                plane_rs.at[d],
                at(to_x, to_y, z, core),
            )
            copy.start()
            plane_copies[d] = copy
    sends += list(plane_copies.values())

    for copy in bline_copies:
        copy.wait_recv()
    part_sum = bline_r[0]
    for part in range(1, ZLO):
        part_sum = part_sum + bline_r[part]
    brow_r[y] = part_sum
    brow_copies = []
    for d in range(1, 4):
        to = (y + d) % 4
        copy = remote(brow_r.at[y], brow_r.at[y], brow_ss.at[d], brow_rs.at[d], at(x, to, z, core))
        copy.start()
        brow_copies.append(copy)
    sends += brow_copies

    for copy in plane_copies.values():
        copy.wait_recv()
    for part in range(ZLO):
        block = plane_r[0, part].astype(F32)
        for source in range(1, 16):
            block = block + plane_r[source, part].astype(F32)
        line_s[part] = block.astype(BF16)
    line_r[z] = line_s[z_lo]
    line_copies = []
    for d in range(1, 16):
        to = (z + d) % 16
        copy = remote(line_s.at[to % ZLO], line_r.at[z], line_ss.at[d], line_rs.at[d], at(x, y, to, core))
        copy.start()
        line_copies.append(copy)
    sends += line_copies

    for copy in brow_copies:
        copy.wait_recv()
    bias_part = (brow_r[0] + brow_r[1]) + (brow_r[2] + brow_r[3])
    ball[core, z_lo] = bias_part
    ball_copies = []
    for d in range(1, ZLO):
        to = (z_lo + d) % ZLO
        copy = remote(
            ball.at[core, z_lo], ball.at[core, z_lo], ball_ss.at[d], ball_rs.at[d], at(x, y, z_hi * ZLO + to, core)
        )
        copy.start()
        ball_copies.append(copy)
    sends += ball_copies

    for copy in line_copies:
        copy.wait_recv()
    piece = line_r[0].astype(F32)
    for source in range(1, 16):
        piece = piece + line_r[source].astype(F32)
    square = 0.5 * jnp.sum(piece * piece) + 0.25 * jnp.sum(bias_part * bias_part)
    mine = core * 4 + x
    share[mine, 0:16, :] = piece
    share[mine, 16:24, :] = jnp.full((8, LANES), square, F32)
    share_copies = []
    for dx, dcore in ((1, 0), (2, 0), (3, 0), (0, 1), (1, 1), (2, 1), (3, 1)):
        d = dcore * 4 + dx
        copy = remote(
            share.at[mine],
            share.at[mine],
            share_ss.at[d],
            share_rs.at[d],
            at((x + dx) % 4, y, z, core + dcore * (1 - 2 * core)),
        )
        copy.start()
        share_copies.append(copy)
    sends += share_copies

    for copy in ball_copies:
        copy.wait_recv()
    bpair = remote(ball.at[core], ball.at[core], bpair_ss, bpair_rs, at(x, y, z, other))
    bpair.start()
    sends.append(bpair)

    for copy in share_copies:
        copy.wait_recv()
    square = share[0, 16:17, :]
    for source in range(1, 8):
        square = square + share[source, 16:17, :]
    squares_z[z] = square
    sz_copies = []
    for d in range(1, 16):
        to = (z + d) % 16
        copy = remote(squares_z.at[z], squares_z.at[z], sz_ss.at[d], sz_rs.at[d], at(x, y, to, core))
        copy.start()
        sz_copies.append(copy)
    sends += sz_copies
    for source in range(8):
        dense_out[source] = share[source, 0:16, :]
    back_out[3] = back_ref[0]
    for slot, copy in back_copies:
        copy.wait_recv()
        back_out[3 - slot] = back_r[3 - slot]
    for copy in sz_copies:
        copy.wait_recv()
    square = squares_z[0]
    for source in range(1, 16):
        square = square + squares_z[source]
    squares_y[y] = square
    sy_copies = []
    for d in range(1, 4):
        copy = remote(squares_y.at[y], squares_y.at[y], sy_ss.at[d], sy_rs.at[d], at(x, (y + d) % 4, z, core))
        copy.start()
        sy_copies.append(copy)
    sends += sy_copies
    bpair.wait_recv()
    bias_out[...] = ball[...]
    for copy in sy_copies:
        copy.wait_recv()
    total_out[...] = (squares_y[0] + squares_y[1]) + (squares_y[2] + squares_y[3])
    for copy in sends:
        copy.wait_send()


def reduce(grads, bias, back):
    vmem = pl.BlockSpec(memory_space=pltpu.VMEM)
    dma = pltpu.SemaphoreType.DMA
    return pl.pallas_call(
        reduce_kernel,
        out_shape=(
            jax.ShapeDtypeStruct((8, 16, LANES), F32),
            jax.ShapeDtypeStruct((2, ZLO, 16, LANES), F32),
            jax.ShapeDtypeStruct((4, 32, 2 * C), BF16),
            jax.ShapeDtypeStruct((1, LANES), F32),
        ),
        in_specs=[vmem] * 3,
        out_specs=(vmem,) * 4,
        scratch_shapes=[
            pltpu.VMEM((4, 4, ZLO, 16, LANES), BF16),
            pltpu.VMEM((4, 4, ZLO, 16, LANES), BF16),
            pltpu.VMEM((16, ZLO, 16, LANES), BF16),
            pltpu.VMEM((ZLO, 16, LANES), BF16),
            pltpu.VMEM((16, 16, LANES), BF16),
            pltpu.VMEM((8, 24, LANES), F32),
            pltpu.VMEM((ZLO, 16, LANES), F32),
            pltpu.VMEM((ZLO, 16, LANES), F32),
            pltpu.VMEM((ZLO, 16, LANES), F32),
            pltpu.VMEM((4, 16, LANES), F32),
            pltpu.VMEM((2, ZLO, 16, LANES), F32),
            pltpu.VMEM((4, 32, 2 * C), BF16),
            pltpu.VMEM((16, 1, LANES), F32),
            pltpu.VMEM((4, 1, LANES), F32),
            dma((4,)), dma((4,)),
            dma((16,)), dma((16,)),
            dma((16,)), dma((16,)),
            dma((8,)), dma((8,)),
            dma, dma,
            dma((8,)), dma((8,)),
            dma((4,)), dma((4,)),
            dma((8,)), dma((8,)),
            dma, dma,
            dma((4,)), dma((4,)),
            dma((16,)), dma((16,)),
            dma((4,)), dma((4,)),
        ],
        compiler_params=pltpu.CompilerParams(collective_id=1, has_side_effects=True, vmem_limit_bytes=VMEM_LIMIT),
        name="sum_over_devices",
    )(grads, bias, back)


def output_kernel(
    dense_ref, bias_ref, back_ref, total_ref,
    token_ref, mix_ref, out_ref, up_ref, down_ref, gain_ref, embed_ref, table_ref,
    dense_s, flat_s, bias_s, back_s, token_s,
):
    count = C * COLS + (KINDS + 2) * C + LAT * HEADS * PAIRS
    factor = lax.rsqrt(total_ref[...] / count + RMS_EPS)
    odd = lax.axis_index("lon") % 2 == 1
    for part in range(8):
        dense_s[part // 4, 16 * (part % 4) : 16 * (part % 4) + 16, :] = dense_ref[part] * factor
    for tile in range(TILES):
        half, t = tile // 9, tile % 9
        even_rows = dense_s[half, pl.ds(t, 3, stride=9), :]
        odd_rows = dense_s[half, pl.ds(27 + t, 3, stride=9), :]
        flat_s[0:3, tile * LANES : (tile + 1) * LANES] = jnp.where(odd, odd_rows, even_rows)
    flat = flat_s[0:3, :]
    mix_ref[...] = flat[:, 0 : 3 * C]
    out_ref[...] = flat[:, 3 * C : 4 * C]
    up_ref[...] = flat[:, 4 * C : 8 * C]
    for row in range(3):
        for part in range(4):
            down_ref[4 * row + part : 4 * row + part + 1, :] = flat[row : row + 1, (8 + part) * C : (9 + part) * C]
    extra = dense_s[0, 54:55, :]
    lane = lax.broadcasted_iota(jnp.int32, (24, LANES), 1)
    sub = lax.broadcasted_iota(jnp.int32, (24, LANES), 0)
    small = jnp.zeros((24, LANES), F32)
    for row in range(3):
        start = jnp.where(odd, 18 * (3 + row), 18 * row)
        column = jnp.sum(jnp.where(lane == sub + start, extra, 0.0), axis=1, keepdims=True)
        small = small + jnp.where(lane == row, column, 0.0)
    embed_ref[...] = small[0:KINDS, 0:3]
    gain_ref[...] = small[KINDS : KINDS + 2, 0:3]
    for block in range(16):
        bias_s[12 * block : 12 * block + 12, :] = bias_ref[block // 8, block % 8, 0:12, :] * factor
    for row in range(HI):
        width = min(LANES, PAIRS - row * LANES)
        table_ref[0, :, row * LANES : row * LANES + width] = bias_s[pl.ds(row, HEADS, stride=32), :][:, 0:width]
    for quarter in range(4):
        back_s[quarter] = back_ref[quarter].astype(F32)
        for i in range(3):
            row, half = 3 * (quarter // 2) + i, quarter % 2
            token_s[row, 6 * half : 6 * half + 6, :] = back_s[quarter, 6 * i : 6 * i + 6, :]
    for row in range(WIN_LAT):
        token_ref[row] = token_s[row, 0:WIN_LON, :].astype(BF16)


def outputs(dense, bias, back, total):
    vmem = pl.BlockSpec(memory_space=pltpu.VMEM)
    return pl.pallas_call(
        output_kernel,
        out_shape=(
            jax.ShapeDtypeStruct((WIN_LAT, WIN_LON, 2 * C), BF16),
            jax.ShapeDtypeStruct((3, 3 * C), F32),
            jax.ShapeDtypeStruct((3, C), F32),
            jax.ShapeDtypeStruct((3, FF), F32),
            jax.ShapeDtypeStruct((12, C), F32),
            jax.ShapeDtypeStruct((2, 3), F32),
            jax.ShapeDtypeStruct((KINDS, 3), F32),
            jax.ShapeDtypeStruct((1, HEADS, PAIRS), F32),
        ),
        in_specs=[vmem] * 4,
        out_specs=(vmem,) * 8,
        scratch_shapes=[
            pltpu.VMEM((2, 64, LANES), F32),
            pltpu.VMEM((8, COLS), F32),
            pltpu.VMEM((HEADS * 32, LANES), F32),
            pltpu.VMEM((4, 32, 2 * C), F32),
            pltpu.VMEM((WIN_LAT, 16, 2 * C), F32),
        ],
        compiler_params=pltpu.CompilerParams(vmem_limit_bytes=VMEM_LIMIT),
        name="scaled_outputs",
    )(dense, bias, back, total)


def shards(
    tokens, kinds, kind_embed, pair_index, bias_table, attn_gain, mlp_gain,
    mix_weight, out_weight, up_weight, down_weight, cotangent,
):
    block = halo(tokens, kinds, kind_embed, cotangent)
    grads, bias, back = window(
        block, pair_index, bias_table, attn_gain.reshape(1, C), mlp_gain.reshape(1, C),
        mix_weight, out_weight, up_weight, down_weight,
    )
    return outputs(*reduce(grads, bias, back))


def solution(mesh):
    return jax.shard_map(
        shards,
        mesh=mesh,
        in_specs=(
            P("lat", "lon", None),
            P("lat", "lon", None),
            P(),
            P(),
            P("lat", None, None),
            P(),
            P(),
            P(),
            P(),
            P(),
            P(),
            P("lat", "lon", None),
        ),
        out_specs=(
            P("lat", "lon", None),
            P("lon", None),
            P("lon", None),
            P("lon", None),
            P("lon", None),
            P(None, "lon"),
            P(None, "lon"),
            P("lat", None, None),
        ),
        check_vma=False,
    )
```

```python
import jax
import jax.numpy as jnp
import numpy as np
from jax import lax
from jax.experimental import pallas as pl
from jax.experimental.pallas import tpu as pltpu
from jax.sharding import PartitionSpec as P

F32 = jnp.float32
BF16 = jnp.bfloat16
MESH = pl.DeviceIdType.MESH

C = 192
HEADS = 6
HEAD = 32
FF = 768
WIN_LAT = 6
WIN_LON = 12
KINDS = 16
PAIRS = 3312
TOK = 144
CELLS = 18
PART = 36
LANES = 128
HI = 26
COLS = 2304
TILES = 18
NORM_EPS = 1e-05
RMS_EPS = 1e-06
GELU_SQRT = 0.7978845608028654
GELU_CUBE = 0.044715
LON, LAT = 64, 8
ZLO = 8
VMEM_LIMIT = 56 * 1024 * 1024


def place():
    lon, lat = lax.axis_index("lon"), lax.axis_index("lat")
    return lat // 2, lon // 16, (lat % 2) * ZLO + (lon // 2) % ZLO, lon % 2


def at(x, y, z, core):
    return {"lon": y * 16 + (z % ZLO) * 2 + core, "lat": x * 2 + z // ZLO}


def dot(a, b):
    return lax.dot_general(a, b, (((1,), (0,)), ((), ())), preferred_element_type=F32)


def dot_nt(a, b):
    return lax.dot_general(a, b, (((1,), (1,)), ((), ())), preferred_element_type=F32)


def dot_tn(a, b):
    return lax.dot_general(a, b, (((0,), (0,)), ((), ())), preferred_element_type=F32)


def two_terms(v):
    high = v.astype(BF16)
    return high, (v - high.astype(F32)).astype(BF16)


def dense_rows(ref, values, base):
    ref[base : base + TOK, :] = values[:, 0:LANES]
    tail = values[:, LANES:TOK]
    tail = jnp.concatenate([tail, jnp.zeros((TOK, LANES - 16), tail.dtype)], axis=1)
    row = tail[0:16]
    for group in range(1, 8):
        row = row + pltpu.roll(tail[16 * group : 16 * group + 16], 16 * group, 1)
    ref[base + TOK : base + TOK + 16, :] = row
    ref[base + TOK + 16 : base + TOK + 32, :] = tail[LANES:TOK]


DENSE = TOK + 32
FLAT = 3 * PART
SENT = FLAT + 4


def halo_kernel(
    tok_ref, kind_ref, embed_ref, cot_ref, index_ref, table_ref, order_ref,
    out_ref, bias_ref, high_ref, low_ref,
    tok_s, kind_s, flat_s, pack_s, send, recv, table_s, dense_s, send_sem, recv_sem,
):
    lon, lat = lax.axis_index("lon"), lax.axis_index("lat")
    barrier = pltpu.get_barrier_semaphore()
    for dr, dc in ((1, 0), (0, 1), (1, 1)):
        for sign in (1, -1):
            pl.semaphore_signal(
                barrier,
                inc=1,
                device_id={"lon": (lon + sign * dc + LON) % LON, "lat": (lat + sign * dr + LAT) % LAT},
                device_id_type=MESH,
            )
    embed = embed_ref[...].astype(F32)
    blank = jnp.zeros((KINDS, C), F32)
    wide = jnp.concatenate(
        [jnp.concatenate([embed, blank], axis=1), jnp.concatenate([blank, embed], axis=1)], axis=0
    ).astype(BF16)
    kind_s[...] = jnp.zeros((4, 8, LANES), F32)
    for row in range(WIN_LAT):
        tok = tok_ref[row].astype(F32)
        cot = cot_ref[row].astype(F32)
        kind = kind_ref[row].astype(F32)
        for half in range(2):
            quarter = 2 * (row // 3) + half
            start = 6 * (row % 3)
            cells = slice(6 * half, 6 * half + 6)
            tok_s[quarter, start : start + 6, :] = tok[cells]
            flat_s[quarter, CELLS + start : CELLS + start + 6, :] = cot[cells]
            kind_s[quarter, 0:2, start : start + 6] = kind[:, cells]
    sub = lax.broadcasted_iota(jnp.int32, (2 * KINDS, LANES), 0).astype(F32)
    for quarter in range(4):
        kinds = kind_s[quarter]
        hot = (sub == kinds[0:1]) | (sub - KINDS == kinds[1:2])
        hot = jnp.where(hot, 1.0, 0.0).astype(BF16)[:, 0:24]
        stored = tok_s[quarter] + dot_tn(hot, wide)
        flat_s[quarter, 0:CELLS, :] = stored[0:CELLS]
        for tile in range(3):
            pack_s[quarter, PART * tile : PART * tile + PART, :] = flat_s[
                quarter, 0:PART, tile * LANES : (tile + 1) * LANES
            ]
        pack_s[quarter, FLAT:SENT, :] = jnp.zeros((4, LANES), F32)
        pack_s[quarter, FLAT : FLAT + 1, :] = kinds[0:1] + pltpu.roll(kinds, CELLS, 1)[1:2]
        send[quarter] = pack_s[quarter].astype(BF16)
    pl.semaphore_wait(barrier, 6)
    copies = []
    for slot in (3, 2, 1):
        dr, dc = slot // 2, slot % 2
        copy = pltpu.make_async_remote_copy(
            src_ref=send.at[3 - slot],
            dst_ref=recv.at[slot],
            send_sem=send_sem.at[slot],
            recv_sem=recv_sem.at[slot],
            device_id={"lon": (lon - dc + LON) % LON, "lat": (lat - dr + LAT) % LAT},
            device_id_type=MESH,
        )
        copy.start()
        copies.append(copy)

    order = order_ref[...]
    index = index_ref[...]
    high = (index // LANES).astype(F32).astype(BF16)
    low = (index % LANES).astype(F32).astype(BF16)
    dense_rows(high_ref, dot_nt(dot(order, high).astype(BF16), order), 0)
    dense_rows(low_ref, dot_nt(dot(order, low).astype(BF16), order), 0)
    table_s[...] = jnp.zeros((HEADS * 32, LANES), F32)
    for row in range(HI):
        width = min(LANES, PAIRS - row * LANES)
        for head in range(HEADS):
            table_s[32 * head + row : 32 * head + row + 1, 0:width] = table_ref[
                head, :, row * LANES : row * LANES + width
            ]

    def gather(step, carry):
        start = pl.multiple_of(step * 16, 16)
        lows = low_ref[pl.ds(start, 16), :].astype(jnp.int32)
        highs = high_ref[pl.ds(start, 16), :]
        totals = [jnp.zeros((16, LANES), F32) for _ in range(HEADS)]
        for row in range(HI):
            chosen = highs == float(row)
            for head in range(HEADS):
                line = jnp.broadcast_to(table_s[32 * head + row : 32 * head + row + 1, :], (16, LANES))
                found = jnp.take_along_axis(line, lows, axis=1, mode="promise_in_bounds")
                totals[head] = jnp.where(chosen, found, totals[head])
        for head in range(HEADS):
            dense_s[pl.ds(pl.multiple_of(head * DENSE + start, 16), 16), :] = totals[head]
        return carry

    lax.fori_loop(0, DENSE // 16, gather, 0)
    for head in range(HEADS):
        base = head * DENSE
        bias_ref[head * TOK : head * TOK + TOK, 0:LANES] = dense_s[base : base + TOK, :]
        row = dense_s[base + TOK : base + TOK + 16, :]
        for group in range(8):
            turned = row if group == 0 else pltpu.roll(row, LANES - 16 * group, 1)
            bias_ref[head * TOK + 16 * group : head * TOK + 16 * group + 16, LANES:TOK] = turned[:, 0:16]
        bias_ref[head * TOK + LANES : head * TOK + TOK, LANES:TOK] = dense_s[base + TOK + 16 : base + TOK + 32, 0:16]

    out_ref[0] = send[3]
    for slot, copy in zip((3, 2, 1), copies):
        copy.wait_recv()
        out_ref[slot] = recv[slot]
    for copy in copies:
        copy.wait_send()


def halo(tokens, kinds, kind_embed, cotangent, pair_index, bias_table):
    token = np.arange(TOK)
    slot, level, cell = token // PART, (token % PART) // CELLS, token % CELLS
    row, col = 3 * (slot // 2) + cell // 6, 6 * (slot % 2) + cell % 6
    order = np.zeros((TOK, TOK), np.float32)
    order[token, (row * WIN_LON + col) * 2 + level] = 1.0
    vmem = pl.BlockSpec(memory_space=pltpu.VMEM)
    return pl.pallas_call(
        halo_kernel,
        out_shape=(
            jax.ShapeDtypeStruct((4, SENT, LANES), BF16),
            jax.ShapeDtypeStruct((HEADS * TOK, TOK), F32),
            jax.ShapeDtypeStruct((DENSE, LANES), F32),
            jax.ShapeDtypeStruct((DENSE, LANES), F32),
        ),
        in_specs=[vmem] * 7,
        out_specs=(vmem,) * 4,
        scratch_shapes=[
            pltpu.VMEM((4, 24, 2 * C), F32),
            pltpu.VMEM((4, 8, LANES), F32),
            pltpu.VMEM((4, 40, 2 * C), F32),
            pltpu.VMEM((4, SENT, LANES), F32),
            pltpu.VMEM((4, SENT, LANES), BF16),
            pltpu.VMEM((4, SENT, LANES), BF16),
            pltpu.VMEM((HEADS * 32, LANES), F32),
            pltpu.VMEM((HEADS * DENSE, LANES), F32),
            pltpu.SemaphoreType.DMA((4,)),
            pltpu.SemaphoreType.DMA((4,)),
        ],
        compiler_params=pltpu.CompilerParams(collective_id=0, has_side_effects=True, vmem_limit_bytes=VMEM_LIMIT),
        name="halo_in",
    )(tokens, kinds, kind_embed, cotangent, pair_index, bias_table, jnp.asarray(order, BF16))


def layer_norm(values, gain):
    centred = values - jnp.mean(values, axis=-1, keepdims=True)
    inverse = lax.rsqrt(jnp.mean(centred * centred, axis=-1, keepdims=True) + NORM_EPS)
    normed = centred * inverse
    return normed * gain, normed, inverse


def norm_backward(upstream, normed, inverse, gain):
    scaled = upstream * gain
    return inverse * (
        scaled
        - jnp.mean(scaled, axis=-1, keepdims=True)
        - normed * jnp.mean(scaled * normed, axis=-1, keepdims=True)
    )


def window_kernel(
    block_ref, bias_ref, gain1_ref, gain2_ref, mix_ref, out_ref, up_ref, down_ref,
    first_in_ref, query_grad_ref, key_grad_ref, value_grad_ref, context_ref, mid_low_ref, second_in_ref, hidden_grad_ref,
    hidden_low_ref, upstream_ref, score_ref, extra_ref, back_ref,
    flat_s, x_s, g_s, hot_s, ge_s, moved_s, pack_s,
):
    lane36 = lax.broadcasted_iota(jnp.int32, (PART, LANES), 1)
    sub36 = lax.broadcasted_iota(jnp.int32, (PART, LANES), 0)
    for slot in range(4):
        pack_s[slot] = block_ref[slot].astype(F32)
        for tile in range(3):
            flat_s[slot, 0:PART, tile * LANES : (tile + 1) * LANES] = pack_s[slot, PART * tile : PART * tile + PART, :]
        toks = flat_s[slot, 0:CELLS, :]
        cots = flat_s[slot, CELLS:PART, :]
        base = PART * slot
        x_s[base : base + CELLS, :] = toks[:, 0:C]
        x_s[base + CELLS : base + PART, :] = toks[:, C : 2 * C]
        g_s[base : base + CELLS, :] = cots[:, 0:C]
        g_s[base + CELLS : base + PART, :] = cots[:, C : 2 * C]
        kind_row = pack_s[slot, FLAT : FLAT + 1, :]
        kind_col = jnp.sum(jnp.where(lane36 == sub36, kind_row, 0.0), axis=1, keepdims=True)
        hot_s[base : base + PART, :] = jnp.where(lane36.astype(F32) == kind_col, 1.0, 0.0)

    gain1, gain2 = gain1_ref[...], gain2_ref[...]
    mix_weight, out_weight = mix_ref[...], out_ref[...]
    up_weight, down_weight = up_ref[...], down_ref[...]
    residual = x_s[...]
    upstream = g_s[...]
    upstream_low = upstream.astype(BF16)
    first, hat1, inv1 = layer_norm(residual, gain1)
    first_in = first.astype(BF16)
    mixed = dot(first_in, mix_weight)
    queries = mixed[:, 0:C].astype(BF16).astype(F32)
    keys = mixed[:, C : 2 * C].astype(BF16)
    values = mixed[:, 2 * C : 3 * C].astype(BF16)
    channel = lax.broadcasted_iota(jnp.int32, (TOK, C), 1)
    of_head = [(channel >= HEAD * n) & (channel < HEAD * n + HEAD) for n in range(HEADS)]
    q_stack = jnp.concatenate([jnp.where(m, queries, 0.0) for m in of_head], axis=0).astype(BF16)
    scores = dot_nt(q_stack, keys) * (HEAD**-0.5) + bias_ref[...]
    last = lax.axis_index("lat") == LAT - 1
    group_q = ((lax.broadcasted_iota(jnp.int32, (HEADS * TOK, TOK), 0) // 72) % 2).astype(F32)
    group_k = (lax.broadcasted_iota(jnp.int32, (HEADS * TOK, TOK), 1) >= 72).astype(F32)
    allowed = jnp.abs(group_q - group_k) * jnp.where(last, 1.0, 0.0) < 0.5
    expon = jnp.where(allowed, jnp.exp(scores), 0.0)
    attend = expon / jnp.sum(expon, axis=-1, keepdims=True)
    attend_low = attend.astype(BF16)
    context = jnp.zeros((TOK, C), F32)
    for n in range(HEADS):
        context += jnp.where(of_head[n], dot(attend_low[n * TOK : (n + 1) * TOK], values), 0.0)
    context = context.astype(BF16)
    mid = residual + dot(context, out_weight)
    second, hat2, inv2 = layer_norm(mid, gain2)
    second_in = second.astype(BF16)
    inner = dot(second_in, up_weight)
    tangent = jnp.tanh(GELU_SQRT * (inner + GELU_CUBE * inner * inner * inner))
    hidden_low = (0.5 * inner * (1.0 + tangent)).astype(BF16)
    slope = 0.5 * (1.0 + tangent) + 0.5 * inner * (1.0 - tangent * tangent) * GELU_SQRT * (
        1.0 + 3.0 * GELU_CUBE * inner * inner
    )
    hidden_grad = (dot(upstream_low, down_weight) * slope).astype(BF16)
    second_grad = dot_nt(hidden_grad, up_weight)
    mid_grad = upstream + norm_backward(second_grad, hat2, inv2, gain2)
    mid_low = mid_grad.astype(BF16)
    context_grad = dot_nt(mid_low, out_weight).astype(BF16).astype(F32)
    c_stack = jnp.concatenate([jnp.where(m, context_grad, 0.0) for m in of_head], axis=0).astype(BF16)
    attend_grad = dot_nt(c_stack, values)
    value_grad = dot_tn(attend_low, c_stack).astype(BF16)
    score_grad = attend * (attend_grad - jnp.sum(attend * attend_grad, axis=-1, keepdims=True))
    score_low = score_grad.astype(BF16)
    query_grad = jnp.zeros((TOK, C), F32)
    for n in range(HEADS):
        query_grad += jnp.where(of_head[n], dot(score_low[n * TOK : (n + 1) * TOK], keys), 0.0)
        dense_rows(score_ref, score_grad[n * TOK : (n + 1) * TOK], n * DENSE)
    query_grad = (query_grad * (HEAD**-0.5)).astype(BF16)
    key_grad = (dot_tn(score_low, q_stack) * (HEAD**-0.5)).astype(BF16)
    first_grad = (
        dot_nt(query_grad, mix_weight[:, 0:C])
        + dot_nt(key_grad, mix_weight[:, C : 2 * C])
        + dot_nt(value_grad, mix_weight[:, 2 * C : 3 * C])
    )
    moved = mid_grad + norm_backward(first_grad, hat1, inv1, gain1)

    moved_s[...] = moved
    for slot in range(4):
        base = PART * slot
        flat_s[slot, 0:CELLS, 0:C] = moved_s[base : base + CELLS, :]
        flat_s[slot, 0:CELLS, C : 2 * C] = moved_s[base + CELLS : base + PART, :]
        for tile in range(3):
            pack_s[slot, CELLS * tile : CELLS * tile + CELLS, :] = flat_s[
                slot, 0:CELLS, tile * LANES : (tile + 1) * LANES
            ]
        back_ref[slot] = pack_s[slot, 0:64, :].astype(BF16)

    first_in_ref[...] = first_in
    query_grad_ref[...] = query_grad
    key_grad_ref[...] = key_grad
    value_grad_ref[...] = value_grad
    context_ref[...] = context
    mid_low_ref[...] = mid_low
    second_in_ref[...] = second_in
    hidden_grad_ref[...] = hidden_grad
    hidden_low_ref[...] = hidden_low
    upstream_ref[...] = upstream_low
    lane = lax.broadcasted_iota(jnp.int32, (TOK, LANES), 1)
    small = jnp.zeros((C, LANES), F32)
    for left, right in (
        (moved, hot_s[...]),
        (first_grad * hat1, jnp.where(lane == KINDS, 1.0, 0.0)),
        (second_grad * hat2, jnp.where(lane == KINDS + 1, 1.0, 0.0)),
    ):
        for term in two_terms(left):
            small += dot_tn(term, right.astype(BF16))
    ge_s[...] = small
    extra = jnp.zeros((32, LANES), F32)
    for k in range(6):
        line = ge_s[pl.ds(k, 32, stride=6), :]
        extra += pltpu.roll(line, 18 * k, 1) if k else line
    extra_ref[...] = extra


def window(block, bias, gain1, gain2, mix_weight, out_weight, up_weight, down_weight):
    vmem = pl.BlockSpec(memory_space=pltpu.VMEM)
    narrow = jax.ShapeDtypeStruct((TOK, C), BF16)
    wide = jax.ShapeDtypeStruct((TOK, FF), BF16)
    return pl.pallas_call(
        window_kernel,
        out_shape=(
            narrow, narrow, narrow, narrow, narrow, narrow, narrow, wide, wide, narrow,
            jax.ShapeDtypeStruct((HEADS * DENSE, LANES), F32),
            jax.ShapeDtypeStruct((32, LANES), F32),
            jax.ShapeDtypeStruct((4, 64, LANES), BF16),
        ),
        in_specs=[vmem] * 8,
        out_specs=(vmem,) * 13,
        scratch_shapes=[
            pltpu.VMEM((4, 40, 2 * C), F32),
            pltpu.VMEM((TOK, C), F32),
            pltpu.VMEM((TOK, C), F32),
            pltpu.VMEM((TOK, LANES), F32),
            pltpu.VMEM((C, LANES), F32),
            pltpu.VMEM((TOK, C), F32),
            pltpu.VMEM((4, SENT, LANES), F32),
        ],
        compiler_params=pltpu.CompilerParams(vmem_limit_bytes=VMEM_LIMIT),
        name="window",
    )(block, bias, gain1, gain2, mix_weight, out_weight, up_weight, down_weight)


def reduce_kernel(
    first_in_ref, query_grad_ref, key_grad_ref, value_grad_ref, context_ref, mid_low_ref, second_in_ref, hidden_grad_ref,
    hidden_low_ref, upstream_ref, score_ref, extra_ref, back_ref, high_ref, low_ref, spread_ref,
    dense_out, bias_out, back_out, total_out,
    grad_s, rows_s, grads, acc_s, bias_s,
    core_r, plane_s, plane_r, line_s, line_r, share, bcore_r, bline_s, bline_r, brow_r, ball, back_r, squares_z, squares_y,
    core_ss, core_rs, plane_ss, plane_rs, line_ss, line_rs, share_ss, share_rs, bcore_ss, bcore_rs, bline_ss, bline_rs,
    brow_ss, brow_rs, ball_ss, ball_rs, bpair_ss, bpair_rs, back_ss, back_rs, sz_ss, sz_rs, sy_ss, sy_rs,
):
    lon, lat = lax.axis_index("lon"), lax.axis_index("lat")
    x, y, z, core = place()
    z_lo, z_hi = z % ZLO, z // ZLO
    other = 1 - core

    def remote(src, dst, send_sem, recv_sem, target):
        return pltpu.make_async_remote_copy(
            src_ref=src, dst_ref=dst, send_sem=send_sem, recv_sem=recv_sem, device_id=target, device_id_type=MESH
        )

    barrier = pltpu.get_barrier_semaphore()
    peers = [at(x, y, z, other)]
    peers += [at((x + d // 4) % 4, (y + d % 4) % 4, z, core) for d in range(1, 16)]
    peers += [at(x, y, (z + d) % 16, core) for d in range(1, 16)]
    peers += [at((x + d) % 4, y, z, other) for d in range(1, 4)]
    for dr, dc in ((1, 0), (0, 1), (1, 1)):
        for sign in (1, -1):
            peers.append({"lon": (lon + sign * dc + LON) % LON, "lat": (lat + sign * dr + LAT) % LAT})
    for peer in peers:
        pl.semaphore_signal(barrier, inc=1, device_id=peer, device_id_type=MESH)

    first_in = first_in_ref[...]
    upstream_low = upstream_ref[...]
    grad_s[:, 0:C] = dot_tn(first_in, query_grad_ref[...])
    grad_s[:, C : 2 * C] = dot_tn(first_in, key_grad_ref[...])
    grad_s[:, 2 * C : 3 * C] = dot_tn(first_in, value_grad_ref[...])
    grad_s[:, 3 * C : 4 * C] = dot_tn(context_ref[...], mid_low_ref[...])
    grad_s[:, 4 * C : 8 * C] = dot_tn(second_in_ref[...], hidden_grad_ref[...])
    spread = dot(hidden_low_ref[...], spread_ref[...]).astype(BF16)
    for part in range(4):
        grad_s[:, (8 + part) * C : (9 + part) * C] = dot_tn(spread[:, part * C : (part + 1) * C], upstream_low)
    for tile in range(TILES):
        rows_s[tile // 9, pl.ds(tile % 9, C, stride=9), :] = grad_s[:, tile * LANES : (tile + 1) * LANES]
    sub64 = lax.broadcasted_iota(jnp.int32, (64, LANES), 0)
    for half in range(2):
        for block in range(32):
            got = rows_s[half, 54 * block : 54 * block + 64, :]
            tail = jnp.where(sub64 == 54, extra_ref[block : block + 1, :], 0.0) if half == 0 else 0.0
            got = jnp.where(sub64 < 54, got, tail).astype(BF16)
            for part in range(4):
                grads[half, block // 8, part, block % 8] = got[16 * part : 16 * part + 16]

    pl.semaphore_wait(barrier, len(peers))
    sends = []

    core_copies = []
    for j in range(4):
        to = (y + 1 + j) % 4
        copy = remote(grads.at[other, to], core_r.at[to], core_ss.at[j], core_rs.at[j], at(x, y, z, other))
        copy.start()
        core_copies.append(copy)
    sends += core_copies
    back_copies = []
    for slot in (3, 2, 1):
        dr, dc = slot // 2, slot % 2
        copy = remote(
            back_ref.at[slot],
            back_r.at[3 - slot],
            back_ss.at[slot],
            back_rs.at[slot],
            {"lon": (lon + dc) % LON, "lat": (lat + dr) % LAT},
        )
        copy.start()
        back_copies.append((slot, copy))
    sends += [copy for _, copy in back_copies]

    plane_copies = {}
    for j in range(4):
        to_y = (y + 1 + j) % 4
        core_copies[j].wait_recv()
        for part in range(4):
            plane_s[to_y, part] = (grads[core, to_y, part].astype(F32) + core_r[to_y, part].astype(F32)).astype(BF16)
        for i in range(4):
            dx, dy = (i + 1) % 4, (j + 1) % 4
            d = dx * 4 + dy
            to_x = (x + dx) % 4
            if d == 0:
                plane_r[x * 4 + y] = plane_s[y, x]
                continue
            copy = remote(
                plane_s.at[to_y, to_x],
                plane_r.at[x * 4 + y],
                plane_ss.at[d],
                plane_rs.at[d],
                at(to_x, to_y, z, core),
            )
            copy.start()
            plane_copies[d] = copy
    sends += list(plane_copies.values())

    acc_s[...] = jnp.zeros((208, LANES), F32)
    row32 = lax.broadcasted_iota(jnp.int32, (32, 2 * LANES), 0).astype(F32)
    row128 = lax.broadcasted_iota(jnp.int32, (LANES, 2 * LANES), 0).astype(F32)

    def pair(ref, row):
        return jnp.concatenate([ref[pl.ds(row, 1), :], ref[pl.ds(row + DENSE // 2, 1), :]], axis=1)

    def scatter(step, carry):
        chosen = row32 == pair(high_ref, step)
        hot = jnp.where(row128 == pair(low_ref, step), 1.0, 0.0).astype(BF16)
        spread_out = [jnp.where(chosen, pair(score_ref, n * DENSE + step), 0.0) for n in range(HEADS)]
        acc_s[0 : 32 * HEADS, :] += dot_nt(jnp.concatenate(spread_out, axis=0).astype(BF16), hot)
        return carry

    lax.fori_loop(0, DENSE // 2, scatter, 0)
    sub16 = lax.broadcasted_iota(jnp.int32, (16, LANES), 0)
    for block in range(16):
        bias_s[block // 8, block % 8] = jnp.where(sub16 < 12, acc_s[12 * block : 12 * block + 16, :], 0.0)

    bcore = remote(bias_s.at[other], bcore_r, bcore_ss, bcore_rs, at(x, y, z, other))
    bcore.start()
    sends.append(bcore)
    bcore.wait_recv()
    for part in range(ZLO):
        bline_s[part] = bias_s[core, part] + bcore_r[part]
    bline_r[z_lo] = bline_s[z_lo]
    bline_copies = []
    for d in range(1, ZLO):
        to = (z_lo + d) % ZLO
        copy = remote(
            bline_s.at[to], bline_r.at[z_lo], bline_ss.at[d], bline_rs.at[d], at(x, y, z_hi * ZLO + to, core)
        )
        copy.start()
        bline_copies.append(copy)
    sends += bline_copies

    for copy in plane_copies.values():
        copy.wait_recv()
    for part in range(ZLO):
        block = plane_r[0, part].astype(F32)
        for source in range(1, 16):
            block = block + plane_r[source, part].astype(F32)
        line_s[part] = block.astype(BF16)
    line_r[z] = line_s[z_lo]
    line_copies = []
    for d in range(1, 16):
        to = (z + d) % 16
        copy = remote(line_s.at[to % ZLO], line_r.at[z], line_ss.at[d], line_rs.at[d], at(x, y, to, core))
        copy.start()
        line_copies.append(copy)
    sends += line_copies

    for copy in bline_copies:
        copy.wait_recv()
    part_sum = bline_r[0]
    for part in range(1, ZLO):
        part_sum = part_sum + bline_r[part]
    brow_r[y] = part_sum
    brow_copies = []
    for d in range(1, 4):
        to = (y + d) % 4
        copy = remote(brow_r.at[y], brow_r.at[y], brow_ss.at[d], brow_rs.at[d], at(x, to, z, core))
        copy.start()
        brow_copies.append(copy)
    sends += brow_copies

    for copy in brow_copies:
        copy.wait_recv()
    bias_part = (brow_r[0] + brow_r[1]) + (brow_r[2] + brow_r[3])
    ball[core, z_lo] = bias_part
    ball_copies = []
    for d in range(1, ZLO):
        to = (z_lo + d) % ZLO
        copy = remote(
            ball.at[core, z_lo], ball.at[core, z_lo], ball_ss.at[d], ball_rs.at[d], at(x, y, z_hi * ZLO + to, core)
        )
        copy.start()
        ball_copies.append(copy)
    sends += ball_copies

    for copy in line_copies:
        copy.wait_recv()
    piece = line_r[0].astype(F32)
    for source in range(1, 16):
        piece = piece + line_r[source].astype(F32)
    square = 0.5 * jnp.sum(piece * piece) + 0.25 * jnp.sum(bias_part * bias_part)
    mine = core * 4 + x
    share[mine, 0:16, :] = piece
    share[mine, 16:24, :] = jnp.full((8, LANES), square, F32)
    share_copies = []
    for dx, dcore in ((1, 0), (2, 0), (3, 0), (0, 1), (1, 1), (2, 1), (3, 1)):
        d = dcore * 4 + dx
        copy = remote(
            share.at[mine],
            share.at[mine],
            share_ss.at[d],
            share_rs.at[d],
            at((x + dx) % 4, y, z, core + dcore * (1 - 2 * core)),
        )
        copy.start()
        share_copies.append(copy)
    sends += share_copies

    for copy in ball_copies:
        copy.wait_recv()
    bpair = remote(ball.at[core], ball.at[core], bpair_ss, bpair_rs, at(x, y, z, other))
    bpair.start()
    sends.append(bpair)

    for copy in share_copies:
        copy.wait_recv()
    square = share[0, 16:17, :]
    for source in range(1, 8):
        square = square + share[source, 16:17, :]
    squares_z[z] = square
    sz_copies = []
    for d in range(1, 16):
        to = (z + d) % 16
        copy = remote(squares_z.at[z], squares_z.at[z], sz_ss.at[d], sz_rs.at[d], at(x, y, to, core))
        copy.start()
        sz_copies.append(copy)
    sends += sz_copies
    for source in range(8):
        dense_out[source] = share[source, 0:16, :]
    back_out[3] = back_ref[0]
    for slot, copy in back_copies:
        copy.wait_recv()
        back_out[3 - slot] = back_r[3 - slot]
    for copy in sz_copies:
        copy.wait_recv()
    square = squares_z[0]
    for source in range(1, 16):
        square = square + squares_z[source]
    squares_y[y] = square
    sy_copies = []
    for d in range(1, 4):
        copy = remote(squares_y.at[y], squares_y.at[y], sy_ss.at[d], sy_rs.at[d], at(x, (y + d) % 4, z, core))
        copy.start()
        sy_copies.append(copy)
    sends += sy_copies
    bpair.wait_recv()
    bias_out[...] = ball[...]
    for copy in sy_copies:
        copy.wait_recv()
    total_out[...] = (squares_y[0] + squares_y[1]) + (squares_y[2] + squares_y[3])
    for copy in sends:
        copy.wait_send()


def reduce(*operands):
    column = np.arange(FF)
    spread = np.zeros((FF, FF), np.float32)
    spread[4 * (column % C) + column // C, column] = 1.0
    vmem = pl.BlockSpec(memory_space=pltpu.VMEM)
    dma = pltpu.SemaphoreType.DMA
    return pl.pallas_call(
        reduce_kernel,
        out_shape=(
            jax.ShapeDtypeStruct((8, 16, LANES), F32),
            jax.ShapeDtypeStruct((2, ZLO, 16, LANES), F32),
            jax.ShapeDtypeStruct((4, 64, LANES), BF16),
            jax.ShapeDtypeStruct((1, LANES), F32),
        ),
        in_specs=[vmem] * 16,
        out_specs=(vmem,) * 4,
        scratch_shapes=[
            pltpu.VMEM((C, COLS), F32),
            pltpu.VMEM((2, 9 * C + 16, LANES), F32),
            pltpu.VMEM((2, 4, 4, ZLO, 16, LANES), BF16),
            pltpu.VMEM((208, LANES), F32),
            pltpu.VMEM((2, ZLO, 16, LANES), F32),
            pltpu.VMEM((4, 4, ZLO, 16, LANES), BF16),
            pltpu.VMEM((4, 4, ZLO, 16, LANES), BF16),
            pltpu.VMEM((16, ZLO, 16, LANES), BF16),
            pltpu.VMEM((ZLO, 16, LANES), BF16),
            pltpu.VMEM((16, 16, LANES), BF16),
            pltpu.VMEM((8, 24, LANES), F32),
            pltpu.VMEM((ZLO, 16, LANES), F32),
            pltpu.VMEM((ZLO, 16, LANES), F32),
            pltpu.VMEM((ZLO, 16, LANES), F32),
            pltpu.VMEM((4, 16, LANES), F32),
            pltpu.VMEM((2, ZLO, 16, LANES), F32),
            pltpu.VMEM((4, 64, LANES), BF16),
            pltpu.VMEM((16, 1, LANES), F32),
            pltpu.VMEM((4, 1, LANES), F32),
            dma((4,)), dma((4,)),
            dma((16,)), dma((16,)),
            dma((16,)), dma((16,)),
            dma((8,)), dma((8,)),
            dma, dma,
            dma((8,)), dma((8,)),
            dma((4,)), dma((4,)),
            dma((8,)), dma((8,)),
            dma, dma,
            dma((4,)), dma((4,)),
            dma((16,)), dma((16,)),
            dma((4,)), dma((4,)),
        ],
        compiler_params=pltpu.CompilerParams(collective_id=1, has_side_effects=True, vmem_limit_bytes=VMEM_LIMIT),
        name="sum_over_devices",
    )(*operands, jnp.asarray(spread, BF16))


def output_kernel(
    dense_ref, bias_ref, back_ref, total_ref,
    token_ref, mix_ref, out_ref, up_ref, down_ref, gain_ref, embed_ref, table_ref,
    dense_s, flat_s, bias_s, back_s, token_s,
):
    count = C * COLS + (KINDS + 2) * C + LAT * HEADS * PAIRS
    factor = lax.rsqrt(total_ref[...] / count + RMS_EPS)
    odd = lax.axis_index("lon") % 2 == 1
    for part in range(8):
        dense_s[part // 4, 16 * (part % 4) : 16 * (part % 4) + 16, :] = dense_ref[part] * factor
    for tile in range(TILES):
        half, t = tile // 9, tile % 9
        even_rows = dense_s[half, pl.ds(t, 3, stride=9), :]
        odd_rows = dense_s[half, pl.ds(27 + t, 3, stride=9), :]
        flat_s[0:3, tile * LANES : (tile + 1) * LANES] = jnp.where(odd, odd_rows, even_rows)
    flat = flat_s[0:3, :]
    mix_ref[...] = flat[:, 0 : 3 * C]
    out_ref[...] = flat[:, 3 * C : 4 * C]
    up_ref[...] = flat[:, 4 * C : 8 * C]
    for row in range(3):
        for part in range(4):
            down_ref[4 * row + part : 4 * row + part + 1, :] = flat[row : row + 1, (8 + part) * C : (9 + part) * C]
    extra = dense_s[0, 54:55, :]
    lane = lax.broadcasted_iota(jnp.int32, (24, LANES), 1)
    sub = lax.broadcasted_iota(jnp.int32, (24, LANES), 0)
    small = jnp.zeros((24, LANES), F32)
    wide = jnp.zeros((8, LANES), F32)
    sub8 = lax.broadcasted_iota(jnp.int32, (8, LANES), 0)
    line8 = jnp.broadcast_to(extra, (8, LANES))
    for row in range(3):
        turned = jnp.where(odd, pltpu.roll(line8, LANES - 18 * (3 + row), 1), pltpu.roll(line8, (LANES - 18 * row) % LANES, 1))
        wide = jnp.where(sub8 == row, turned, wide)
        start = jnp.where(odd, 18 * (3 + row), 18 * row)
        column = jnp.sum(jnp.where(lane == sub + start, extra, 0.0), axis=1, keepdims=True)
        small = small + jnp.where(lane == row, column, 0.0)
    embed_ref[...] = wide[0:3, 0:KINDS]
    gain_ref[...] = small[KINDS : KINDS + 2, 0:3]
    for block in range(16):
        bias_s[12 * block : 12 * block + 12, :] = bias_ref[block // 8, block % 8, 0:12, :] * factor
    for row in range(HI):
        width = min(LANES, PAIRS - row * LANES)
        line = bias_s[pl.ds(row, HEADS, stride=32), :][:, 0:width]
        for head in range(HEADS):
            table_ref[head, :, row * LANES : row * LANES + width] = line[head : head + 1]
    for quarter in range(4):
        packed = back_ref[quarter].astype(F32)
        for tile in range(3):
            back_s[quarter, 0:CELLS, tile * LANES : (tile + 1) * LANES] = packed[CELLS * tile : CELLS * tile + CELLS]
        for i in range(3):
            row, half = 3 * (quarter // 2) + i, quarter % 2
            token_s[row, 6 * half : 6 * half + 6, :] = back_s[quarter, 6 * i : 6 * i + 6, :]
    for row in range(WIN_LAT):
        token_ref[row] = token_s[row, 0:WIN_LON, :].astype(BF16)


def outputs(dense, bias, back, total):
    vmem = pl.BlockSpec(memory_space=pltpu.VMEM)
    return pl.pallas_call(
        output_kernel,
        out_shape=(
            jax.ShapeDtypeStruct((WIN_LAT, WIN_LON, 2 * C), BF16),
            jax.ShapeDtypeStruct((3, 3 * C), F32),
            jax.ShapeDtypeStruct((3, C), F32),
            jax.ShapeDtypeStruct((3, FF), F32),
            jax.ShapeDtypeStruct((12, C), F32),
            jax.ShapeDtypeStruct((2, 3), F32),
            jax.ShapeDtypeStruct((3, KINDS), F32),
            jax.ShapeDtypeStruct((HEADS, 1, PAIRS), F32),
        ),
        in_specs=[vmem] * 4,
        out_specs=(vmem,) * 8,
        scratch_shapes=[
            pltpu.VMEM((2, 64, LANES), F32),
            pltpu.VMEM((8, COLS), F32),
            pltpu.VMEM((HEADS * 32, LANES), F32),
            pltpu.VMEM((4, 32, 2 * C), F32),
            pltpu.VMEM((WIN_LAT, 16, 2 * C), F32),
        ],
        compiler_params=pltpu.CompilerParams(vmem_limit_bytes=VMEM_LIMIT),
        name="scaled_outputs",
    )(dense, bias, back, total)


def shards(
    tokens, kinds, kind_embed, pair_index, bias_table, attn_gain, mlp_gain,
    mix_weight, out_weight, up_weight, down_weight, cotangent,
):
    block, bias, high, low = halo(
        tokens, kinds.transpose(0, 2, 1), kind_embed, cotangent, pair_index, bias_table.transpose(1, 0, 2)
    )
    parts = window(
        block, bias, attn_gain.reshape(1, C), mlp_gain.reshape(1, C), mix_weight, out_weight, up_weight, down_weight.T
    )
    token, mix, out, up, down, gain, embed, table = outputs(*reduce(*parts, high, low))
    return token, mix, out, up, down, gain, embed.T, table.transpose(1, 0, 2)


def solution(mesh):
    return jax.shard_map(
        shards,
        mesh=mesh,
        in_specs=(
            P("lat", "lon", None),
            P("lat", "lon", None),
            P(),
            P(),
            P("lat", None, None),
            P(),
            P(),
            P(),
            P(),
            P(),
            P(),
            P("lat", "lon", None),
        ),
        out_specs=(
            P("lat", "lon", None),
            P("lon", None),
            P("lon", None),
            P("lon", None),
            P("lon", None),
            P(None, "lon"),
            P(None, "lon"),
            P("lat", None, None),
        ),
        check_vma=False,
    )
```

```python
import jax
import jax.numpy as jnp
import numpy as np
from jax import lax
from jax.experimental import pallas as pl
from jax.experimental.pallas import tpu as pltpu
from jax.sharding import PartitionSpec as P

F32 = jnp.float32
BF16 = jnp.bfloat16
MESH = pl.DeviceIdType.MESH

C = 192
HEADS = 6
HEAD = 32
FF = 768
WIN_LAT = 6
WIN_LON = 12
KINDS = 16
PAIRS = 3312
TOK = 144
CELLS = 18
PART = 36
LANES = 128
HI = 26
COLS = 2304
TILES = 18
NORM_EPS = 1e-05
RMS_EPS = 1e-06
GELU_SQRT = 0.7978845608028654
GELU_CUBE = 0.044715
LON, LAT = 64, 8
ZLO = 8
VMEM_LIMIT = 56 * 1024 * 1024


def place():
    lon, lat = lax.axis_index("lon"), lax.axis_index("lat")
    return lat >> 1, lon >> 4, ((lat & 1) << 3) + ((lon >> 1) & 7), lon & 1


def at(x, y, z, core):
    return {"lon": (y << 4) + ((z & 7) << 1) + core, "lat": (x << 1) + (z >> 3)}


def beside(lat, lon, rows, columns):
    return {"lon": (lon + columns) & (LON - 1), "lat": (lat + rows) & (LAT - 1)}


def dot(a, b):
    return lax.dot_general(a, b, (((1,), (0,)), ((), ())), preferred_element_type=F32)


def dot_nt(a, b):
    return lax.dot_general(a, b, (((1,), (1,)), ((), ())), preferred_element_type=F32)


def dot_tn(a, b):
    return lax.dot_general(a, b, (((0,), (0,)), ((), ())), preferred_element_type=F32)


def two_terms(v):
    high = v.astype(BF16)
    return high, (v - high.astype(F32)).astype(BF16)


def dense_rows(ref, values, base):
    ref[base : base + TOK, :] = values[:, 0:LANES]
    tail = values[:, LANES:TOK]
    tail = jnp.concatenate([tail, jnp.zeros((TOK, LANES - 16), tail.dtype)], axis=1)
    row = tail[0:16]
    for group in range(1, 8):
        row = row + pltpu.roll(tail[16 * group : 16 * group + 16], 16 * group, 1)
    ref[base + TOK : base + TOK + 16, :] = row
    ref[base + TOK + 16 : base + TOK + 32, :] = tail[LANES:TOK]


DENSE = TOK + 32
FLAT = 3 * PART
SENT = FLAT + 4


def layer_norm(values, gain):
    centred = values - jnp.mean(values, axis=-1, keepdims=True)
    inverse = lax.rsqrt(jnp.mean(centred * centred, axis=-1, keepdims=True) + NORM_EPS)
    normed = centred * inverse
    return normed * gain, normed, inverse


def norm_backward(upstream, normed, inverse, gain):
    scaled = upstream * gain
    return inverse * (
        scaled
        - jnp.mean(scaled, axis=-1, keepdims=True)
        - normed * jnp.mean(scaled * normed, axis=-1, keepdims=True)
    )


def main_kernel(
    tok_ref, kind_ref, embed_ref, cot_ref, index_ref, table_ref, order_ref,
    gain1_ref, gain2_ref, mix_ref, outw_ref, up_ref, down_ref,
    dense_out, bias_out, back_out, total_out,
    tok_s, kind_s, flat_s, pack_s, send, recv, table_s, dense_s, high_s, low_s, bias_s, spread_s,
    grid_s, x_s, g_s, hot_s, ge_s, moved_s, unpack_s, score_s, extra_s, back_s,
    grad_s, rows_s, grads, acc_s, parts_s,
    core_r, plane_s, plane_r, line_s, line_r, share, bcore_r, bline_s, bline_r, brow_r, ball, back_r, squares_z, squares_y,
    halo_ss, halo_rs,
    core_ss, core_rs, plane_ss, plane_rs, line_ss, line_rs, share_ss, share_rs, bcore_ss, bcore_rs, bline_ss, bline_rs,
    brow_ss, brow_rs, ball_ss, ball_rs, bpair_ss, bpair_rs, back_ss, back_rs, sz_ss, sz_rs, sy_ss, sy_rs,
):
    lon, lat = lax.axis_index("lon"), lax.axis_index("lat")
    x, y, z, core = place()
    z_lo, z_hi = z & 7, z >> 3
    other = 1 - core

    def remote(src, dst, send_sem, recv_sem, target):
        return pltpu.make_async_remote_copy(
            src_ref=src, dst_ref=dst, send_sem=send_sem, recv_sem=recv_sem, device_id=target, device_id_type=MESH
        )

    barrier = pltpu.get_barrier_semaphore()
    peers = []
    for dr, dc in ((1, 0), (0, 1), (1, 1)):
        peers += [beside(lat, lon, -dr, -dc), beside(lat, lon, dr, dc)]
    peers += [at(x, y, (z + d) & 15, core) for d in range(1, 16)]
    peers += [at((x + d // 4) & 3, (y + d % 4) & 3, z, core) for d in range(1, 16)]
    peers += [at((x + d) & 3, y, z, other) for d in range(4)]
    for peer in peers:
        pl.semaphore_signal(barrier, inc=1, device_id=peer, device_id_type=MESH)

    embed = embed_ref[...].astype(F32)
    blank = jnp.zeros((KINDS, C), F32)
    wide = jnp.concatenate(
        [jnp.concatenate([embed, blank], axis=1), jnp.concatenate([blank, embed], axis=1)], axis=0
    ).astype(BF16)
    kind_s[...] = jnp.zeros((4, 8, LANES), F32)
    for row in range(WIN_LAT):
        tok = tok_ref[row].astype(F32)
        cot = cot_ref[row].astype(F32)
        kind = kind_ref[row].astype(F32)
        for half in range(2):
            quarter = 2 * (row // 3) + half
            start = 6 * (row % 3)
            cells = slice(6 * half, 6 * half + 6)
            tok_s[quarter, start : start + 6, :] = tok[cells]
            flat_s[quarter, CELLS + start : CELLS + start + 6, :] = cot[cells]
            kind_s[quarter, 0:2, start : start + 6] = kind[:, cells]
    sub = lax.broadcasted_iota(jnp.int32, (2 * KINDS, LANES), 0).astype(F32)
    for quarter in range(4):
        kinds = kind_s[quarter]
        hot = (sub == kinds[0:1]) | (sub - KINDS == kinds[1:2])
        hot = jnp.where(hot, 1.0, 0.0).astype(BF16)[:, 0:24]
        stored = tok_s[quarter] + dot_tn(hot, wide)
        flat_s[quarter, 0:CELLS, :] = stored[0:CELLS]
        for tile in range(3):
            pack_s[quarter, PART * tile : PART * tile + PART, :] = flat_s[
                quarter, 0:PART, tile * LANES : (tile + 1) * LANES
            ]
        pack_s[quarter, FLAT:SENT, :] = jnp.zeros((4, LANES), F32)
        pack_s[quarter, FLAT : FLAT + 1, :] = kinds[0:1] + pltpu.roll(kinds, CELLS, 1)[1:2]
        send[quarter] = pack_s[quarter].astype(BF16)
    order = order_ref[...]
    index = index_ref[...]
    high = (index // LANES).astype(F32).astype(BF16)
    low = (index % LANES).astype(F32).astype(BF16)
    dense_rows(high_s, dot_nt(dot(order, high).astype(BF16), order), 0)
    dense_rows(low_s, dot_nt(dot(order, low).astype(BF16), order), 0)
    table_s[...] = jnp.zeros((HEADS * 32, LANES), F32)
    for row in range(HI):
        width = min(LANES, PAIRS - row * LANES)
        for head in range(HEADS):
            table_s[32 * head + row : 32 * head + row + 1, 0:width] = table_ref[
                head, :, row * LANES : row * LANES + width
            ]

    column = lax.broadcasted_iota(jnp.int32, (1, FF), 1)
    part = jnp.where(column >= C, 1, 0) + jnp.where(column >= 2 * C, 1, 0) + jnp.where(column >= 3 * C, 1, 0)
    unit = (4 * (column - C * part) + part).astype(F32)
    for block in range(6):
        place_at = (lax.broadcasted_iota(jnp.int32, (LANES, FF), 0) + LANES * block).astype(F32)
        spread_s[LANES * block : LANES * (block + 1), :] = jnp.where(place_at == unit, 1.0, 0.0).astype(BF16)

    pl.semaphore_wait(barrier, len(peers))
    halo_copies = []
    for slot in (3, 2, 1):
        copy = remote(
            send.at[3 - slot], recv.at[slot], halo_ss.at[slot], halo_rs.at[slot], beside(lat, lon, -(slot // 2), -(slot % 2))
        )
        copy.start()
        halo_copies.append(copy)
    sends = list(halo_copies)

    def gather(step, carry):
        start = pl.multiple_of(step * 16, 16)
        lows = low_s[pl.ds(start, 16), :].astype(jnp.int32)
        highs = high_s[pl.ds(start, 16), :]
        totals = [jnp.zeros((16, LANES), F32) for _ in range(HEADS)]
        for row in range(HI):
            chosen = highs == float(row)
            for head in range(HEADS):
                line = jnp.broadcast_to(table_s[32 * head + row : 32 * head + row + 1, :], (16, LANES))
                found = jnp.take_along_axis(line, lows, axis=1, mode="promise_in_bounds")
                totals[head] = jnp.where(chosen, found, totals[head])
        for head in range(HEADS):
            dense_s[pl.ds(pl.multiple_of(head * DENSE + start, 16), 16), :] = totals[head]
        return carry

    lax.fori_loop(0, DENSE // 16, gather, 0)
    for head in range(HEADS):
        base = head * DENSE
        bias_s[head * TOK : head * TOK + TOK, 0:LANES] = dense_s[base : base + TOK, :]
        row = dense_s[base + TOK : base + TOK + 16, :]
        for group in range(8):
            turned = row if group == 0 else pltpu.roll(row, LANES - 16 * group, 1)
            bias_s[head * TOK + 16 * group : head * TOK + 16 * group + 16, LANES:TOK] = turned[:, 0:16]
        bias_s[head * TOK + LANES : head * TOK + TOK, LANES:TOK] = dense_s[base + TOK + 16 : base + TOK + 32, 0:16]

    for copy in halo_copies:
        copy.wait_recv()
    lane36 = lax.broadcasted_iota(jnp.int32, (PART, LANES), 1)
    sub36 = lax.broadcasted_iota(jnp.int32, (PART, LANES), 0)
    for slot in range(4):
        unpack_s[slot] = (send[3] if slot == 0 else recv[slot]).astype(F32)
        for tile in range(3):
            grid_s[slot, 0:PART, tile * LANES : (tile + 1) * LANES] = unpack_s[slot, PART * tile : PART * tile + PART, :]
        toks = grid_s[slot, 0:CELLS, :]
        cots = grid_s[slot, CELLS:PART, :]
        base = PART * slot
        x_s[base : base + CELLS, :] = toks[:, 0:C]
        x_s[base + CELLS : base + PART, :] = toks[:, C : 2 * C]
        g_s[base : base + CELLS, :] = cots[:, 0:C]
        g_s[base + CELLS : base + PART, :] = cots[:, C : 2 * C]
        kind_row = unpack_s[slot, FLAT : FLAT + 1, :]
        kind_col = jnp.sum(jnp.where(lane36 == sub36, kind_row, 0.0), axis=1, keepdims=True)
        hot_s[base : base + PART, :] = jnp.where(lane36.astype(F32) == kind_col, 1.0, 0.0)

    gain1, gain2 = gain1_ref[...], gain2_ref[...]
    mix_weight, out_weight = mix_ref[...], outw_ref[...]
    up_weight, down_weight = up_ref[...], down_ref[...]
    residual = x_s[...]
    upstream = g_s[...]
    upstream_low = upstream.astype(BF16)
    first, hat1, inv1 = layer_norm(residual, gain1)
    first_in = first.astype(BF16)
    mixed = dot(first_in, mix_weight)
    queries = mixed[:, 0:C].astype(BF16).astype(F32)
    keys = mixed[:, C : 2 * C].astype(BF16)
    values = mixed[:, 2 * C : 3 * C].astype(BF16)
    channel = lax.broadcasted_iota(jnp.int32, (TOK, C), 1)
    of_head = [(channel >= HEAD * n) & (channel < HEAD * n + HEAD) for n in range(HEADS)]
    q_stack = jnp.concatenate([jnp.where(m, queries, 0.0) for m in of_head], axis=0).astype(BF16)
    scores = dot_nt(q_stack, keys) * (HEAD**-0.5) + bias_s[...]
    last = lat == LAT - 1
    group_q = ((lax.broadcasted_iota(jnp.int32, (HEADS * TOK, TOK), 0) // 72) % 2).astype(F32)
    group_k = (lax.broadcasted_iota(jnp.int32, (HEADS * TOK, TOK), 1) >= 72).astype(F32)
    allowed = jnp.abs(group_q - group_k) * jnp.where(last, 1.0, 0.0) < 0.5
    expon = jnp.where(allowed, jnp.exp(scores), 0.0)
    attend = expon / jnp.sum(expon, axis=-1, keepdims=True)
    attend_low = attend.astype(BF16)
    context = jnp.zeros((TOK, C), F32)
    for n in range(HEADS):
        context += jnp.where(of_head[n], dot(attend_low[n * TOK : (n + 1) * TOK], values), 0.0)
    context = context.astype(BF16)
    mid = residual + dot(context, out_weight)
    second, hat2, inv2 = layer_norm(mid, gain2)
    second_in = second.astype(BF16)
    inner = dot(second_in, up_weight)
    tangent = jnp.tanh(GELU_SQRT * (inner + GELU_CUBE * inner * inner * inner))
    hidden_low = (0.5 * inner * (1.0 + tangent)).astype(BF16)
    slope = 0.5 * (1.0 + tangent) + 0.5 * inner * (1.0 - tangent * tangent) * GELU_SQRT * (
        1.0 + 3.0 * GELU_CUBE * inner * inner
    )
    hidden_grad = (dot(upstream_low, down_weight) * slope).astype(BF16)
    second_grad = dot_nt(hidden_grad, up_weight)
    mid_grad = upstream + norm_backward(second_grad, hat2, inv2, gain2)
    mid_low = mid_grad.astype(BF16)
    context_grad = dot_nt(mid_low, out_weight).astype(BF16).astype(F32)
    c_stack = jnp.concatenate([jnp.where(m, context_grad, 0.0) for m in of_head], axis=0).astype(BF16)
    attend_grad = dot_nt(c_stack, values)
    value_grad = dot_tn(attend_low, c_stack).astype(BF16)
    score_grad = attend * (attend_grad - jnp.sum(attend * attend_grad, axis=-1, keepdims=True))
    score_s[...] = score_grad
    score_low = score_grad.astype(BF16)
    query_grad = jnp.zeros((TOK, C), F32)
    for n in range(HEADS):
        query_grad += jnp.where(of_head[n], dot(score_low[n * TOK : (n + 1) * TOK], keys), 0.0)
    query_grad = (query_grad * (HEAD**-0.5)).astype(BF16)
    key_grad = (dot_tn(score_low, q_stack) * (HEAD**-0.5)).astype(BF16)
    first_grad = (
        dot_nt(query_grad, mix_weight[:, 0:C])
        + dot_nt(key_grad, mix_weight[:, C : 2 * C])
        + dot_nt(value_grad, mix_weight[:, 2 * C : 3 * C])
    )
    moved = mid_grad + norm_backward(first_grad, hat1, inv1, gain1)

    moved_s[...] = moved
    for slot in range(4):
        base = PART * slot
        grid_s[slot, 0:CELLS, 0:C] = moved_s[base : base + CELLS, :]
        grid_s[slot, 0:CELLS, C : 2 * C] = moved_s[base + CELLS : base + PART, :]
        for tile in range(3):
            unpack_s[slot, CELLS * tile : CELLS * tile + CELLS, :] = grid_s[
                slot, 0:CELLS, tile * LANES : (tile + 1) * LANES
            ]
        back_s[slot] = unpack_s[slot, 0:64, :].astype(BF16)

    back_copies = []
    for slot in (3, 2, 1):
        copy = remote(
            back_s.at[slot], back_r.at[3 - slot], back_ss.at[slot], back_rs.at[slot], beside(lat, lon, slot // 2, slot % 2)
        )
        copy.start()
        back_copies.append((slot, copy))
    sends += [copy for _, copy in back_copies]

    lane = lax.broadcasted_iota(jnp.int32, (TOK, LANES), 1)
    small = jnp.zeros((C, LANES), F32)
    for left, right in (
        (moved, hot_s[...]),
        (first_grad * hat1, jnp.where(lane == KINDS, 1.0, 0.0)),
        (second_grad * hat2, jnp.where(lane == KINDS + 1, 1.0, 0.0)),
    ):
        for term in two_terms(left):
            small += dot_tn(term, right.astype(BF16))
    ge_s[...] = small
    extra = jnp.zeros((32, LANES), F32)
    for k in range(6):
        line = ge_s[pl.ds(k, 32, stride=6), :]
        extra += pltpu.roll(line, 18 * k, 1) if k else line
    extra_s[...] = extra

    grad_s[:, 0:C] = dot_tn(first_in, query_grad)
    grad_s[:, C : 2 * C] = dot_tn(first_in, key_grad)
    grad_s[:, 2 * C : 3 * C] = dot_tn(first_in, value_grad)
    grad_s[:, 3 * C : 4 * C] = dot_tn(context, mid_low)
    grad_s[:, 4 * C : 8 * C] = dot_tn(second_in, hidden_grad)
    spread = dot(hidden_low, spread_s[...]).astype(BF16)
    for part in range(4):
        grad_s[:, (8 + part) * C : (9 + part) * C] = dot_tn(spread[:, part * C : (part + 1) * C], upstream_low)
    for tile in range(TILES):
        for part in range(4):
            rows_s[tile // 9, part, pl.ds(tile % 9, 48, stride=9), :] = grad_s[
                48 * part : 48 * part + 48, tile * LANES : (tile + 1) * LANES
            ]
    sub64 = lax.broadcasted_iota(jnp.int32, (64, LANES), 0)

    def blocks(half, part):
        for block in range(ZLO):
            got = rows_s[half, part, 54 * block : 54 * block + 64, :]
            line = extra_s[pl.ds(part * ZLO + block, 1), :] * jnp.where(half == 0, 1.0, 0.0)
            got = jnp.where(sub64 < 54, got, jnp.where(sub64 == 54, line, 0.0)).astype(BF16)
            for quarter in range(4):
                grads[half, part, quarter, block] = got[16 * quarter : 16 * quarter + 16]

    core_copies = []
    for j in range(4):
        to = (y + 1 + j) & 3
        blocks(other, to)
        copy = remote(grads.at[other, to], core_r.at[to], core_ss.at[j], core_rs.at[j], at(x, y, z, other))
        copy.start()
        core_copies.append(copy)
    sends += core_copies
    plane_copies = {}
    for j in range(4):
        to_y = (y + 1 + j) & 3
        blocks(core, to_y)
        core_copies[j].wait_recv()
        for part in range(4):
            plane_s[to_y, part] = (grads[core, to_y, part].astype(F32) + core_r[to_y, part].astype(F32)).astype(BF16)
        for i in range(4):
            dx, dy = (i + 1) % 4, (j + 1) % 4
            d = dx * 4 + dy
            to_x = (x + dx) & 3
            if d == 0:
                plane_r[x * 4 + y] = plane_s[y, x]
                continue
            copy = remote(
                plane_s.at[to_y, to_x], plane_r.at[x * 4 + y], plane_ss.at[d], plane_rs.at[d], at(to_x, to_y, z, core)
            )
            copy.start()
            plane_copies[d] = copy
    sends += list(plane_copies.values())

    acc_s[...] = jnp.zeros((208, LANES), F32)
    for n in range(HEADS):
        dense_rows(dense_s, score_s[n * TOK : (n + 1) * TOK, :], n * DENSE)
    row32 = lax.broadcasted_iota(jnp.int32, (32, LANES), 0).astype(F32)
    row128 = lax.broadcasted_iota(jnp.int32, (LANES, LANES), 0).astype(F32)

    def scatter(step, carry):
        left, right = [], []
        start = pl.multiple_of(step * 16, 16)
        highs, lows = high_s[pl.ds(start, 16), :], low_s[pl.ds(start, 16), :]
        scores = [dense_s[pl.ds(pl.multiple_of(n * DENSE + start, 16), 16), :] for n in range(HEADS)]
        for row in range(16):
            chosen = row32 == highs[row : row + 1]
            right.append(jnp.where(row128 == lows[row : row + 1], 1.0, 0.0).astype(BF16))
            taken = [jnp.where(chosen, scores[n][row : row + 1], 0.0).astype(BF16) for n in range(HEADS)]
            left.append(jnp.concatenate(taken, axis=0))
        acc_s[0 : 32 * HEADS, :] += dot_nt(jnp.concatenate(left, axis=1), jnp.concatenate(right, axis=1))
        return carry

    lax.fori_loop(0, DENSE // 16, scatter, 0)
    sub16 = lax.broadcasted_iota(jnp.int32, (16, LANES), 0)
    for block in range(16):
        parts_s[block // 8, block % 8] = jnp.where(sub16 < 12, acc_s[12 * block : 12 * block + 16, :], 0.0)

    bcore = remote(parts_s.at[other], bcore_r, bcore_ss, bcore_rs, at(x, y, z, other))
    bcore.start()
    sends.append(bcore)
    bcore.wait_recv()
    for part in range(ZLO):
        bline_s[part] = parts_s[core, part] + bcore_r[part]
    bline_r[z_lo] = bline_s[z_lo]
    bline_copies = []
    for d in range(1, ZLO):
        to = (z_lo + d) & 7
        copy = remote(
            bline_s.at[to], bline_r.at[z_lo], bline_ss.at[d], bline_rs.at[d], at(x, y, z_hi * ZLO + to, core)
        )
        copy.start()
        bline_copies.append(copy)
    sends += bline_copies

    for copy in plane_copies.values():
        copy.wait_recv()
    for part in range(ZLO):
        block = plane_r[0, part].astype(F32)
        for source in range(1, 16):
            block = block + plane_r[source, part].astype(F32)
        line_s[part] = block.astype(BF16)
    line_r[z] = line_s[z_lo]
    line_copies = []
    for d in range(1, 16):
        to = (z + d) & 15
        copy = remote(line_s.at[to & 7], line_r.at[z], line_ss.at[d], line_rs.at[d], at(x, y, to, core))
        copy.start()
        line_copies.append(copy)
    sends += line_copies

    for copy in bline_copies:
        copy.wait_recv()
    part_sum = bline_r[0]
    for part in range(1, ZLO):
        part_sum = part_sum + bline_r[part]
    brow_r[y] = part_sum
    brow_copies = []
    for d in range(1, 4):
        to = (y + d) & 3
        copy = remote(brow_r.at[y], brow_r.at[y], brow_ss.at[d], brow_rs.at[d], at(x, to, z, core))
        copy.start()
        brow_copies.append(copy)
    sends += brow_copies

    for copy in brow_copies:
        copy.wait_recv()
    bias_part = (brow_r[0] + brow_r[1]) + (brow_r[2] + brow_r[3])
    ball[core, z_lo] = bias_part
    ball_copies = []
    for d in range(1, ZLO):
        to = (z_lo + d) & 7
        copy = remote(
            ball.at[core, z_lo], ball.at[core, z_lo], ball_ss.at[d], ball_rs.at[d], at(x, y, z_hi * ZLO + to, core)
        )
        copy.start()
        ball_copies.append(copy)
    sends += ball_copies

    for copy in line_copies:
        copy.wait_recv()
    piece = line_r[0].astype(F32)
    for source in range(1, 16):
        piece = piece + line_r[source].astype(F32)
    square = 0.5 * jnp.sum(piece * piece) + 0.25 * jnp.sum(bias_part * bias_part)
    mine = core * 4 + x
    share[mine, 0:16, :] = piece
    share[mine, 16:24, :] = jnp.full((8, LANES), square, F32)
    share_copies = []
    for dx, dcore in ((1, 0), (2, 0), (3, 0), (0, 1), (1, 1), (2, 1), (3, 1)):
        d = dcore * 4 + dx
        copy = remote(
            share.at[mine],
            share.at[mine],
            share_ss.at[d],
            share_rs.at[d],
            at((x + dx) & 3, y, z, core + dcore * (1 - 2 * core)),
        )
        copy.start()
        share_copies.append(copy)
    sends += share_copies

    for copy in share_copies:
        copy.wait_recv()
    square = share[0, 16:17, :]
    for source in range(1, 8):
        square = square + share[source, 16:17, :]
    squares_z[z] = square
    sz_copies = []
    for d in range(1, 16):
        to = (z + d) & 15
        copy = remote(squares_z.at[z], squares_z.at[z], sz_ss.at[d], sz_rs.at[d], at(x, y, to, core))
        copy.start()
        sz_copies.append(copy)
    sends += sz_copies
    for copy in ball_copies:
        copy.wait_recv()
    bpair = remote(ball.at[core], ball.at[core], bpair_ss, bpair_rs, at(x, y, z, other))
    bpair.start()
    sends.append(bpair)
    for source in range(8):
        dense_out[source] = share[source, 0:16, :]
    back_out[3] = back_s[0]
    for slot, copy in back_copies:
        copy.wait_recv()
        back_out[3 - slot] = back_r[3 - slot]
    for copy in sz_copies:
        copy.wait_recv()
    square = squares_z[0]
    for source in range(1, 16):
        square = square + squares_z[source]
    squares_y[y] = square
    sy_copies = []
    for d in range(1, 4):
        copy = remote(squares_y.at[y], squares_y.at[y], sy_ss.at[d], sy_rs.at[d], at(x, (y + d) & 3, z, core))
        copy.start()
        sy_copies.append(copy)
    sends += sy_copies
    bpair.wait_recv()
    bias_out[...] = ball[...]
    for copy in sy_copies:
        copy.wait_recv()
    total_out[...] = (squares_y[0] + squares_y[1]) + (squares_y[2] + squares_y[3])
    for copy in sends:
        copy.wait_send()


def main(*operands):
    token = np.arange(TOK)
    slot, level, cell = token // PART, (token % PART) // CELLS, token % CELLS
    row, col = 3 * (slot // 2) + cell // 6, 6 * (slot % 2) + cell % 6
    order = np.zeros((TOK, TOK), np.float32)
    order[token, (row * WIN_LON + col) * 2 + level] = 1.0
    operands = operands[:6] + (jnp.asarray(order, BF16),) + operands[6:]
    vmem = pl.BlockSpec(memory_space=pltpu.VMEM)
    dma = pltpu.SemaphoreType.DMA
    return pl.pallas_call(
        main_kernel,
        out_shape=(
            jax.ShapeDtypeStruct((8, 16, LANES), F32),
            jax.ShapeDtypeStruct((2, ZLO, 16, LANES), F32),
            jax.ShapeDtypeStruct((4, 64, LANES), BF16),
            jax.ShapeDtypeStruct((1, LANES), F32),
        ),
        in_specs=[vmem] * 13,
        out_specs=(vmem,) * 4,
        scratch_shapes=[
            pltpu.VMEM((4, 24, 2 * C), F32),
            pltpu.VMEM((4, 8, LANES), F32),
            pltpu.VMEM((4, 40, 2 * C), F32),
            pltpu.VMEM((4, SENT, LANES), F32),
            pltpu.VMEM((4, SENT, LANES), BF16),
            pltpu.VMEM((4, SENT, LANES), BF16),
            pltpu.VMEM((HEADS * 32, LANES), F32),
            pltpu.VMEM((HEADS * DENSE, LANES), F32),
            pltpu.VMEM((DENSE, LANES), F32),
            pltpu.VMEM((DENSE, LANES), F32),
            pltpu.VMEM((HEADS * TOK, TOK), F32),
            pltpu.VMEM((FF, FF), BF16),
            pltpu.VMEM((4, 40, 2 * C), F32),
            pltpu.VMEM((TOK, C), F32),
            pltpu.VMEM((TOK, C), F32),
            pltpu.VMEM((TOK, LANES), F32),
            pltpu.VMEM((C, LANES), F32),
            pltpu.VMEM((TOK, C), F32),
            pltpu.VMEM((4, SENT, LANES), F32),
            pltpu.VMEM((HEADS * TOK, TOK), F32),
            pltpu.VMEM((32, LANES), F32),
            pltpu.VMEM((4, 64, LANES), BF16),
            pltpu.VMEM((C, COLS), F32),
            pltpu.VMEM((2, 4, 448, LANES), F32),
            pltpu.VMEM((2, 4, 4, ZLO, 16, LANES), BF16),
            pltpu.VMEM((208, LANES), F32),
            pltpu.VMEM((2, ZLO, 16, LANES), F32),
            pltpu.VMEM((4, 4, ZLO, 16, LANES), BF16),
            pltpu.VMEM((4, 4, ZLO, 16, LANES), BF16),
            pltpu.VMEM((16, ZLO, 16, LANES), BF16),
            pltpu.VMEM((ZLO, 16, LANES), BF16),
            pltpu.VMEM((16, 16, LANES), BF16),
            pltpu.VMEM((8, 24, LANES), F32),
            pltpu.VMEM((ZLO, 16, LANES), F32),
            pltpu.VMEM((ZLO, 16, LANES), F32),
            pltpu.VMEM((ZLO, 16, LANES), F32),
            pltpu.VMEM((4, 16, LANES), F32),
            pltpu.VMEM((2, ZLO, 16, LANES), F32),
            pltpu.VMEM((4, 64, LANES), BF16),
            pltpu.VMEM((16, 1, LANES), F32),
            pltpu.VMEM((4, 1, LANES), F32),
            dma((4,)), dma((4,)),
            dma((4,)), dma((4,)),
            dma((16,)), dma((16,)),
            dma((16,)), dma((16,)),
            dma((8,)), dma((8,)),
            dma, dma,
            dma((8,)), dma((8,)),
            dma((4,)), dma((4,)),
            dma((8,)), dma((8,)),
            dma, dma,
            dma((4,)), dma((4,)),
            dma((16,)), dma((16,)),
            dma((4,)), dma((4,)),
        ],
        compiler_params=pltpu.CompilerParams(collective_id=0, has_side_effects=True, vmem_limit_bytes=VMEM_LIMIT),
        name="window_and_sums",
    )(*operands)


def output_kernel(
    dense_ref, bias_ref, back_ref, total_ref,
    token_ref, mix_ref, out_ref, up_ref, down_ref, gain_ref, embed_ref, table_ref,
    dense_s, flat_s, bias_s, back_s, token_s,
):
    count = C * COLS + (KINDS + 2) * C + LAT * HEADS * PAIRS
    factor = lax.rsqrt(total_ref[...] / count + RMS_EPS)
    odd = lax.axis_index("lon") % 2 == 1
    for part in range(8):
        dense_s[part // 4, 16 * (part % 4) : 16 * (part % 4) + 16, :] = dense_ref[part] * factor
    for tile in range(TILES):
        half, t = tile // 9, tile % 9
        even_rows = dense_s[half, pl.ds(t, 3, stride=9), :]
        odd_rows = dense_s[half, pl.ds(27 + t, 3, stride=9), :]
        flat_s[0:3, tile * LANES : (tile + 1) * LANES] = jnp.where(odd, odd_rows, even_rows)
    flat = flat_s[0:3, :]
    mix_ref[...] = flat[:, 0 : 3 * C]
    out_ref[...] = flat[:, 3 * C : 4 * C]
    up_ref[...] = flat[:, 4 * C : 8 * C]
    for row in range(3):
        for part in range(4):
            down_ref[4 * row + part : 4 * row + part + 1, :] = flat[row : row + 1, (8 + part) * C : (9 + part) * C]
    extra = dense_s[0, 54:55, :]
    lane = lax.broadcasted_iota(jnp.int32, (24, LANES), 1)
    sub = lax.broadcasted_iota(jnp.int32, (24, LANES), 0)
    small = jnp.zeros((24, LANES), F32)
    wide = jnp.zeros((8, LANES), F32)
    sub8 = lax.broadcasted_iota(jnp.int32, (8, LANES), 0)
    line8 = jnp.broadcast_to(extra, (8, LANES))
    for row in range(3):
        turned = jnp.where(odd, pltpu.roll(line8, LANES - 18 * (3 + row), 1), pltpu.roll(line8, (LANES - 18 * row) % LANES, 1))
        wide = jnp.where(sub8 == row, turned, wide)
        start = jnp.where(odd, 18 * (3 + row), 18 * row)
        column = jnp.sum(jnp.where(lane == sub + start, extra, 0.0), axis=1, keepdims=True)
        small = small + jnp.where(lane == row, column, 0.0)
    embed_ref[...] = wide[0:3, 0:KINDS]
    gain_ref[...] = small[KINDS : KINDS + 2, 0:3]
    for block in range(16):
        bias_s[12 * block : 12 * block + 12, :] = bias_ref[block // 8, block % 8, 0:12, :] * factor
    for row in range(HI):
        width = min(LANES, PAIRS - row * LANES)
        line = bias_s[pl.ds(row, HEADS, stride=32), :][:, 0:width]
        for head in range(HEADS):
            table_ref[head, :, row * LANES : row * LANES + width] = line[head : head + 1]
    for quarter in range(4):
        packed = back_ref[quarter].astype(F32)
        for tile in range(3):
            back_s[quarter, 0:CELLS, tile * LANES : (tile + 1) * LANES] = packed[CELLS * tile : CELLS * tile + CELLS]
        for i in range(3):
            row, half = 3 * (quarter // 2) + i, quarter % 2
            token_s[row, 6 * half : 6 * half + 6, :] = back_s[quarter, 6 * i : 6 * i + 6, :]
    for row in range(WIN_LAT):
        token_ref[row] = token_s[row, 0:WIN_LON, :].astype(BF16)


def outputs(dense, bias, back, total):
    vmem = pl.BlockSpec(memory_space=pltpu.VMEM)
    return pl.pallas_call(
        output_kernel,
        out_shape=(
            jax.ShapeDtypeStruct((WIN_LAT, WIN_LON, 2 * C), BF16),
            jax.ShapeDtypeStruct((3, 3 * C), F32),
            jax.ShapeDtypeStruct((3, C), F32),
            jax.ShapeDtypeStruct((3, FF), F32),
            jax.ShapeDtypeStruct((12, C), F32),
            jax.ShapeDtypeStruct((2, 3), F32),
            jax.ShapeDtypeStruct((3, KINDS), F32),
            jax.ShapeDtypeStruct((HEADS, 1, PAIRS), F32),
        ),
        in_specs=[vmem] * 4,
        out_specs=(vmem,) * 8,
        scratch_shapes=[
            pltpu.VMEM((2, 64, LANES), F32),
            pltpu.VMEM((8, COLS), F32),
            pltpu.VMEM((HEADS * 32, LANES), F32),
            pltpu.VMEM((4, 32, 2 * C), F32),
            pltpu.VMEM((WIN_LAT, 16, 2 * C), F32),
        ],
        compiler_params=pltpu.CompilerParams(vmem_limit_bytes=VMEM_LIMIT),
        name="scaled_outputs",
    )(dense, bias, back, total)


def shards(
    tokens, kinds, kind_embed, pair_index, bias_table, attn_gain, mlp_gain,
    mix_weight, out_weight, up_weight, down_weight, cotangent,
):
    sums = main(
        tokens, kinds.transpose(0, 2, 1), kind_embed, cotangent, pair_index, bias_table.transpose(1, 0, 2),
        attn_gain.reshape(1, C), mlp_gain.reshape(1, C), mix_weight, out_weight, up_weight, down_weight.T,
    )
    token, mix, out, up, down, gain, embed, table = outputs(*sums)
    return token, mix, out, up, down, gain, embed.T, table.transpose(1, 0, 2)


def solution(mesh):
    return jax.shard_map(
        shards,
        mesh=mesh,
        in_specs=(
            P("lat", "lon", None),
            P("lat", "lon", None),
            P(),
            P(),
            P("lat", None, None),
            P(),
            P(),
            P(),
            P(),
            P(),
            P(),
            P("lat", "lon", None),
        ),
        out_specs=(
            P("lat", "lon", None),
            P("lon", None),
            P("lon", None),
            P("lon", None),
            P("lon", None),
            P(None, "lon"),
            P(None, "lon"),
            P("lat", None, None),
        ),
        check_vma=False,
    )
```

```python
import jax
import jax.numpy as jnp
import numpy as np
from jax import lax
from jax.experimental import pallas as pl
from jax.experimental.pallas import tpu as pltpu
from jax.sharding import PartitionSpec as P

F32 = jnp.float32
BF16 = jnp.bfloat16
MESH = pl.DeviceIdType.MESH

C = 192
HEADS = 6
HEAD = 32
FF = 768
WIN_LAT = 6
WIN_LON = 12
KINDS = 16
PAIRS = 3312
TOK = 144
CELLS = 18
PART = 36
LANES = 128
HI = 26
COLS = 2304
TILES = 18
NORM_EPS = 1e-05
RMS_EPS = 1e-06
GELU_SQRT = 0.7978845608028654
GELU_CUBE = 0.044715
LON, LAT = 64, 8
ZLO = 8
VMEM_LIMIT = 56 * 1024 * 1024


def coords(lat, lon):
    return lat >> 1, lon >> 4, ((lat & 1) << 3) + ((lon >> 1) & 7), lon & 1


def at(x, y, z, core):
    return {"lon": (y << 4) + ((z & 7) << 1) + core, "lat": (x << 1) + (z >> 3)}


def beside(lat, lon, rows, columns):
    return {"lon": (lon + columns) & (LON - 1), "lat": (lat + rows) & (LAT - 1)}


def dot(a, b):
    return lax.dot_general(a, b, (((1,), (0,)), ((), ())), preferred_element_type=F32)


def dot_nt(a, b):
    return lax.dot_general(a, b, (((1,), (1,)), ((), ())), preferred_element_type=F32)


def dot_tn(a, b):
    return lax.dot_general(a, b, (((0,), (0,)), ((), ())), preferred_element_type=F32)


def two_terms(v):
    high = v.astype(BF16)
    return high, (v - high.astype(F32)).astype(BF16)


def dense_rows(ref, values, base):
    ref[base : base + TOK, :] = values[:, 0:LANES]
    tail = values[:, LANES:TOK]
    tail = jnp.concatenate([tail, jnp.zeros((TOK, LANES - 16), tail.dtype)], axis=1)
    row = tail[0:16]
    for group in range(1, 8):
        row = row + pltpu.roll(tail[16 * group : 16 * group + 16], 16 * group, 1)
    ref[base + TOK : base + TOK + 16, :] = row
    ref[base + TOK + 16 : base + TOK + 32, :] = tail[LANES:TOK]


DENSE = TOK + 32
FLAT = 3 * PART
SENT = FLAT + 4


def layer_norm(values, gain):
    centred = values - jnp.mean(values, axis=-1, keepdims=True)
    inverse = lax.rsqrt(jnp.mean(centred * centred, axis=-1, keepdims=True) + NORM_EPS)
    normed = centred * inverse
    return normed * gain, normed, inverse


def norm_backward(upstream, normed, inverse, gain):
    scaled = upstream * gain
    return inverse * (
        scaled
        - jnp.mean(scaled, axis=-1, keepdims=True)
        - normed * jnp.mean(scaled * normed, axis=-1, keepdims=True)
    )


def main_kernel(
    tok_in, kind_in, embed_in, cot_in, index_in, table_in, order_in,
    gain1_in, gain2_in, mix_in, outw_in, up_in, down_in,
    dense_out, bias_out, back_out, total_out,
    tok_ref, kind_ref, embed_ref, cot_ref, index_ref, table_ref, order_ref,
    gain1_ref, gain2_ref, mix_ref, outw_ref, up_ref, down_ref,
    tok_s, kind_s, flat_s, pack_s, send, recv, table_s, dense_s, high_s, low_s, bias_s, spread_s,
    grid_s, x_s, g_s, hot_s, ge_s, moved_s, unpack_s, score_s, extra_s, back_s,
    grad_s, rows_s, grads, acc_s, parts_s,
    core_r, plane_s, plane_r, line_s, line_r, share, bcore_r, bline_s, bline_r, brow_r, ball, back_r, squares_z, squares_y,
    relay, in_sems, relay_ss, relay_rs, halo_ss, halo_rs,
    core_ss, core_rs, plane_ss, plane_rs, line_ss, line_rs, share_ss, share_rs, bcore_ss, bcore_rs, bline_ss, bline_rs,
    brow_ss, brow_rs, ball_ss, ball_rs, bpair_ss, bpair_rs, back_ss, back_rs, sz_ss, sz_rs, sy_ss, sy_rs,
):
    lon, lat = lax.axis_index("lon"), lax.axis_index("lat")
    x, y, z, core = coords(lat, lon)
    z_lo, z_hi = z & 7, z >> 3
    other = 1 - core

    def remote(src, dst, send_sem, recv_sem, target):
        return pltpu.make_async_remote_copy(
            src_ref=src, dst_ref=dst, send_sem=send_sem, recv_sem=recv_sem, device_id=target, device_id_type=MESH
        )

    sources = (
        tok_in, kind_in, embed_in, cot_in, index_in, table_in, order_in,
        gain1_in, gain2_in, mix_in, outw_in, up_in, down_in,
    )
    targets = (
        tok_ref, kind_ref, embed_ref, cot_ref, index_ref, table_ref, order_ref,
        gain1_ref, gain2_ref, mix_ref, outw_ref, up_ref, down_ref,
    )
    fetches = [pltpu.make_async_copy(s, t, in_sems.at[i]) for i, (s, t) in enumerate(zip(sources, targets))]
    for fetch in fetches[:4]:
        fetch.start()

    below, above = at(x, y, z - 4 & 15, core), at(x, y, z + 4 & 15, core)
    relay_to = {2: below, 3: above}
    relayed_to = {
        2: beside(above["lat"], above["lon"], -1, 0),
        3: beside(below["lat"], below["lon"], -1, -1),
    }
    south = beside(lat, lon, 1, 0)
    south_x, south_y, south_z, south_c = coords(south["lat"], south["lon"])
    corner = beside(lat, lon, 1, 1)
    corner_x, corner_y, corner_z, corner_c = coords(corner["lat"], corner["lon"])
    barrier = pltpu.get_barrier_semaphore()
    peers = [relayed_to[2], relayed_to[3]]
    peers += [at(south_x, south_y, south_z - 4 & 15, south_c), at(corner_x, corner_y, corner_z + 4 & 15, corner_c)]
    for dr, dc in ((1, 0), (0, 1), (1, 1)):
        peers += [beside(lat, lon, -dr, -dc), beside(lat, lon, dr, dc)]
    peers += [at(x, y, (z + d) & 15, core) for d in range(1, 16)]
    peers += [at((x + d // 4) & 3, (y + d % 4) & 3, z, core) for d in range(1, 16)]
    peers += [at((x + d) & 3, y, z, other) for d in range(4)]
    for peer in peers:
        pl.semaphore_signal(barrier, inc=1, device_id=peer, device_id_type=MESH)

    for fetch in fetches[4:]:
        fetch.start()
    for fetch in fetches[:4]:
        fetch.wait()
    embed = embed_ref[...].astype(F32)
    blank = jnp.zeros((KINDS, C), F32)
    wide = jnp.concatenate(
        [jnp.concatenate([embed, blank], axis=1), jnp.concatenate([blank, embed], axis=1)], axis=0
    ).astype(BF16)
    kind_s[...] = jnp.zeros((4, 8, LANES), F32)
    for row in range(WIN_LAT):
        tok = tok_ref[row].astype(F32)
        cot = cot_ref[row].astype(F32)
        kind = kind_ref[row].astype(F32)
        for half in range(2):
            quarter = 2 * (row // 3) + half
            start = 6 * (row % 3)
            cells = slice(6 * half, 6 * half + 6)
            tok_s[quarter, start : start + 6, :] = tok[cells]
            flat_s[quarter, CELLS + start : CELLS + start + 6, :] = cot[cells]
            kind_s[quarter, 0:2, start : start + 6] = kind[:, cells]
    sub = lax.broadcasted_iota(jnp.int32, (2 * KINDS, LANES), 0).astype(F32)
    for quarter in range(4):
        kinds = kind_s[quarter]
        hot = (sub == kinds[0:1]) | (sub - KINDS == kinds[1:2])
        hot = jnp.where(hot, 1.0, 0.0).astype(BF16)[:, 0:24]
        stored = tok_s[quarter] + dot_tn(hot, wide)
        flat_s[quarter, 0:CELLS, :] = stored[0:CELLS]
        for tile in range(3):
            pack_s[quarter, PART * tile : PART * tile + PART, :] = flat_s[
                quarter, 0:PART, tile * LANES : (tile + 1) * LANES
            ]
        pack_s[quarter, FLAT:SENT, :] = jnp.zeros((4, LANES), F32)
        pack_s[quarter, FLAT : FLAT + 1, :] = kinds[0:1] + pltpu.roll(kinds, CELLS, 1)[1:2]
        send[quarter] = pack_s[quarter].astype(BF16)
    for fetch in fetches[4:7]:
        fetch.wait()
    order = order_ref[...]
    index = index_ref[...]
    high = (index // LANES).astype(F32).astype(BF16)
    low = (index % LANES).astype(F32).astype(BF16)
    dense_rows(high_s, dot_nt(dot(order, high).astype(BF16), order), 0)
    dense_rows(low_s, dot_nt(dot(order, low).astype(BF16), order), 0)
    table_s[...] = jnp.zeros((HEADS * 32, LANES), F32)
    for row in range(HI):
        width = min(LANES, PAIRS - row * LANES)
        for head in range(HEADS):
            table_s[32 * head + row : 32 * head + row + 1, 0:width] = table_ref[
                head, :, row * LANES : row * LANES + width
            ]

    column = lax.broadcasted_iota(jnp.int32, (1, FF), 1)
    part = jnp.where(column >= C, 1, 0) + jnp.where(column >= 2 * C, 1, 0) + jnp.where(column >= 3 * C, 1, 0)
    unit = (4 * (column - C * part) + part).astype(F32)
    for block in range(6):
        place_at = (lax.broadcasted_iota(jnp.int32, (LANES, FF), 0) + LANES * block).astype(F32)
        spread_s[LANES * block : LANES * (block + 1), :] = jnp.where(place_at == unit, 1.0, 0.0).astype(BF16)

    pl.semaphore_wait(barrier, len(peers))
    relay_copies = []
    for slot in (2, 3):
        copy = remote(send.at[3 - slot], relay.at[slot - 2], relay_ss.at[slot - 2], relay_rs.at[slot - 2], relay_to[slot])
        copy.start()
        relay_copies.append(copy)
    direct = remote(send.at[2], recv.at[1], halo_ss.at[1], halo_rs.at[1], beside(lat, lon, 0, -1))
    direct.start()

    def gather(step, carry):
        start = pl.multiple_of(step * 16, 16)
        lows = low_s[pl.ds(start, 16), :].astype(jnp.int32)
        highs = high_s[pl.ds(start, 16), :]
        totals = [jnp.zeros((16, LANES), F32) for _ in range(HEADS)]
        for row in range(HI):
            chosen = highs == float(row)
            for head in range(HEADS):
                line = jnp.broadcast_to(table_s[32 * head + row : 32 * head + row + 1, :], (16, LANES))
                found = jnp.take_along_axis(line, lows, axis=1, mode="promise_in_bounds")
                totals[head] = jnp.where(chosen, found, totals[head])
        for head in range(HEADS):
            dense_s[pl.ds(pl.multiple_of(head * DENSE + start, 16), 16), :] = totals[head]
        return carry

    lax.fori_loop(0, 5, gather, 0)
    halo_copies = []
    for slot, arrived in zip((2, 3), relay_copies):
        arrived.wait_recv()
        copy = remote(relay.at[slot - 2], recv.at[slot], halo_ss.at[slot], halo_rs.at[slot], relayed_to[slot])
        copy.start()
        halo_copies.append(copy)
    halo_copies.append(direct)
    sends = relay_copies + halo_copies
    lax.fori_loop(5, DENSE // 16, gather, 0)
    for head in range(HEADS):
        base = head * DENSE
        bias_s[head * TOK : head * TOK + TOK, 0:LANES] = dense_s[base : base + TOK, :]
        row = dense_s[base + TOK : base + TOK + 16, :]
        for group in range(8):
            turned = row if group == 0 else pltpu.roll(row, LANES - 16 * group, 1)
            bias_s[head * TOK + 16 * group : head * TOK + 16 * group + 16, LANES:TOK] = turned[:, 0:16]
        bias_s[head * TOK + LANES : head * TOK + TOK, LANES:TOK] = dense_s[base + TOK + 16 : base + TOK + 32, 0:16]

    for copy in halo_copies:
        copy.wait_recv()
    lane36 = lax.broadcasted_iota(jnp.int32, (PART, LANES), 1)
    sub36 = lax.broadcasted_iota(jnp.int32, (PART, LANES), 0)
    for slot in range(4):
        unpack_s[slot] = (send[3] if slot == 0 else recv[slot]).astype(F32)
        for tile in range(3):
            grid_s[slot, 0:PART, tile * LANES : (tile + 1) * LANES] = unpack_s[slot, PART * tile : PART * tile + PART, :]
        toks = grid_s[slot, 0:CELLS, :]
        cots = grid_s[slot, CELLS:PART, :]
        base = PART * slot
        x_s[base : base + CELLS, :] = toks[:, 0:C]
        x_s[base + CELLS : base + PART, :] = toks[:, C : 2 * C]
        g_s[base : base + CELLS, :] = cots[:, 0:C]
        g_s[base + CELLS : base + PART, :] = cots[:, C : 2 * C]
        kind_row = unpack_s[slot, FLAT : FLAT + 1, :]
        kind_col = jnp.sum(jnp.where(lane36 == sub36, kind_row, 0.0), axis=1, keepdims=True)
        hot_s[base : base + PART, :] = jnp.where(lane36.astype(F32) == kind_col, 1.0, 0.0)

    for fetch in fetches[7:]:
        fetch.wait()
    gain1, gain2 = gain1_ref[...], gain2_ref[...]
    mix_weight, out_weight = mix_ref[...], outw_ref[...]
    up_weight, down_weight = up_ref[...], down_ref[...]
    residual = x_s[...]
    upstream = g_s[...]
    upstream_low = upstream.astype(BF16)
    first, hat1, inv1 = layer_norm(residual, gain1)
    first_in = first.astype(BF16)
    mixed = dot(first_in, mix_weight)
    queries = mixed[:, 0:C].astype(BF16).astype(F32)
    keys = mixed[:, C : 2 * C].astype(BF16)
    values = mixed[:, 2 * C : 3 * C].astype(BF16)
    channel = lax.broadcasted_iota(jnp.int32, (TOK, C), 1)
    of_head = [(channel >= HEAD * n) & (channel < HEAD * n + HEAD) for n in range(HEADS)]
    q_stack = jnp.concatenate([jnp.where(m, queries, 0.0) for m in of_head], axis=0).astype(BF16)
    scores = dot_nt(q_stack, keys) * (HEAD**-0.5) + bias_s[...]
    last = lat == LAT - 1
    group_q = ((lax.broadcasted_iota(jnp.int32, (HEADS * TOK, TOK), 0) // 72) % 2).astype(F32)
    group_k = (lax.broadcasted_iota(jnp.int32, (HEADS * TOK, TOK), 1) >= 72).astype(F32)
    allowed = jnp.abs(group_q - group_k) * jnp.where(last, 1.0, 0.0) < 0.5
    expon = jnp.where(allowed, jnp.exp(scores), 0.0)
    attend = expon * (1.0 / jnp.sum(expon, axis=-1, keepdims=True))
    attend_low = attend.astype(BF16)
    context = jnp.zeros((TOK, C), F32)
    for n in range(HEADS):
        context += jnp.where(of_head[n], dot(attend_low[n * TOK : (n + 1) * TOK], values), 0.0)
    context = context.astype(BF16)
    mid = residual + dot(context, out_weight)
    second, hat2, inv2 = layer_norm(mid, gain2)
    second_in = second.astype(BF16)
    inner = dot(second_in, up_weight)
    tangent = jnp.tanh(GELU_SQRT * (inner + GELU_CUBE * inner * inner * inner))
    hidden_low = (0.5 * inner * (1.0 + tangent)).astype(BF16)
    slope = 0.5 * (1.0 + tangent) + 0.5 * inner * (1.0 - tangent * tangent) * GELU_SQRT * (
        1.0 + 3.0 * GELU_CUBE * inner * inner
    )
    hidden_grad = (dot(upstream_low, down_weight) * slope).astype(BF16)
    second_grad = dot_nt(hidden_grad, up_weight)
    mid_grad = upstream + norm_backward(second_grad, hat2, inv2, gain2)
    mid_low = mid_grad.astype(BF16)
    context_grad = dot_nt(mid_low, out_weight).astype(BF16).astype(F32)
    c_stack = jnp.concatenate([jnp.where(m, context_grad, 0.0) for m in of_head], axis=0).astype(BF16)
    attend_grad = dot_nt(c_stack, values)
    value_grad = dot_tn(attend_low, c_stack).astype(BF16)
    score_grad = attend * (attend_grad - jnp.sum(attend * attend_grad, axis=-1, keepdims=True))
    score_s[...] = score_grad
    score_low = score_grad.astype(BF16)
    query_grad = jnp.zeros((TOK, C), F32)
    for n in range(HEADS):
        query_grad += jnp.where(of_head[n], dot(score_low[n * TOK : (n + 1) * TOK], keys), 0.0)
    query_grad = (query_grad * (HEAD**-0.5)).astype(BF16)
    key_grad = (dot_tn(score_low, q_stack) * (HEAD**-0.5)).astype(BF16)
    first_grad = (
        dot_nt(query_grad, mix_weight[:, 0:C])
        + dot_nt(key_grad, mix_weight[:, C : 2 * C])
        + dot_nt(value_grad, mix_weight[:, 2 * C : 3 * C])
    )
    moved = mid_grad + norm_backward(first_grad, hat1, inv1, gain1)

    moved_s[...] = moved
    for slot in range(4):
        base = PART * slot
        grid_s[slot, 0:CELLS, 0:C] = moved_s[base : base + CELLS, :]
        grid_s[slot, 0:CELLS, C : 2 * C] = moved_s[base + CELLS : base + PART, :]
        for tile in range(3):
            unpack_s[slot, CELLS * tile : CELLS * tile + CELLS, :] = grid_s[
                slot, 0:CELLS, tile * LANES : (tile + 1) * LANES
            ]
        back_s[slot] = unpack_s[slot, 0:64, :].astype(BF16)

    back_copies = []
    for slot in (3, 2, 1):
        copy = remote(
            back_s.at[slot], back_r.at[3 - slot], back_ss.at[slot], back_rs.at[slot], beside(lat, lon, slot // 2, slot % 2)
        )
        copy.start()
        back_copies.append((slot, copy))
    sends += [copy for _, copy in back_copies]

    lane = lax.broadcasted_iota(jnp.int32, (TOK, LANES), 1)
    small = jnp.zeros((C, LANES), F32)
    for left, right in (
        (moved, hot_s[...]),
        (first_grad * hat1, jnp.where(lane == KINDS, 1.0, 0.0)),
        (second_grad * hat2, jnp.where(lane == KINDS + 1, 1.0, 0.0)),
    ):
        for term in two_terms(left):
            small += dot_tn(term, right.astype(BF16))
    ge_s[...] = small
    extra = jnp.zeros((32, LANES), F32)
    for k in range(6):
        line = ge_s[pl.ds(k, 32, stride=6), :]
        extra += pltpu.roll(line, 18 * k, 1) if k else line
    extra_s[...] = extra

    grad_s[:, 0:C] = dot_tn(first_in, query_grad)
    grad_s[:, C : 2 * C] = dot_tn(first_in, key_grad)
    grad_s[:, 2 * C : 3 * C] = dot_tn(first_in, value_grad)
    grad_s[:, 3 * C : 4 * C] = dot_tn(context, mid_low)
    grad_s[:, 4 * C : 8 * C] = dot_tn(second_in, hidden_grad)
    spread = dot(hidden_low, spread_s[...]).astype(BF16)
    for part in range(4):
        grad_s[:, (8 + part) * C : (9 + part) * C] = dot_tn(spread[:, part * C : (part + 1) * C], upstream_low)
    for tile in range(TILES):
        for part in range(4):
            rows_s[tile // 9, part, pl.ds(tile % 9, 48, stride=9), :] = grad_s[
                48 * part : 48 * part + 48, tile * LANES : (tile + 1) * LANES
            ]
    sub64 = lax.broadcasted_iota(jnp.int32, (64, LANES), 0)

    def blocks(half, part):
        for block in range(ZLO):
            got = rows_s[half, part, 54 * block : 54 * block + 64, :]
            line = extra_s[pl.ds(part * ZLO + block, 1), :] * jnp.where(half == 0, 1.0, 0.0)
            got = jnp.where(sub64 < 54, got, jnp.where(sub64 == 54, line, 0.0)).astype(BF16)
            for quarter in range(4):
                grads[half, part, quarter, block] = got[16 * quarter : 16 * quarter + 16]

    core_copies = []
    for j in range(4):
        to = (y + 1 + j) & 3
        blocks(other, to)
        copy = remote(grads.at[other, to], core_r.at[to], core_ss.at[j], core_rs.at[j], at(x, y, z, other))
        copy.start()
        core_copies.append(copy)
    sends += core_copies
    plane_copies = {}
    for j in range(4):
        to_y = (y + 1 + j) & 3
        blocks(core, to_y)
        core_copies[j].wait_recv()
        for part in range(4):
            plane_s[to_y, part] = (grads[core, to_y, part].astype(F32) + core_r[to_y, part].astype(F32)).astype(BF16)
        for i in range(4):
            dx, dy = (i + 1) % 4, (j + 1) % 4
            d = dx * 4 + dy
            to_x = (x + dx) & 3
            if d == 0:
                plane_r[x * 4 + y] = plane_s[y, x]
                continue
            copy = remote(
                plane_s.at[to_y, to_x], plane_r.at[x * 4 + y], plane_ss.at[d], plane_rs.at[d], at(to_x, to_y, z, core)
            )
            copy.start()
            plane_copies[d] = copy
    sends += list(plane_copies.values())

    acc_s[...] = jnp.zeros((208, LANES), F32)
    for n in range(HEADS):
        dense_rows(dense_s, score_s[n * TOK : (n + 1) * TOK, :], n * DENSE)
    row32 = lax.broadcasted_iota(jnp.int32, (32, LANES), 0).astype(F32)
    row128 = lax.broadcasted_iota(jnp.int32, (LANES, LANES), 0).astype(F32)

    def scatter(step, carry):
        left, right = [], []
        start = pl.multiple_of(step * 16, 16)
        highs, lows = high_s[pl.ds(start, 16), :], low_s[pl.ds(start, 16), :]
        scores = [dense_s[pl.ds(pl.multiple_of(n * DENSE + start, 16), 16), :] for n in range(HEADS)]
        for row in range(16):
            chosen = row32 == highs[row : row + 1]
            right.append(jnp.where(row128 == lows[row : row + 1], 1.0, 0.0).astype(BF16))
            taken = [jnp.where(chosen, scores[n][row : row + 1], 0.0).astype(BF16) for n in range(HEADS)]
            left.append(jnp.concatenate(taken, axis=0))
        acc_s[0 : 32 * HEADS, :] += dot_nt(jnp.concatenate(left, axis=1), jnp.concatenate(right, axis=1))
        return carry

    lax.fori_loop(0, DENSE // 16, scatter, 0)
    sub16 = lax.broadcasted_iota(jnp.int32, (16, LANES), 0)
    for block in range(16):
        parts_s[block // 8, block % 8] = jnp.where(sub16 < 12, acc_s[12 * block : 12 * block + 16, :], 0.0)

    bcore = remote(parts_s.at[other], bcore_r, bcore_ss, bcore_rs, at(x, y, z, other))
    bcore.start()
    sends.append(bcore)
    bcore.wait_recv()
    for part in range(ZLO):
        bline_s[part] = (parts_s[core, part] + bcore_r[part]).astype(BF16)
    bline_r[z_lo] = bline_s[z_lo]
    bline_copies = []
    for d in range(1, ZLO):
        to = (z_lo + d) & 7
        copy = remote(
            bline_s.at[to], bline_r.at[z_lo], bline_ss.at[d], bline_rs.at[d], at(x, y, z_hi * ZLO + to, core)
        )
        copy.start()
        bline_copies.append(copy)
    sends += bline_copies

    for copy in plane_copies.values():
        copy.wait_recv()
    for part in range(ZLO):
        block = plane_r[0, part].astype(F32)
        for source in range(1, 16):
            block = block + plane_r[source, part].astype(F32)
        line_s[part] = block.astype(BF16)
    line_r[z] = line_s[z_lo]
    line_copies = []
    for d in range(1, 16):
        to = (z + d) & 15
        copy = remote(line_s.at[to & 7], line_r.at[z], line_ss.at[d], line_rs.at[d], at(x, y, to, core))
        copy.start()
        line_copies.append(copy)
    sends += line_copies

    for copy in bline_copies:
        copy.wait_recv()
    part_sum = bline_r[0].astype(F32)
    for part in range(1, ZLO):
        part_sum = part_sum + bline_r[part].astype(F32)
    brow_r[y] = part_sum
    brow_copies = []
    for d in range(1, 4):
        to = (y + d) & 3
        copy = remote(brow_r.at[y], brow_r.at[y], brow_ss.at[d], brow_rs.at[d], at(x, to, z, core))
        copy.start()
        brow_copies.append(copy)
    sends += brow_copies

    for copy in brow_copies:
        copy.wait_recv()
    bias_part = (brow_r[0] + brow_r[1]) + (brow_r[2] + brow_r[3])
    ball[core, z_lo] = bias_part
    ball_copies = []
    for d in range(1, ZLO):
        to = (z_lo + d) & 7
        copy = remote(
            ball.at[core, z_lo], ball.at[core, z_lo], ball_ss.at[d], ball_rs.at[d], at(x, y, z_hi * ZLO + to, core)
        )
        copy.start()
        ball_copies.append(copy)
    sends += ball_copies

    for copy in line_copies:
        copy.wait_recv()
    piece = line_r[0].astype(F32)
    for source in range(1, 16):
        piece = piece + line_r[source].astype(F32)
    square = 0.5 * jnp.sum(piece * piece) + 0.25 * jnp.sum(bias_part * bias_part)
    mine = core * 4 + x
    share[mine, 0:16, :] = piece
    share[mine, 16:24, :] = jnp.full((8, LANES), square, F32)
    share_copies = []
    for dx, dcore in ((1, 0), (2, 0), (3, 0), (0, 1), (1, 1), (2, 1), (3, 1)):
        d = dcore * 4 + dx
        copy = remote(
            share.at[mine],
            share.at[mine],
            share_ss.at[d],
            share_rs.at[d],
            at((x + dx) & 3, y, z, core + dcore * (1 - 2 * core)),
        )
        copy.start()
        share_copies.append(copy)
    sends += share_copies

    for copy in share_copies:
        copy.wait_recv()
    square = share[0, 16:17, :]
    for source in range(1, 8):
        square = square + share[source, 16:17, :]
    squares_z[z] = square
    sz_copies = []
    for d in range(1, 16):
        to = (z + d) & 15
        copy = remote(squares_z.at[z], squares_z.at[z], sz_ss.at[d], sz_rs.at[d], at(x, y, to, core))
        copy.start()
        sz_copies.append(copy)
    sends += sz_copies
    for copy in ball_copies:
        copy.wait_recv()
    bpair = remote(ball.at[core], ball.at[core], bpair_ss, bpair_rs, at(x, y, z, other))
    bpair.start()
    sends.append(bpair)
    for source in range(8):
        dense_out[source] = share[source, 0:16, :]
    back_out[3] = back_s[0]
    for slot, copy in back_copies:
        copy.wait_recv()
        back_out[3 - slot] = back_r[3 - slot]
    for copy in sz_copies:
        copy.wait_recv()
    square = squares_z[0]
    for source in range(1, 16):
        square = square + squares_z[source]
    squares_y[y] = square
    sy_copies = []
    for d in range(1, 4):
        copy = remote(squares_y.at[y], squares_y.at[y], sy_ss.at[d], sy_rs.at[d], at(x, (y + d) & 3, z, core))
        copy.start()
        sy_copies.append(copy)
    sends += sy_copies
    bpair.wait_recv()
    bias_out[...] = ball[...]
    for copy in sy_copies:
        copy.wait_recv()
    total_out[...] = (squares_y[0] + squares_y[1]) + (squares_y[2] + squares_y[3])
    for copy in sends:
        copy.wait_send()


def main(*operands):
    token = np.arange(TOK)
    slot, level, cell = token // PART, (token % PART) // CELLS, token % CELLS
    row, col = 3 * (slot // 2) + cell // 6, 6 * (slot % 2) + cell % 6
    order = np.zeros((TOK, TOK), np.float32)
    order[token, (row * WIN_LON + col) * 2 + level] = 1.0
    operands = operands[:6] + (jnp.asarray(order, BF16),) + operands[6:]
    vmem = pl.BlockSpec(memory_space=pltpu.VMEM)
    dma = pltpu.SemaphoreType.DMA
    return pl.pallas_call(
        main_kernel,
        out_shape=(
            jax.ShapeDtypeStruct((8, 16, LANES), F32),
            jax.ShapeDtypeStruct((2, ZLO, 16, LANES), F32),
            jax.ShapeDtypeStruct((4, 64, LANES), BF16),
            jax.ShapeDtypeStruct((1, LANES), F32),
        ),
        in_specs=[pl.BlockSpec(memory_space=pl.ANY)] * 13,
        out_specs=(vmem,) * 4,
        scratch_shapes=[pltpu.VMEM(v.shape, v.dtype) for v in operands] + [
            pltpu.VMEM((4, 24, 2 * C), F32),
            pltpu.VMEM((4, 8, LANES), F32),
            pltpu.VMEM((4, 40, 2 * C), F32),
            pltpu.VMEM((4, SENT, LANES), F32),
            pltpu.VMEM((4, SENT, LANES), BF16),
            pltpu.VMEM((4, SENT, LANES), BF16),
            pltpu.VMEM((HEADS * 32, LANES), F32),
            pltpu.VMEM((HEADS * DENSE, LANES), F32),
            pltpu.VMEM((DENSE, LANES), F32),
            pltpu.VMEM((DENSE, LANES), F32),
            pltpu.VMEM((HEADS * TOK, TOK), F32),
            pltpu.VMEM((FF, FF), BF16),
            pltpu.VMEM((4, 40, 2 * C), F32),
            pltpu.VMEM((TOK, C), F32),
            pltpu.VMEM((TOK, C), F32),
            pltpu.VMEM((TOK, LANES), F32),
            pltpu.VMEM((C, LANES), F32),
            pltpu.VMEM((TOK, C), F32),
            pltpu.VMEM((4, SENT, LANES), F32),
            pltpu.VMEM((HEADS * TOK, TOK), F32),
            pltpu.VMEM((32, LANES), F32),
            pltpu.VMEM((4, 64, LANES), BF16),
            pltpu.VMEM((C, COLS), F32),
            pltpu.VMEM((2, 4, 448, LANES), F32),
            pltpu.VMEM((2, 4, 4, ZLO, 16, LANES), BF16),
            pltpu.VMEM((208, LANES), F32),
            pltpu.VMEM((2, ZLO, 16, LANES), F32),
            pltpu.VMEM((4, 4, ZLO, 16, LANES), BF16),
            pltpu.VMEM((4, 4, ZLO, 16, LANES), BF16),
            pltpu.VMEM((16, ZLO, 16, LANES), BF16),
            pltpu.VMEM((ZLO, 16, LANES), BF16),
            pltpu.VMEM((16, 16, LANES), BF16),
            pltpu.VMEM((8, 24, LANES), F32),
            pltpu.VMEM((ZLO, 16, LANES), F32),
            pltpu.VMEM((ZLO, 16, LANES), BF16),
            pltpu.VMEM((ZLO, 16, LANES), BF16),
            pltpu.VMEM((4, 16, LANES), F32),
            pltpu.VMEM((2, ZLO, 16, LANES), F32),
            pltpu.VMEM((4, 64, LANES), BF16),
            pltpu.VMEM((16, 1, LANES), F32),
            pltpu.VMEM((4, 1, LANES), F32),
            pltpu.VMEM((2, SENT, LANES), BF16),
            dma((13,)), dma((2,)), dma((2,)),
            dma((4,)), dma((4,)),
            dma((4,)), dma((4,)),
            dma((16,)), dma((16,)),
            dma((16,)), dma((16,)),
            dma((8,)), dma((8,)),
            dma, dma,
            dma((8,)), dma((8,)),
            dma((4,)), dma((4,)),
            dma((8,)), dma((8,)),
            dma, dma,
            dma((4,)), dma((4,)),
            dma((16,)), dma((16,)),
            dma((4,)), dma((4,)),
        ],
        compiler_params=pltpu.CompilerParams(collective_id=0, has_side_effects=True, vmem_limit_bytes=VMEM_LIMIT),
        name="window_and_sums",
    )(*operands)


def output_kernel(
    dense_ref, bias_ref, back_ref, total_ref,
    token_ref, mix_ref, out_ref, up_ref, down_ref, gain_ref, embed_ref, table_ref,
    dense_s, flat_s, bias_s, back_s, token_s,
):
    count = C * COLS + (KINDS + 2) * C + LAT * HEADS * PAIRS
    factor = lax.rsqrt(total_ref[...] / count + RMS_EPS)
    odd = lax.axis_index("lon") % 2 == 1
    for part in range(8):
        dense_s[part // 4, 16 * (part % 4) : 16 * (part % 4) + 16, :] = dense_ref[part] * factor
    for tile in range(TILES):
        half, t = tile // 9, tile % 9
        even_rows = dense_s[half, pl.ds(t, 3, stride=9), :]
        odd_rows = dense_s[half, pl.ds(27 + t, 3, stride=9), :]
        flat_s[0:3, tile * LANES : (tile + 1) * LANES] = jnp.where(odd, odd_rows, even_rows)
    flat = flat_s[0:3, :]
    mix_ref[...] = flat[:, 0 : 3 * C]
    out_ref[...] = flat[:, 3 * C : 4 * C]
    up_ref[...] = flat[:, 4 * C : 8 * C]
    for row in range(3):
        for part in range(4):
            down_ref[4 * row + part : 4 * row + part + 1, :] = flat[row : row + 1, (8 + part) * C : (9 + part) * C]
    extra = dense_s[0, 54:55, :]
    lane = lax.broadcasted_iota(jnp.int32, (24, LANES), 1)
    sub = lax.broadcasted_iota(jnp.int32, (24, LANES), 0)
    small = jnp.zeros((24, LANES), F32)
    wide = jnp.zeros((8, LANES), F32)
    sub8 = lax.broadcasted_iota(jnp.int32, (8, LANES), 0)
    line8 = jnp.broadcast_to(extra, (8, LANES))
    for row in range(3):
        turned = jnp.where(odd, pltpu.roll(line8, LANES - 18 * (3 + row), 1), pltpu.roll(line8, (LANES - 18 * row) % LANES, 1))
        wide = jnp.where(sub8 == row, turned, wide)
        start = jnp.where(odd, 18 * (3 + row), 18 * row)
        column = jnp.sum(jnp.where(lane == sub + start, extra, 0.0), axis=1, keepdims=True)
        small = small + jnp.where(lane == row, column, 0.0)
    embed_ref[...] = wide[0:3, 0:KINDS]
    gain_ref[...] = small[KINDS : KINDS + 2, 0:3]
    for block in range(16):
        bias_s[12 * block : 12 * block + 12, :] = bias_ref[block // 8, block % 8, 0:12, :] * factor
    for row in range(HI):
        width = min(LANES, PAIRS - row * LANES)
        line = bias_s[pl.ds(row, HEADS, stride=32), :][:, 0:width]
        for head in range(HEADS):
            table_ref[head, :, row * LANES : row * LANES + width] = line[head : head + 1]
    for quarter in range(4):
        packed = back_ref[quarter].astype(F32)
        for tile in range(3):
            back_s[quarter, 0:CELLS, tile * LANES : (tile + 1) * LANES] = packed[CELLS * tile : CELLS * tile + CELLS]
        for i in range(3):
            row, half = 3 * (quarter // 2) + i, quarter % 2
            token_s[row, 6 * half : 6 * half + 6, :] = back_s[quarter, 6 * i : 6 * i + 6, :]
    for row in range(WIN_LAT):
        token_ref[row] = token_s[row, 0:WIN_LON, :].astype(BF16)


def outputs(dense, bias, back, total):
    vmem = pl.BlockSpec(memory_space=pltpu.VMEM)
    return pl.pallas_call(
        output_kernel,
        out_shape=(
            jax.ShapeDtypeStruct((WIN_LAT, WIN_LON, 2 * C), BF16),
            jax.ShapeDtypeStruct((3, 3 * C), F32),
            jax.ShapeDtypeStruct((3, C), F32),
            jax.ShapeDtypeStruct((3, FF), F32),
            jax.ShapeDtypeStruct((12, C), F32),
            jax.ShapeDtypeStruct((2, 3), F32),
            jax.ShapeDtypeStruct((3, KINDS), F32),
            jax.ShapeDtypeStruct((HEADS, 1, PAIRS), F32),
        ),
        in_specs=[vmem] * 4,
        out_specs=(vmem,) * 8,
        scratch_shapes=[
            pltpu.VMEM((2, 64, LANES), F32),
            pltpu.VMEM((8, COLS), F32),
            pltpu.VMEM((HEADS * 32, LANES), F32),
            pltpu.VMEM((4, 32, 2 * C), F32),
            pltpu.VMEM((WIN_LAT, 16, 2 * C), F32),
        ],
        compiler_params=pltpu.CompilerParams(vmem_limit_bytes=VMEM_LIMIT),
        name="scaled_outputs",
    )(dense, bias, back, total)


def shards(
    tokens, kinds, kind_embed, pair_index, bias_table, attn_gain, mlp_gain,
    mix_weight, out_weight, up_weight, down_weight, cotangent,
):
    sums = main(
        tokens, kinds.transpose(0, 2, 1), kind_embed, cotangent, pair_index, bias_table.transpose(1, 0, 2),
        attn_gain.reshape(1, C), mlp_gain.reshape(1, C), mix_weight, out_weight, up_weight, down_weight.T,
    )
    token, mix, out, up, down, gain, embed, table = outputs(*sums)
    return token, mix, out, up, down, gain, embed.T, table.transpose(1, 0, 2)


def solution(mesh):
    return jax.shard_map(
        shards,
        mesh=mesh,
        in_specs=(
            P("lat", "lon", None),
            P("lat", "lon", None),
            P(),
            P(),
            P("lat", None, None),
            P(),
            P(),
            P(),
            P(),
            P(),
            P(),
            P("lat", "lon", None),
        ),
        out_specs=(
            P("lat", "lon", None),
            P("lon", None),
            P("lon", None),
            P("lon", None),
            P("lon", None),
            P(None, "lon"),
            P(None, "lon"),
            P("lat", None, None),
        ),
        check_vma=False,
    )
```

```python
import jax
import jax.numpy as jnp
import numpy as np
from jax import lax
from jax.experimental import pallas as pl
from jax.experimental.pallas import tpu as pltpu
from jax.sharding import PartitionSpec as P

F32 = jnp.float32
BF16 = jnp.bfloat16
MESH = pl.DeviceIdType.MESH

C = 192
HEADS = 6
HEAD = 32
FF = 768
WIN_LAT = 6
WIN_LON = 12
KINDS = 16
PAIRS = 3312
TOK = 144
CELLS = 18
PART = 36
LANES = 128
HI = 26
COLS = 2304
TILES = 18
NORM_EPS = 1e-05
RMS_EPS = 1e-06
GELU_SQRT = 0.7978845608028654
GELU_CUBE = 0.044715
LON, LAT = 64, 8
ZLO = 8
VMEM_LIMIT = 56 * 1024 * 1024


def coords(lat, lon):
    return lat >> 1, lon >> 4, ((lat & 1) << 3) + ((lon >> 1) & 7), lon & 1


def at(x, y, z, core):
    return {"lon": (y << 4) + ((z & 7) << 1) + core, "lat": (x << 1) + (z >> 3)}


def beside(lat, lon, rows, columns):
    return {"lon": (lon + columns) & (LON - 1), "lat": (lat + rows) & (LAT - 1)}


def dot(a, b):
    return lax.dot_general(a, b, (((1,), (0,)), ((), ())), preferred_element_type=F32)


def dot_nt(a, b):
    return lax.dot_general(a, b, (((1,), (1,)), ((), ())), preferred_element_type=F32)


def dot_tn(a, b):
    return lax.dot_general(a, b, (((0,), (0,)), ((), ())), preferred_element_type=F32)


def two_terms(v):
    high = v.astype(BF16)
    return high, (v - high.astype(F32)).astype(BF16)


def dense_rows(ref, values, base):
    ref[base : base + TOK, :] = values[:, 0:LANES]
    tail = values[:, LANES:TOK]
    tail = jnp.concatenate([tail, jnp.zeros((TOK, LANES - 16), tail.dtype)], axis=1)
    row = tail[0:16]
    for group in range(1, 8):
        row = row + pltpu.roll(tail[16 * group : 16 * group + 16], 16 * group, 1)
    ref[base + TOK : base + TOK + 16, :] = row
    ref[base + TOK + 16 : base + TOK + 32, :] = tail[LANES:TOK]


DENSE = TOK + 32
FLAT = 3 * PART
SENT = FLAT + 4


def layer_norm(values, gain):
    centred = values - jnp.mean(values, axis=-1, keepdims=True)
    inverse = lax.rsqrt(jnp.mean(centred * centred, axis=-1, keepdims=True) + NORM_EPS)
    normed = centred * inverse
    return normed * gain, normed, inverse


def norm_backward(upstream, normed, inverse, gain):
    scaled = upstream * gain
    return inverse * (
        scaled
        - jnp.mean(scaled, axis=-1, keepdims=True)
        - normed * jnp.mean(scaled * normed, axis=-1, keepdims=True)
    )


def main_kernel(
    tok_in, kind_in, embed_in, cot_in, index_in, table_in, order_in,
    gain1_in, gain2_in, mix_in, outw_in, up_in, down_in,
    dense_out, bias_out, back_out, total_out,
    tok_ref, kind_ref, embed_ref, cot_ref, index_ref, table_ref, order_ref,
    gain1_ref, gain2_ref, mix_ref, outw_ref, up_ref, down_ref,
    tok_s, kind_s, flat_s, pack_s, send, recv, table_s, dense_s, high_s, low_s, bias_s, spread_s,
    grid_s, x_s, g_s, hot_s, ge_s, moved_s, unpack_s, score_s, extra_s, back_s,
    grad_s, rows_s, grads, acc_s, parts_s,
    core_r, plane_s, plane_r, line_s, line_r, share, bcore_r, bline_s, bline_r, brow_r, ball, back_r, squares_z, squares_y,
    in_sems, halo_ss, halo_rs,
    core_ss, core_rs, plane_ss, plane_rs, line_ss, line_rs, share_ss, share_rs, bcore_ss, bcore_rs, bline_ss, bline_rs,
    brow_ss, brow_rs, ball_ss, ball_rs, bpair_ss, bpair_rs, back_ss, back_rs, sz_ss, sz_rs, sy_ss, sy_rs,
):
    lon, lat = lax.axis_index("lon"), lax.axis_index("lat")
    x, y, z, core = coords(lat, lon)
    z_lo, z_hi = z & 7, z >> 3
    other = 1 - core

    def remote(src, dst, send_sem, recv_sem, target):
        return pltpu.make_async_remote_copy(
            src_ref=src, dst_ref=dst, send_sem=send_sem, recv_sem=recv_sem, device_id=target, device_id_type=MESH
        )

    sources = (
        tok_in, kind_in, embed_in, cot_in, index_in, table_in, order_in,
        gain1_in, gain2_in, mix_in, outw_in, up_in, down_in,
    )
    targets = (
        tok_ref, kind_ref, embed_ref, cot_ref, index_ref, table_ref, order_ref,
        gain1_ref, gain2_ref, mix_ref, outw_ref, up_ref, down_ref,
    )
    fetches = [pltpu.make_async_copy(s, t, in_sems.at[i]) for i, (s, t) in enumerate(zip(sources, targets))]
    for fetch in fetches[:4]:
        fetch.start()

    barrier = pltpu.get_barrier_semaphore()
    peers = []
    for dr, dc in ((1, 0), (0, 1), (1, 1)):
        peers += [beside(lat, lon, -dr, -dc), beside(lat, lon, dr, dc)]
    peers += [at(x, y, (z + d) & 15, core) for d in range(1, 16)]
    peers += [at((x + d // 4) & 3, (y + d % 4) & 3, z, core) for d in range(1, 16)]
    peers += [at((x + d // 4) & 3, (y + d % 4) & 3, z, other) for d in range(16)]
    for peer in peers:
        pl.semaphore_signal(barrier, inc=1, device_id=peer, device_id_type=MESH)

    for fetch in fetches[4:]:
        fetch.start()
    for fetch in fetches[:4]:
        fetch.wait()
    embed = embed_ref[...].astype(F32)
    blank = jnp.zeros((KINDS, C), F32)
    wide = jnp.concatenate(
        [jnp.concatenate([embed, blank], axis=1), jnp.concatenate([blank, embed], axis=1)], axis=0
    ).astype(BF16)
    kind_s[...] = jnp.zeros((4, 8, LANES), F32)
    for row in range(WIN_LAT):
        tok = tok_ref[row].astype(F32)
        cot = cot_ref[row].astype(F32)
        kind = kind_ref[row].astype(F32)
        for half in range(2):
            quarter = 2 * (row // 3) + half
            start = 6 * (row % 3)
            cells = slice(6 * half, 6 * half + 6)
            tok_s[quarter, start : start + 6, :] = tok[cells]
            flat_s[quarter, CELLS + start : CELLS + start + 6, :] = cot[cells]
            kind_s[quarter, 0:2, start : start + 6] = kind[:, cells]
    sub = lax.broadcasted_iota(jnp.int32, (2 * KINDS, LANES), 0).astype(F32)
    for quarter in range(4):
        kinds = kind_s[quarter]
        hot = (sub == kinds[0:1]) | (sub - KINDS == kinds[1:2])
        hot = jnp.where(hot, 1.0, 0.0).astype(BF16)[:, 0:24]
        stored = tok_s[quarter] + dot_tn(hot, wide)
        flat_s[quarter, 0:CELLS, :] = stored[0:CELLS]
        for tile in range(3):
            pack_s[quarter, PART * tile : PART * tile + PART, :] = flat_s[
                quarter, 0:PART, tile * LANES : (tile + 1) * LANES
            ]
        pack_s[quarter, FLAT:SENT, :] = jnp.zeros((4, LANES), F32)
        pack_s[quarter, FLAT : FLAT + 1, :] = kinds[0:1] + pltpu.roll(kinds, CELLS, 1)[1:2]
        send[quarter] = pack_s[quarter].astype(BF16)
    pl.semaphore_wait(barrier, len(peers))
    halo_copies = []
    for slot in (3, 2, 1):
        copy = remote(
            send.at[3 - slot], recv.at[slot], halo_ss.at[slot], halo_rs.at[slot], beside(lat, lon, -(slot // 2), -(slot % 2))
        )
        copy.start()
        halo_copies.append(copy)
    sends = list(halo_copies)

    for fetch in fetches[4:7]:
        fetch.wait()
    order = order_ref[...]
    index = index_ref[...]
    high = (index // LANES).astype(F32).astype(BF16)
    low = (index % LANES).astype(F32).astype(BF16)
    dense_rows(high_s, dot_nt(dot(order, high).astype(BF16), order), 0)
    dense_rows(low_s, dot_nt(dot(order, low).astype(BF16), order), 0)
    table_s[...] = jnp.zeros((HEADS * 32, LANES), F32)
    for row in range(HI):
        width = min(LANES, PAIRS - row * LANES)
        for head in range(HEADS):
            table_s[32 * head + row : 32 * head + row + 1, 0:width] = table_ref[
                head, :, row * LANES : row * LANES + width
            ]

    column = lax.broadcasted_iota(jnp.int32, (1, FF), 1)
    part = jnp.where(column >= C, 1, 0) + jnp.where(column >= 2 * C, 1, 0) + jnp.where(column >= 3 * C, 1, 0)
    unit = (4 * (column - C * part) + part).astype(F32)
    for block in range(6):
        place_at = (lax.broadcasted_iota(jnp.int32, (LANES, FF), 0) + LANES * block).astype(F32)
        spread_s[LANES * block : LANES * (block + 1), :] = jnp.where(place_at == unit, 1.0, 0.0).astype(BF16)

    def gather(step, carry):
        start = pl.multiple_of(step * 16, 16)
        lows = low_s[pl.ds(start, 16), :].astype(jnp.int32)
        highs = high_s[pl.ds(start, 16), :]
        totals = [jnp.zeros((16, LANES), F32) for _ in range(HEADS)]
        for row in range(HI):
            chosen = highs == float(row)
            for head in range(HEADS):
                line = jnp.broadcast_to(table_s[32 * head + row : 32 * head + row + 1, :], (16, LANES))
                found = jnp.take_along_axis(line, lows, axis=1, mode="promise_in_bounds")
                totals[head] = jnp.where(chosen, found, totals[head])
        for head in range(HEADS):
            dense_s[pl.ds(pl.multiple_of(head * DENSE + start, 16), 16), :] = totals[head]
        return carry

    lax.fori_loop(0, DENSE // 16, gather, 0)
    for head in range(HEADS):
        base = head * DENSE
        bias_s[head * TOK : head * TOK + TOK, 0:LANES] = dense_s[base : base + TOK, :]
        row = dense_s[base + TOK : base + TOK + 16, :]
        for group in range(8):
            turned = row if group == 0 else pltpu.roll(row, LANES - 16 * group, 1)
            bias_s[head * TOK + 16 * group : head * TOK + 16 * group + 16, LANES:TOK] = turned[:, 0:16]
        bias_s[head * TOK + LANES : head * TOK + TOK, LANES:TOK] = dense_s[base + TOK + 16 : base + TOK + 32, 0:16]

    for copy in halo_copies:
        copy.wait_recv()
    lane36 = lax.broadcasted_iota(jnp.int32, (PART, LANES), 1)
    sub36 = lax.broadcasted_iota(jnp.int32, (PART, LANES), 0)
    for slot in range(4):
        unpack_s[slot] = (send[3] if slot == 0 else recv[slot]).astype(F32)
        for tile in range(3):
            grid_s[slot, 0:PART, tile * LANES : (tile + 1) * LANES] = unpack_s[slot, PART * tile : PART * tile + PART, :]
        toks = grid_s[slot, 0:CELLS, :]
        cots = grid_s[slot, CELLS:PART, :]
        base = PART * slot
        x_s[base : base + CELLS, :] = toks[:, 0:C]
        x_s[base + CELLS : base + PART, :] = toks[:, C : 2 * C]
        g_s[base : base + CELLS, :] = cots[:, 0:C]
        g_s[base + CELLS : base + PART, :] = cots[:, C : 2 * C]
        kind_row = unpack_s[slot, FLAT : FLAT + 1, :]
        kind_col = jnp.sum(jnp.where(lane36 == sub36, kind_row, 0.0), axis=1, keepdims=True)
        hot_s[base : base + PART, :] = jnp.where(lane36.astype(F32) == kind_col, 1.0, 0.0)

    for fetch in fetches[7:]:
        fetch.wait()
    gain1, gain2 = gain1_ref[...], gain2_ref[...]
    mix_weight, out_weight = mix_ref[...], outw_ref[...]
    up_weight, down_weight = up_ref[...], down_ref[...]
    residual = x_s[...]
    upstream = g_s[...]
    upstream_low = upstream.astype(BF16)
    first, hat1, inv1 = layer_norm(residual, gain1)
    first_in = first.astype(BF16)
    mixed = dot(first_in, mix_weight)
    queries = mixed[:, 0:C].astype(BF16).astype(F32)
    keys = mixed[:, C : 2 * C].astype(BF16)
    values = mixed[:, 2 * C : 3 * C].astype(BF16)
    channel = lax.broadcasted_iota(jnp.int32, (TOK, C), 1)
    of_head = [(channel >= HEAD * n) & (channel < HEAD * n + HEAD) for n in range(HEADS)]
    q_stack = jnp.concatenate([jnp.where(m, queries, 0.0) for m in of_head], axis=0).astype(BF16)
    scores = dot_nt(q_stack, keys) * (HEAD**-0.5) + bias_s[...]
    last = lat == LAT - 1
    group_q = ((lax.broadcasted_iota(jnp.int32, (HEADS * TOK, TOK), 0) // 72) % 2).astype(F32)
    group_k = (lax.broadcasted_iota(jnp.int32, (HEADS * TOK, TOK), 1) >= 72).astype(F32)
    allowed = jnp.abs(group_q - group_k) * jnp.where(last, 1.0, 0.0) < 0.5
    expon = jnp.where(allowed, jnp.exp(scores), 0.0)
    attend = expon * (1.0 / jnp.sum(expon, axis=-1, keepdims=True))
    attend_low = attend.astype(BF16)
    context = jnp.zeros((TOK, C), F32)
    for n in range(HEADS):
        context += jnp.where(of_head[n], dot(attend_low[n * TOK : (n + 1) * TOK], values), 0.0)
    context = context.astype(BF16)
    mid = residual + dot(context, out_weight)
    second, hat2, inv2 = layer_norm(mid, gain2)
    second_in = second.astype(BF16)
    inner = dot(second_in, up_weight)
    tangent = jnp.tanh(GELU_SQRT * (inner + GELU_CUBE * inner * inner * inner))
    hidden_low = (0.5 * inner * (1.0 + tangent)).astype(BF16)
    slope = 0.5 * (1.0 + tangent) + 0.5 * inner * (1.0 - tangent * tangent) * GELU_SQRT * (
        1.0 + 3.0 * GELU_CUBE * inner * inner
    )
    hidden_grad = (dot(upstream_low, down_weight) * slope).astype(BF16)
    second_grad = dot_nt(hidden_grad, up_weight)
    mid_grad = upstream + norm_backward(second_grad, hat2, inv2, gain2)
    mid_low = mid_grad.astype(BF16)
    context_grad = dot_nt(mid_low, out_weight).astype(BF16).astype(F32)
    c_stack = jnp.concatenate([jnp.where(m, context_grad, 0.0) for m in of_head], axis=0).astype(BF16)
    attend_grad = dot_nt(c_stack, values)
    value_grad = dot_tn(attend_low, c_stack).astype(BF16)
    score_grad = attend * (attend_grad - jnp.sum(attend * attend_grad, axis=-1, keepdims=True))
    score_s[...] = score_grad
    score_low = score_grad.astype(BF16)
    query_grad = jnp.zeros((TOK, C), F32)
    for n in range(HEADS):
        query_grad += jnp.where(of_head[n], dot(score_low[n * TOK : (n + 1) * TOK], keys), 0.0)
    query_grad = (query_grad * (HEAD**-0.5)).astype(BF16)
    key_grad = (dot_tn(score_low, q_stack) * (HEAD**-0.5)).astype(BF16)
    first_grad = (
        dot_nt(query_grad, mix_weight[:, 0:C])
        + dot_nt(key_grad, mix_weight[:, C : 2 * C])
        + dot_nt(value_grad, mix_weight[:, 2 * C : 3 * C])
    )
    moved = mid_grad + norm_backward(first_grad, hat1, inv1, gain1)

    lane = lax.broadcasted_iota(jnp.int32, (TOK, LANES), 1)
    small = jnp.zeros((C, LANES), F32)
    for left, right in (
        (moved, hot_s[...]),
        (first_grad * hat1, jnp.where(lane == KINDS, 1.0, 0.0)),
        (second_grad * hat2, jnp.where(lane == KINDS + 1, 1.0, 0.0)),
    ):
        for term in two_terms(left):
            small += dot_tn(term, right.astype(BF16))
    ge_s[...] = small
    extra = jnp.zeros((32, LANES), F32)
    for k in range(6):
        line = ge_s[pl.ds(k, 32, stride=6), :]
        extra += pltpu.roll(line, 18 * k, 1) if k else line
    extra_s[...] = extra

    grad_s[:, 0:C] = dot_tn(first_in, query_grad)
    grad_s[:, C : 2 * C] = dot_tn(first_in, key_grad)
    grad_s[:, 2 * C : 3 * C] = dot_tn(first_in, value_grad)
    grad_s[:, 3 * C : 4 * C] = dot_tn(context, mid_low)
    grad_s[:, 4 * C : 8 * C] = dot_tn(second_in, hidden_grad)
    spread = dot(hidden_low, spread_s[...]).astype(BF16)
    for part in range(4):
        grad_s[:, (8 + part) * C : (9 + part) * C] = dot_tn(spread[:, part * C : (part + 1) * C], upstream_low)
    for tile in range(TILES):
        for part in range(4):
            rows_s[tile // 9, part, pl.ds(tile % 9, 48, stride=9), :] = grad_s[
                48 * part : 48 * part + 48, tile * LANES : (tile + 1) * LANES
            ]
    sub64 = lax.broadcasted_iota(jnp.int32, (64, LANES), 0)

    def blocks(half, part):
        for block in range(ZLO):
            got = rows_s[half, part, 54 * block : 54 * block + 64, :]
            line = extra_s[pl.ds(part * ZLO + block, 1), :] * jnp.where(half == 0, 1.0, 0.0)
            got = jnp.where(sub64 < 54, got, jnp.where(sub64 == 54, line, 0.0)).astype(BF16)
            for quarter in range(4):
                grads[half, part, quarter, block] = got[16 * quarter : 16 * quarter + 16]

    core_copies = []
    for j in range(4):
        to = (y + 1 + j) & 3
        blocks(other, to)
        copy = remote(grads.at[other, to], core_r.at[to], core_ss.at[j], core_rs.at[j], at(x, y, z, other))
        copy.start()
        core_copies.append(copy)
    sends += core_copies
    moved_s[...] = moved
    for slot in range(4):
        base = PART * slot
        grid_s[slot, 0:CELLS, 0:C] = moved_s[base : base + CELLS, :]
        grid_s[slot, 0:CELLS, C : 2 * C] = moved_s[base + CELLS : base + PART, :]
        for tile in range(3):
            unpack_s[slot, CELLS * tile : CELLS * tile + CELLS, :] = grid_s[
                slot, 0:CELLS, tile * LANES : (tile + 1) * LANES
            ]
        back_s[slot] = unpack_s[slot, 0:64, :].astype(BF16)

    back_copies = []
    for slot in (3, 2, 1):
        copy = remote(
            back_s.at[slot], back_r.at[3 - slot], back_ss.at[slot], back_rs.at[slot], beside(lat, lon, slot // 2, slot % 2)
        )
        copy.start()
        back_copies.append((slot, copy))
    sends += [copy for _, copy in back_copies]

    plane_copies = {}
    for j in range(4):
        to_y = (y + 1 + j) & 3
        blocks(core, to_y)
        core_copies[j].wait_recv()
        for part in range(4):
            plane_s[to_y, part] = (grads[core, to_y, part].astype(F32) + core_r[to_y, part].astype(F32)).astype(BF16)
        for i in range(4):
            dx, dy = (i + 1) % 4, (j + 1) % 4
            d = dx * 4 + dy
            to_x = (x + dx) & 3
            if d == 0:
                plane_r[x * 4 + y] = plane_s[y, x]
                continue
            copy = remote(
                plane_s.at[to_y, to_x], plane_r.at[x * 4 + y], plane_ss.at[d], plane_rs.at[d], at(to_x, to_y, z, core)
            )
            copy.start()
            plane_copies[d] = copy
    sends += list(plane_copies.values())

    acc_s[...] = jnp.zeros((208, LANES), F32)
    for n in range(HEADS):
        dense_rows(dense_s, score_s[n * TOK : (n + 1) * TOK, :], n * DENSE)
    row32 = lax.broadcasted_iota(jnp.int32, (32, LANES), 0).astype(F32).astype(BF16)
    row128 = lax.broadcasted_iota(jnp.int32, (LANES, LANES), 0).astype(F32).astype(BF16)
    zero, one = jnp.zeros((), BF16), jnp.ones((), BF16)

    def low_rows(line, count):
        return jnp.concatenate([jnp.broadcast_to(line, (16, LANES)).astype(BF16)] * (count // 16), axis=0)

    def scatter(step, carry):
        left, right = [], []
        start = pl.multiple_of(step * 16, 16)
        highs, lows = high_s[pl.ds(start, 16), :], low_s[pl.ds(start, 16), :]
        scores = [dense_s[pl.ds(pl.multiple_of(n * DENSE + start, 16), 16), :] for n in range(HEADS)]
        for row in range(16):
            chosen = row32 == low_rows(highs[row : row + 1], 32)
            right.append(jnp.where(row128 == low_rows(lows[row : row + 1], LANES), one, zero))
            left.append(
                jnp.concatenate([jnp.where(chosen, low_rows(scores[n][row : row + 1], 32), zero) for n in range(HEADS)], axis=0)
            )
        acc_s[0 : 32 * HEADS, :] += dot_nt(jnp.concatenate(left, axis=1), jnp.concatenate(right, axis=1))
        return carry

    lax.fori_loop(0, DENSE // 16, scatter, 0)
    sub16 = lax.broadcasted_iota(jnp.int32, (16, LANES), 0)
    for block in range(16):
        parts_s[block // 8, block % 8] = jnp.where(sub16 < 12, acc_s[12 * block : 12 * block + 16, :], 0.0)

    bcore = remote(parts_s.at[other], bcore_r, bcore_ss, bcore_rs, at(x, y, z, other))
    bcore.start()
    sends.append(bcore)
    bcore.wait_recv()
    for part in range(ZLO):
        bline_s[part] = (parts_s[core, part] + bcore_r[part]).astype(BF16)
    bline_r[z_lo] = bline_s[z_lo]
    bline_copies = []
    for d in range(1, ZLO):
        to = (z_lo + d) & 7
        copy = remote(
            bline_s.at[to], bline_r.at[z_lo], bline_ss.at[d], bline_rs.at[d], at(x, y, z_hi * ZLO + to, core)
        )
        copy.start()
        bline_copies.append(copy)
    sends += bline_copies

    for copy in plane_copies.values():
        copy.wait_recv()
    for part in range(ZLO):
        block = plane_r[0, part].astype(F32)
        for source in range(1, 16):
            block = block + plane_r[source, part].astype(F32)
        line_s[part] = block.astype(BF16)
    line_r[z] = line_s[z_lo]
    line_copies = []
    for d in range(1, 16):
        to = (z + d) & 15
        copy = remote(line_s.at[to & 7], line_r.at[z], line_ss.at[d], line_rs.at[d], at(x, y, to, core))
        copy.start()
        line_copies.append(copy)
    sends += line_copies

    for copy in bline_copies:
        copy.wait_recv()
    part_sum = bline_r[0].astype(F32)
    for part in range(1, ZLO):
        part_sum = part_sum + bline_r[part].astype(F32)
    brow_r[y] = part_sum
    brow_copies = []
    for d in range(1, 4):
        to = (y + d) & 3
        copy = remote(brow_r.at[y], brow_r.at[y], brow_ss.at[d], brow_rs.at[d], at(x, to, z, core))
        copy.start()
        brow_copies.append(copy)
    sends += brow_copies

    for copy in brow_copies:
        copy.wait_recv()
    bias_part = (brow_r[0] + brow_r[1]) + (brow_r[2] + brow_r[3])
    for copy in line_copies:
        copy.wait_recv()
    piece = line_r[0].astype(F32)
    for source in range(1, 16):
        piece = piece + line_r[source].astype(F32)
    square = 0.5 * jnp.sum(piece * piece) + 0.25 * jnp.sum(bias_part * bias_part)
    squares_z[z] = jnp.full((1, LANES), square, F32)
    sz_copies = []
    for d in range(1, 16):
        to = (z + d) & 15
        copy = remote(squares_z.at[z], squares_z.at[z], sz_ss.at[d], sz_rs.at[d], at(x, y, to, core))
        copy.start()
        sz_copies.append(copy)
    sends += sz_copies
    mine = core * 4 + x
    share[mine] = piece
    share_copies = []
    for dx, dcore in ((1, 0), (2, 0), (3, 0), (0, 1), (1, 1), (2, 1), (3, 1)):
        d = dcore * 4 + dx
        copy = remote(
            share.at[mine],
            share.at[mine],
            share_ss.at[d],
            share_rs.at[d],
            at((x + dx) & 3, y, z, core + dcore * (1 - 2 * core)),
        )
        copy.start()
        share_copies.append(copy)
    sends += share_copies
    ball[core, z_lo] = bias_part
    ball_copies = []
    for d in range(1, ZLO):
        to = (z_lo + d) & 7
        copy = remote(
            ball.at[core, z_lo], ball.at[core, z_lo], ball_ss.at[d], ball_rs.at[d], at(x, y, z_hi * ZLO + to, core)
        )
        copy.start()
        ball_copies.append(copy)
    sends += ball_copies

    for copy in sz_copies:
        copy.wait_recv()
    square = squares_z[0]
    for source in range(1, 16):
        square = square + squares_z[source]
    spot = core * 16 + x * 4 + y
    squares_y[spot] = square
    sy_copies = []
    for d in range(1, 32):
        target = at((x + (d >> 2 & 3)) & 3, (y + (d & 3)) & 3, z, core + (d >> 4) * (1 - 2 * core))
        copy = remote(squares_y.at[spot], squares_y.at[spot], sy_ss.at[d], sy_rs.at[d], target)
        copy.start()
        sy_copies.append(copy)
    sends += sy_copies
    for copy in ball_copies:
        copy.wait_recv()
    bpair = remote(ball.at[core], ball.at[core], bpair_ss, bpair_rs, at(x, y, z, other))
    bpair.start()
    sends.append(bpair)
    for copy in share_copies:
        copy.wait_recv()
    dense_out[...] = share[...]
    back_out[3] = back_s[0]
    for slot, copy in back_copies:
        copy.wait_recv()
        back_out[3 - slot] = back_r[3 - slot]
    for copy in sy_copies:
        copy.wait_recv()
    square = squares_y[0]
    for source in range(1, 32):
        square = square + squares_y[source]
    total_out[...] = square
    bpair.wait_recv()
    bias_out[...] = ball[...]
    for copy in sends:
        copy.wait_send()


def main(*operands):
    token = np.arange(TOK)
    slot, level, cell = token // PART, (token % PART) // CELLS, token % CELLS
    row, col = 3 * (slot // 2) + cell // 6, 6 * (slot % 2) + cell % 6
    order = np.zeros((TOK, TOK), np.float32)
    order[token, (row * WIN_LON + col) * 2 + level] = 1.0
    operands = operands[:6] + (jnp.asarray(order, BF16),) + operands[6:]
    vmem = pl.BlockSpec(memory_space=pltpu.VMEM)
    dma = pltpu.SemaphoreType.DMA
    return pl.pallas_call(
        main_kernel,
        out_shape=(
            jax.ShapeDtypeStruct((8, 16, LANES), F32),
            jax.ShapeDtypeStruct((2, ZLO, 16, LANES), F32),
            jax.ShapeDtypeStruct((4, 64, LANES), BF16),
            jax.ShapeDtypeStruct((1, LANES), F32),
        ),
        in_specs=[pl.BlockSpec(memory_space=pl.ANY)] * 13,
        out_specs=(vmem,) * 4,
        scratch_shapes=[pltpu.VMEM(v.shape, v.dtype) for v in operands] + [
            pltpu.VMEM((4, 24, 2 * C), F32),
            pltpu.VMEM((4, 8, LANES), F32),
            pltpu.VMEM((4, 40, 2 * C), F32),
            pltpu.VMEM((4, SENT, LANES), F32),
            pltpu.VMEM((4, SENT, LANES), BF16),
            pltpu.VMEM((4, SENT, LANES), BF16),
            pltpu.VMEM((HEADS * 32, LANES), F32),
            pltpu.VMEM((HEADS * DENSE, LANES), F32),
            pltpu.VMEM((DENSE, LANES), F32),
            pltpu.VMEM((DENSE, LANES), F32),
            pltpu.VMEM((HEADS * TOK, TOK), F32),
            pltpu.VMEM((FF, FF), BF16),
            pltpu.VMEM((4, 40, 2 * C), F32),
            pltpu.VMEM((TOK, C), F32),
            pltpu.VMEM((TOK, C), F32),
            pltpu.VMEM((TOK, LANES), F32),
            pltpu.VMEM((C, LANES), F32),
            pltpu.VMEM((TOK, C), F32),
            pltpu.VMEM((4, SENT, LANES), F32),
            pltpu.VMEM((HEADS * TOK, TOK), F32),
            pltpu.VMEM((32, LANES), F32),
            pltpu.VMEM((4, 64, LANES), BF16),
            pltpu.VMEM((C, COLS), F32),
            pltpu.VMEM((2, 4, 448, LANES), F32),
            pltpu.VMEM((2, 4, 4, ZLO, 16, LANES), BF16),
            pltpu.VMEM((208, LANES), F32),
            pltpu.VMEM((2, ZLO, 16, LANES), F32),
            pltpu.VMEM((4, 4, ZLO, 16, LANES), BF16),
            pltpu.VMEM((4, 4, ZLO, 16, LANES), BF16),
            pltpu.VMEM((16, ZLO, 16, LANES), BF16),
            pltpu.VMEM((ZLO, 16, LANES), BF16),
            pltpu.VMEM((16, 16, LANES), BF16),
            pltpu.VMEM((8, 16, LANES), F32),
            pltpu.VMEM((ZLO, 16, LANES), F32),
            pltpu.VMEM((ZLO, 16, LANES), BF16),
            pltpu.VMEM((ZLO, 16, LANES), BF16),
            pltpu.VMEM((4, 16, LANES), F32),
            pltpu.VMEM((2, ZLO, 16, LANES), F32),
            pltpu.VMEM((4, 64, LANES), BF16),
            pltpu.VMEM((16, 1, LANES), F32),
            pltpu.VMEM((32, 1, LANES), F32),
            dma((13,)),
            dma((4,)), dma((4,)),
            dma((4,)), dma((4,)),
            dma((16,)), dma((16,)),
            dma((16,)), dma((16,)),
            dma((8,)), dma((8,)),
            dma, dma,
            dma((8,)), dma((8,)),
            dma((4,)), dma((4,)),
            dma((8,)), dma((8,)),
            dma, dma,
            dma((4,)), dma((4,)),
            dma((16,)), dma((16,)),
            dma((32,)), dma((32,)),
        ],
        compiler_params=pltpu.CompilerParams(collective_id=0, has_side_effects=True, vmem_limit_bytes=VMEM_LIMIT),
        name="window_and_sums",
    )(*operands)


def output_kernel(
    dense_ref, bias_ref, back_ref, total_ref,
    token_ref, mix_ref, out_ref, up_ref, down_ref, gain_ref, embed_ref, table_ref,
    dense_s, flat_s, bias_s, back_s, token_s,
):
    count = C * COLS + (KINDS + 2) * C + LAT * HEADS * PAIRS
    factor = lax.rsqrt(total_ref[...] / count + RMS_EPS)
    odd = lax.axis_index("lon") % 2 == 1
    for part in range(8):
        dense_s[part // 4, 16 * (part % 4) : 16 * (part % 4) + 16, :] = dense_ref[part] * factor
    for tile in range(TILES):
        half, t = tile // 9, tile % 9
        even_rows = dense_s[half, pl.ds(t, 3, stride=9), :]
        odd_rows = dense_s[half, pl.ds(27 + t, 3, stride=9), :]
        flat_s[0:3, tile * LANES : (tile + 1) * LANES] = jnp.where(odd, odd_rows, even_rows)
    flat = flat_s[0:3, :]
    mix_ref[...] = flat[:, 0 : 3 * C]
    out_ref[...] = flat[:, 3 * C : 4 * C]
    up_ref[...] = flat[:, 4 * C : 8 * C]
    for row in range(3):
        for part in range(4):
            down_ref[4 * row + part : 4 * row + part + 1, :] = flat[row : row + 1, (8 + part) * C : (9 + part) * C]
    extra = dense_s[0, 54:55, :]
    lane = lax.broadcasted_iota(jnp.int32, (24, LANES), 1)
    sub = lax.broadcasted_iota(jnp.int32, (24, LANES), 0)
    small = jnp.zeros((24, LANES), F32)
    wide = jnp.zeros((8, LANES), F32)
    sub8 = lax.broadcasted_iota(jnp.int32, (8, LANES), 0)
    line8 = jnp.broadcast_to(extra, (8, LANES))
    for row in range(3):
        turned = jnp.where(odd, pltpu.roll(line8, LANES - 18 * (3 + row), 1), pltpu.roll(line8, (LANES - 18 * row) % LANES, 1))
        wide = jnp.where(sub8 == row, turned, wide)
        start = jnp.where(odd, 18 * (3 + row), 18 * row)
        column = jnp.sum(jnp.where(lane == sub + start, extra, 0.0), axis=1, keepdims=True)
        small = small + jnp.where(lane == row, column, 0.0)
    embed_ref[...] = wide[0:3, 0:KINDS]
    gain_ref[...] = small[KINDS : KINDS + 2, 0:3]
    for block in range(16):
        bias_s[12 * block : 12 * block + 12, :] = bias_ref[block // 8, block % 8, 0:12, :] * factor
    for row in range(HI):
        width = min(LANES, PAIRS - row * LANES)
        line = bias_s[pl.ds(row, HEADS, stride=32), :][:, 0:width]
        for head in range(HEADS):
            table_ref[head, :, row * LANES : row * LANES + width] = line[head : head + 1]
    for quarter in range(4):
        packed = back_ref[quarter].astype(F32)
        for tile in range(3):
            back_s[quarter, 0:CELLS, tile * LANES : (tile + 1) * LANES] = packed[CELLS * tile : CELLS * tile + CELLS]
        for i in range(3):
            row, half = 3 * (quarter // 2) + i, quarter % 2
            token_s[row, 6 * half : 6 * half + 6, :] = back_s[quarter, 6 * i : 6 * i + 6, :]
    for row in range(WIN_LAT):
        token_ref[row] = token_s[row, 0:WIN_LON, :].astype(BF16)


def outputs(dense, bias, back, total):
    vmem = pl.BlockSpec(memory_space=pltpu.VMEM)
    return pl.pallas_call(
        output_kernel,
        out_shape=(
            jax.ShapeDtypeStruct((WIN_LAT, WIN_LON, 2 * C), BF16),
            jax.ShapeDtypeStruct((3, 3 * C), F32),
            jax.ShapeDtypeStruct((3, C), F32),
            jax.ShapeDtypeStruct((3, FF), F32),
            jax.ShapeDtypeStruct((12, C), F32),
            jax.ShapeDtypeStruct((2, 3), F32),
            jax.ShapeDtypeStruct((3, KINDS), F32),
            jax.ShapeDtypeStruct((HEADS, 1, PAIRS), F32),
        ),
        in_specs=[vmem] * 4,
        out_specs=(vmem,) * 8,
        scratch_shapes=[
            pltpu.VMEM((2, 64, LANES), F32),
            pltpu.VMEM((8, COLS), F32),
            pltpu.VMEM((HEADS * 32, LANES), F32),
            pltpu.VMEM((4, 32, 2 * C), F32),
            pltpu.VMEM((WIN_LAT, 16, 2 * C), F32),
        ],
        compiler_params=pltpu.CompilerParams(vmem_limit_bytes=VMEM_LIMIT),
        name="scaled_outputs",
    )(dense, bias, back, total)


def shards(
    tokens, kinds, kind_embed, pair_index, bias_table, attn_gain, mlp_gain,
    mix_weight, out_weight, up_weight, down_weight, cotangent,
):
    sums = main(
        tokens, kinds.transpose(0, 2, 1), kind_embed, cotangent, pair_index, bias_table.transpose(1, 0, 2),
        attn_gain.reshape(1, C), mlp_gain.reshape(1, C), mix_weight, out_weight, up_weight, down_weight.T,
    )
    token, mix, out, up, down, gain, embed, table = outputs(*sums)
    return token, mix, out, up, down, gain, embed.T, table.transpose(1, 0, 2)


def solution(mesh):
    return jax.shard_map(
        shards,
        mesh=mesh,
        in_specs=(
            P("lat", "lon", None),
            P("lat", "lon", None),
            P(),
            P(),
            P("lat", None, None),
            P(),
            P(),
            P(),
            P(),
            P(),
            P(),
            P("lat", "lon", None),
        ),
        out_specs=(
            P("lat", "lon", None),
            P("lon", None),
            P("lon", None),
            P("lon", None),
            P("lon", None),
            P(None, "lon"),
            P(None, "lon"),
            P("lat", None, None),
        ),
        check_vma=False,
    )
```

```python
import jax
import jax.numpy as jnp
import numpy as np
from jax import lax
from jax.experimental import pallas as pl
from jax.experimental.pallas import tpu as pltpu
from jax.sharding import PartitionSpec as P

F32 = jnp.float32
BF16 = jnp.bfloat16
MESH = pl.DeviceIdType.MESH

C = 192
HEADS = 6
HEAD = 32
FF = 768
WIN_LAT = 6
WIN_LON = 12
KINDS = 16
PAIRS = 3312
TOK = 144
CELLS = 18
PART = 36
LANES = 128
HI = 26
COLS = 2304
TILES = 18
NORM_EPS = 1e-05
RMS_EPS = 1e-06
GELU_SQRT = 0.7978845608028654
GELU_CUBE = 0.044715
LON, LAT = 64, 8
ZLO = 8
VMEM_LIMIT = 56 * 1024 * 1024


def coords(lat, lon):
    return lat >> 1, lon >> 4, ((lat & 1) << 3) + ((lon >> 1) & 7), lon & 1


def at(x, y, z, core):
    return {"lon": (y << 4) + ((z & 7) << 1) + core, "lat": (x << 1) + (z >> 3)}


def beside(lat, lon, rows, columns):
    return {"lon": (lon + columns) & (LON - 1), "lat": (lat + rows) & (LAT - 1)}


def dot(a, b):
    return lax.dot_general(a, b, (((1,), (0,)), ((), ())), preferred_element_type=F32)


def dot_nt(a, b):
    return lax.dot_general(a, b, (((1,), (1,)), ((), ())), preferred_element_type=F32)


def dot_tn(a, b):
    return lax.dot_general(a, b, (((0,), (0,)), ((), ())), preferred_element_type=F32)


def two_terms(v):
    high = v.astype(BF16)
    return high, (v - high.astype(F32)).astype(BF16)


def dense_rows(ref, values, base):
    ref[base : base + TOK, :] = values[:, 0:LANES]
    tail = values[:, LANES:TOK]
    tail = jnp.concatenate([tail, jnp.zeros((TOK, LANES - 16), tail.dtype)], axis=1)
    row = tail[0:16]
    for group in range(1, 8):
        row = row + pltpu.roll(tail[16 * group : 16 * group + 16], 16 * group, 1)
    ref[base + TOK : base + TOK + 16, :] = row
    ref[base + TOK + 16 : base + TOK + 32, :] = tail[LANES:TOK]


DENSE = TOK + 32
FLAT = 3 * CELLS
SENT = 64


def layer_norm(values, gain):
    centred = values - jnp.mean(values, axis=-1, keepdims=True)
    inverse = lax.rsqrt(jnp.mean(centred * centred, axis=-1, keepdims=True) + NORM_EPS)
    normed = centred * inverse
    return normed * gain, normed, inverse


def norm_backward(upstream, normed, inverse, gain):
    scaled = upstream * gain
    return inverse * (
        scaled
        - jnp.mean(scaled, axis=-1, keepdims=True)
        - normed * jnp.mean(scaled * normed, axis=-1, keepdims=True)
    )


def main_kernel(
    tok_in, kind_in, embed_in, cot_in, index_in, table_in, order_in,
    gain1_in, gain2_in, mix_in, outw_in, up_in, down_in,
    dense_out, bias_out, back_out, total_out,
    tok_ref, kind_ref, embed_ref, cot_ref, index_ref, table_ref, order_ref,
    gain1_ref, gain2_ref, mix_ref, outw_ref, up_ref, down_ref,
    tok_s, kind_s, flat_s, pack_s, cots_s, send, recv, send_g, recv_g, table_s, dense_s, high_s, low_s, bias_s, spread_s,
    grid_s, x_s, g_s, hot_s, ge_s, moved_s, unpack_s, score_s, extra_s, back_s,
    grad_s, wide_s, rows_s, grads, acc_s, parts_s,
    core_r, plane_s, plane_r, line_s, line_r, share, bcore_r, bline_s, bline_r, brow_r, ball, back_r, squares_z, squares_y,
    in_sems, halo_ss, halo_rs,
    core_ss, core_rs, plane_ss, plane_rs, line_ss, line_rs, share_ss, share_rs, bcore_ss, bcore_rs, bline_ss, bline_rs,
    brow_ss, brow_rs, ball_ss, ball_rs, bpair_ss, bpair_rs, back_ss, back_rs, sz_ss, sz_rs, sy_ss, sy_rs,
):
    lon, lat = lax.axis_index("lon"), lax.axis_index("lat")
    x, y, z, core = coords(lat, lon)
    z_lo, z_hi = z & 7, z >> 3
    other = 1 - core

    def remote(src, dst, send_sem, recv_sem, target):
        return pltpu.make_async_remote_copy(
            src_ref=src, dst_ref=dst, send_sem=send_sem, recv_sem=recv_sem, device_id=target, device_id_type=MESH
        )

    sources = (
        tok_in, kind_in, embed_in, cot_in, index_in, table_in, order_in,
        gain1_in, gain2_in, mix_in, outw_in, up_in, down_in,
    )
    targets = (
        tok_ref, kind_ref, embed_ref, cot_ref, index_ref, table_ref, order_ref,
        gain1_ref, gain2_ref, mix_ref, outw_ref, up_ref, down_ref,
    )
    fetches = [pltpu.make_async_copy(s, t, in_sems.at[i]) for i, (s, t) in enumerate(zip(sources, targets))]
    for fetch in fetches[:4]:
        fetch.start()

    barrier = pltpu.get_barrier_semaphore()
    peers = []
    for dr, dc in ((1, 0), (0, 1), (1, 1)):
        peers += [beside(lat, lon, -dr, -dc), beside(lat, lon, dr, dc)]
    peers += [at(x, y, (z + d) & 15, core) for d in range(1, 16)]
    peers += [at((x + d // 4) & 3, (y + d % 4) & 3, z, core) for d in range(1, 16)]
    peers += [at((x + d // 4) & 3, (y + d % 4) & 3, z, other) for d in range(16)]
    for peer in peers:
        pl.semaphore_signal(barrier, inc=1, device_id=peer, device_id_type=MESH)

    for fetch in fetches[4:]:
        fetch.start()
    for fetch in fetches[:4]:
        fetch.wait()
    embed = embed_ref[...].astype(F32)
    blank = jnp.zeros((KINDS, C), F32)
    wide = jnp.concatenate(
        [jnp.concatenate([embed, blank], axis=1), jnp.concatenate([blank, embed], axis=1)], axis=0
    ).astype(BF16)
    kind_s[...] = jnp.zeros((4, 8, LANES), F32)
    for row in range(WIN_LAT):
        tok = tok_ref[row].astype(F32)
        cot = cot_ref[row].astype(F32)
        kind = kind_ref[row].astype(F32)
        for half in range(2):
            quarter = 2 * (row // 3) + half
            start = 6 * (row % 3)
            cells = slice(6 * half, 6 * half + 6)
            tok_s[quarter, start : start + 6, :] = tok[cells]
            flat_s[quarter, start : start + 6, :] = cot[cells]
            kind_s[quarter, 0:2, start : start + 6] = kind[:, cells]
    sub = lax.broadcasted_iota(jnp.int32, (2 * KINDS, LANES), 0).astype(F32)
    for quarter in range(4):
        kinds = kind_s[quarter]
        hot = (sub == kinds[0:1]) | (sub - KINDS == kinds[1:2])
        hot = jnp.where(hot, 1.0, 0.0).astype(BF16)[:, 0:24]
        stored = tok_s[quarter] + dot_tn(hot, wide)
        tok_s[quarter, 0:CELLS, :] = stored[0:CELLS]
        pack_s[quarter, FLAT:SENT, :] = jnp.zeros((SENT - FLAT, LANES), F32)
        cots_s[quarter, FLAT:SENT, :] = jnp.zeros((SENT - FLAT, LANES), F32)
        for tile in range(3):
            rows, lanes = slice(CELLS * tile, CELLS * tile + CELLS), slice(tile * LANES, (tile + 1) * LANES)
            pack_s[quarter, rows, :] = tok_s[quarter, 0:CELLS, lanes]
            cots_s[quarter, rows, :] = flat_s[quarter, 0:CELLS, lanes]
        pack_s[quarter, FLAT : FLAT + 1, :] = kinds[0:1] + pltpu.roll(kinds, CELLS, 1)[1:2]
        send[quarter] = pack_s[quarter].astype(BF16)
        send_g[quarter] = cots_s[quarter].astype(BF16)
    pl.semaphore_wait(barrier, len(peers))
    halo_copies, cot_copies = [], []
    for copies, src, dst, base in ((halo_copies, send, recv, 0), (cot_copies, send_g, recv_g, 4)):
        for slot in (3, 2, 1):
            copy = remote(
                src.at[3 - slot],
                dst.at[slot],
                halo_ss.at[base + slot],
                halo_rs.at[base + slot],
                beside(lat, lon, -(slot // 2), -(slot % 2)),
            )
            copy.start()
            copies.append(copy)
    sends = halo_copies + cot_copies

    for fetch in fetches[4:7]:
        fetch.wait()
    order = order_ref[...]
    index = index_ref[...]
    high = (index // LANES).astype(F32).astype(BF16)
    low = (index % LANES).astype(F32).astype(BF16)
    dense_rows(high_s, dot_nt(dot(order, high).astype(BF16), order), 0)
    dense_rows(low_s, dot_nt(dot(order, low).astype(BF16), order), 0)
    table_s[...] = jnp.zeros((HEADS * 32, LANES), F32)
    for row in range(HI):
        width = min(LANES, PAIRS - row * LANES)
        for head in range(HEADS):
            table_s[32 * head + row : 32 * head + row + 1, 0:width] = table_ref[
                head, :, row * LANES : row * LANES + width
            ]

    column = lax.broadcasted_iota(jnp.int32, (1, FF), 1)
    part = jnp.where(column >= C, 1, 0) + jnp.where(column >= 2 * C, 1, 0) + jnp.where(column >= 3 * C, 1, 0)
    unit = (4 * (column - C * part) + part).astype(F32)
    for block in range(6):
        place_at = (lax.broadcasted_iota(jnp.int32, (LANES, FF), 0) + LANES * block).astype(F32)
        spread_s[LANES * block : LANES * (block + 1), :] = jnp.where(place_at == unit, 1.0, 0.0).astype(BF16)

    def gather(step, carry):
        start = pl.multiple_of(step * 16, 16)
        lows = low_s[pl.ds(start, 16), :].astype(jnp.int32)
        highs = high_s[pl.ds(start, 16), :]
        totals = [jnp.zeros((16, LANES), F32) for _ in range(HEADS)]
        for row in range(HI):
            chosen = highs == float(row)
            for head in range(HEADS):
                line = jnp.broadcast_to(table_s[32 * head + row : 32 * head + row + 1, :], (16, LANES))
                found = jnp.take_along_axis(line, lows, axis=1, mode="promise_in_bounds")
                totals[head] = jnp.where(chosen, found, totals[head])
        for head in range(HEADS):
            dense_s[pl.ds(pl.multiple_of(head * DENSE + start, 16), 16), :] = totals[head]
        return carry

    lax.fori_loop(0, DENSE // 16, gather, 0)
    for head in range(HEADS):
        base = head * DENSE
        bias_s[head * TOK : head * TOK + TOK, 0:LANES] = dense_s[base : base + TOK, :]
        row = dense_s[base + TOK : base + TOK + 16, :]
        for group in range(8):
            turned = row if group == 0 else pltpu.roll(row, LANES - 16 * group, 1)
            bias_s[head * TOK + 16 * group : head * TOK + 16 * group + 16, LANES:TOK] = turned[:, 0:16]
        bias_s[head * TOK + LANES : head * TOK + TOK, LANES:TOK] = dense_s[base + TOK + 16 : base + TOK + 32, 0:16]

    for copy in halo_copies:
        copy.wait_recv()
    lane36 = lax.broadcasted_iota(jnp.int32, (PART, LANES), 1)
    sub36 = lax.broadcasted_iota(jnp.int32, (PART, LANES), 0)
    for slot in range(4):
        unpack_s[slot] = (send[3] if slot == 0 else recv[slot]).astype(F32)
        for tile in range(3):
            grid_s[slot, 0:CELLS, tile * LANES : (tile + 1) * LANES] = unpack_s[
                slot, CELLS * tile : CELLS * tile + CELLS, :
            ]
        toks = grid_s[slot, 0:CELLS, :]
        base = PART * slot
        x_s[base : base + CELLS, :] = toks[:, 0:C]
        x_s[base + CELLS : base + PART, :] = toks[:, C : 2 * C]
        kind_row = unpack_s[slot, FLAT : FLAT + 1, :]
        kind_col = jnp.sum(jnp.where(lane36 == sub36, kind_row, 0.0), axis=1, keepdims=True)
        hot_s[base : base + PART, :] = jnp.where(lane36.astype(F32) == kind_col, 1.0, 0.0)

    for fetch in fetches[7:]:
        fetch.wait()
    gain1, gain2 = gain1_ref[...], gain2_ref[...]
    mix_weight, out_weight = mix_ref[...], outw_ref[...]
    up_weight, down_weight = up_ref[...], down_ref[...]
    residual = x_s[...]
    first, hat1, inv1 = layer_norm(residual, gain1)
    first_in = first.astype(BF16)
    mixed = dot(first_in, mix_weight)
    queries = mixed[:, 0:C].astype(BF16).astype(F32)
    keys = mixed[:, C : 2 * C].astype(BF16)
    values = mixed[:, 2 * C : 3 * C].astype(BF16)
    channel = lax.broadcasted_iota(jnp.int32, (TOK, C), 1)
    of_head = [(channel >= HEAD * n) & (channel < HEAD * n + HEAD) for n in range(HEADS)]
    q_stack = jnp.concatenate([jnp.where(m, queries, 0.0) for m in of_head], axis=0).astype(BF16)
    scores = dot_nt(q_stack, keys) * (HEAD**-0.5) + bias_s[...]
    last = lat == LAT - 1
    group_q = ((lax.broadcasted_iota(jnp.int32, (HEADS * TOK, TOK), 0) // 72) % 2).astype(F32)
    group_k = (lax.broadcasted_iota(jnp.int32, (HEADS * TOK, TOK), 1) >= 72).astype(F32)
    allowed = jnp.abs(group_q - group_k) * jnp.where(last, 1.0, 0.0) < 0.5
    expon = jnp.where(allowed, jnp.exp(scores), 0.0)
    attend = expon * (1.0 / jnp.sum(expon, axis=-1, keepdims=True))
    attend_low = attend.astype(BF16)
    context = jnp.zeros((TOK, C), F32)
    for n in range(HEADS):
        context += jnp.where(of_head[n], dot(attend_low[n * TOK : (n + 1) * TOK], values), 0.0)
    context = context.astype(BF16)
    mid = residual + dot(context, out_weight)
    second, hat2, inv2 = layer_norm(mid, gain2)
    second_in = second.astype(BF16)
    inner = dot(second_in, up_weight)
    tangent = jnp.tanh(GELU_SQRT * (inner + GELU_CUBE * inner * inner * inner))
    hidden_low = (0.5 * inner * (1.0 + tangent)).astype(BF16)
    slope = 0.5 * (1.0 + tangent) + 0.5 * inner * (1.0 - tangent * tangent) * GELU_SQRT * (
        1.0 + 3.0 * GELU_CUBE * inner * inner
    )
    for copy in cot_copies:
        copy.wait_recv()
    for slot in range(4):
        cots_s[slot] = (send_g[3] if slot == 0 else recv_g[slot]).astype(F32)
        for tile in range(3):
            flat_s[slot, 0:CELLS, tile * LANES : (tile + 1) * LANES] = cots_s[
                slot, CELLS * tile : CELLS * tile + CELLS, :
            ]
        cots = flat_s[slot, 0:CELLS, :]
        base = PART * slot
        g_s[base : base + CELLS, :] = cots[:, 0:C]
        g_s[base + CELLS : base + PART, :] = cots[:, C : 2 * C]
    upstream = g_s[...]
    upstream_low = upstream.astype(BF16)
    hidden_grad = (dot(upstream_low, down_weight) * slope).astype(BF16)

    grad_s[:, 4 * C : 8 * C] = dot_tn(second_in, hidden_grad)
    spread = dot(hidden_low, spread_s[...]).astype(BF16)
    for part in range(4):
        grad_s[:, (8 + part) * C : (9 + part) * C] = dot_tn(spread[:, part * C : (part + 1) * C], upstream_low)
    for tile in range(12):
        for part in range(4):
            wide_s[tile // 6, part, pl.ds(tile % 6, 48, stride=6), :] = grad_s[
                48 * part : 48 * part + 48, (6 + tile) * LANES : (7 + tile) * LANES
            ]

    def first_blocks(half):
        for part in range(4):
            for block in range(ZLO):
                got = wide_s[half, part, 36 * block : 36 * block + 32, :].astype(BF16)
                grads[half, 0, part, 0, block] = got[0:16]
                grads[half, 0, part, 1, block] = got[16:32]

    first_blocks(other)
    core_copies = [remote(grads.at[other, 0], core_r.at[0], core_ss.at[0], core_rs.at[0], at(x, y, z, other))]
    core_copies[0].start()
    first_blocks(core)

    second_grad = dot_nt(hidden_grad, up_weight)
    mid_grad = upstream + norm_backward(second_grad, hat2, inv2, gain2)
    mid_low = mid_grad.astype(BF16)
    context_grad = dot_nt(mid_low, out_weight).astype(BF16).astype(F32)
    c_stack = jnp.concatenate([jnp.where(m, context_grad, 0.0) for m in of_head], axis=0).astype(BF16)
    attend_grad = dot_nt(c_stack, values)
    value_grad = dot_tn(attend_low, c_stack).astype(BF16)
    score_grad = attend * (attend_grad - jnp.sum(attend * attend_grad, axis=-1, keepdims=True))
    score_s[...] = score_grad
    score_low = score_grad.astype(BF16)
    query_grad = jnp.zeros((TOK, C), F32)
    for n in range(HEADS):
        query_grad += jnp.where(of_head[n], dot(score_low[n * TOK : (n + 1) * TOK], keys), 0.0)
    query_grad = (query_grad * (HEAD**-0.5)).astype(BF16)
    key_grad = (dot_tn(score_low, q_stack) * (HEAD**-0.5)).astype(BF16)
    first_grad = (
        dot_nt(query_grad, mix_weight[:, 0:C])
        + dot_nt(key_grad, mix_weight[:, C : 2 * C])
        + dot_nt(value_grad, mix_weight[:, 2 * C : 3 * C])
    )
    moved = mid_grad + norm_backward(first_grad, hat1, inv1, gain1)

    here = x * 4 + y

    def plane(batch):
        core_copies[batch].wait_recv()
        for part in range(4):
            for i in range(2):
                plane_s[batch, part, i] = (
                    grads[core, batch, part, i].astype(F32) + core_r[batch, part, i].astype(F32)
                ).astype(BF16)
        for dy in (1, 2, 3, 0):
            for i in (1, 0) if dy else (1,):
                to_y, to_i = (y + dy) & 3, (x + i) & 1
                copy = remote(
                    plane_s.at[batch, to_y, to_i],
                    plane_r.at[here],
                    plane_ss.at[batch * 8 + dy * 2 + i],
                    plane_rs.at[here],
                    at(batch * 2 + to_i, to_y, z, core),
                )
                copy.start()
                sends.append(copy)

    plane(0)

    lane = lax.broadcasted_iota(jnp.int32, (TOK, LANES), 1)
    small = jnp.zeros((C, LANES), F32)
    for left, right in (
        (moved, hot_s[...]),
        (first_grad * hat1, jnp.where(lane == KINDS, 1.0, 0.0)),
        (second_grad * hat2, jnp.where(lane == KINDS + 1, 1.0, 0.0)),
    ):
        for term in two_terms(left):
            small += dot_tn(term, right.astype(BF16))
    ge_s[...] = small
    extra = jnp.zeros((32, LANES), F32)
    for k in range(6):
        line = ge_s[pl.ds(k, 32, stride=6), :]
        extra += pltpu.roll(line, 18 * k, 1) if k else line
    extra_s[...] = extra

    grad_s[:, 0:C] = dot_tn(first_in, query_grad)
    grad_s[:, C : 2 * C] = dot_tn(first_in, key_grad)
    grad_s[:, 2 * C : 3 * C] = dot_tn(first_in, value_grad)
    grad_s[:, 3 * C : 4 * C] = dot_tn(context, mid_low)
    for tile in range(6):
        for part in range(4):
            rows_s[tile // 3, part, pl.ds(8 + tile % 3, 48, stride=3), :] = grad_s[
                48 * part : 48 * part + 48, tile * LANES : (tile + 1) * LANES
            ]
    sub16 = lax.broadcasted_iota(jnp.int32, (16, LANES), 0)

    def last_blocks(half):
        for part in range(4):
            for block in range(ZLO):
                wide_rows = wide_s[half, part, 36 * block + 32 : 36 * block + 48, :]
                upper = rows_s[half, part, 18 * block + 4 : 18 * block + 20, :]
                lower = rows_s[half, part, 18 * block + 20 : 18 * block + 36, :]
                line = extra_s[part * ZLO + block : part * ZLO + block + 1, :] * jnp.where(half == 0, 1.0, 0.0)
                grads[half, 1, part, 0, block] = jnp.where(sub16 < 4, wide_rows, upper).astype(BF16)
                lower = jnp.where(sub16 < 6, lower, jnp.where(sub16 == 6, line, 0.0))
                grads[half, 1, part, 1, block] = lower.astype(BF16)

    last_blocks(other)
    core_copies.append(remote(grads.at[other, 1], core_r.at[1], core_ss.at[1], core_rs.at[1], at(x, y, z, other)))
    core_copies[1].start()
    sends += core_copies
    last_blocks(core)
    moved_s[...] = moved
    for slot in range(4):
        base = PART * slot
        grid_s[slot, 0:CELLS, 0:C] = moved_s[base : base + CELLS, :]
        grid_s[slot, 0:CELLS, C : 2 * C] = moved_s[base + CELLS : base + PART, :]
        for tile in range(3):
            unpack_s[slot, CELLS * tile : CELLS * tile + CELLS, :] = grid_s[
                slot, 0:CELLS, tile * LANES : (tile + 1) * LANES
            ]
        back_s[slot] = unpack_s[slot, 0:64, :].astype(BF16)

    back_copies = []
    for slot in (3, 2, 1):
        copy = remote(
            back_s.at[slot], back_r.at[3 - slot], back_ss.at[slot], back_rs.at[slot], beside(lat, lon, slot // 2, slot % 2)
        )
        copy.start()
        back_copies.append((slot, copy))
    sends += [copy for _, copy in back_copies]

    plane(1)
    copy = remote(
        plane_s.at[1 - (x >> 1), y, x & 1], plane_r.at[here], plane_ss.at[0], plane_rs.at[here], at(x ^ 2, y, z, core)
    )
    copy.start()
    sends.append(copy)
    plane_r[here] = plane_s[x >> 1, y, x & 1]

    acc_s[...] = jnp.zeros((208, LANES), F32)
    for n in range(HEADS):
        dense_rows(dense_s, score_s[n * TOK : (n + 1) * TOK, :], n * DENSE)
    row32 = lax.broadcasted_iota(jnp.int32, (32, LANES), 0).astype(F32).astype(BF16)
    row128 = lax.broadcasted_iota(jnp.int32, (LANES, LANES), 0).astype(F32).astype(BF16)
    zero, one = jnp.zeros((), BF16), jnp.ones((), BF16)

    def low_rows(line, count):
        return jnp.concatenate([jnp.broadcast_to(line, (16, LANES)).astype(BF16)] * (count // 16), axis=0)

    def scatter(step, carry):
        left, right = [], []
        start = pl.multiple_of(step * 16, 16)
        highs, lows = high_s[pl.ds(start, 16), :], low_s[pl.ds(start, 16), :]
        scores = [dense_s[pl.ds(pl.multiple_of(n * DENSE + start, 16), 16), :] for n in range(HEADS)]
        for row in range(16):
            chosen = row32 == low_rows(highs[row : row + 1], 32)
            right.append(jnp.where(row128 == low_rows(lows[row : row + 1], LANES), one, zero))
            left.append(
                jnp.concatenate([jnp.where(chosen, low_rows(scores[n][row : row + 1], 32), zero) for n in range(HEADS)], axis=0)
            )
        acc_s[0 : 32 * HEADS, :] += dot_nt(jnp.concatenate(left, axis=1), jnp.concatenate(right, axis=1))
        return carry

    lax.fori_loop(0, DENSE // 16, scatter, 0)
    for block in range(16):
        parts_s[block // 8, block % 8] = jnp.where(sub16 < 12, acc_s[12 * block : 12 * block + 16, :], 0.0)

    bcore = remote(parts_s.at[other], bcore_r, bcore_ss, bcore_rs, at(x, y, z, other))
    bcore.start()
    sends.append(bcore)
    bcore.wait_recv()
    for part in range(ZLO):
        bline_s[part] = (parts_s[core, part] + bcore_r[part]).astype(BF16)
    bline_r[z_lo] = bline_s[z_lo]
    bline_copies = []
    for d in range(1, ZLO):
        to = (z_lo + d) & 7
        copy = remote(
            bline_s.at[to], bline_r.at[z_lo], bline_ss.at[d], bline_rs.at[d], at(x, y, z_hi * ZLO + to, core)
        )
        copy.start()
        bline_copies.append(copy)
    sends += bline_copies

    for d in range(1, 16):
        source = ((x + (d >> 2)) & 3) * 4 + ((y + d) & 3)
        remote(
            plane_s.at[0, 0, 0], plane_r.at[source], plane_ss.at[0], plane_rs.at[source], at(x, y, z, other)
        ).wait_recv()
    for part in range(ZLO):
        block = plane_r[0, part].astype(F32)
        for source in range(1, 16):
            block = block + plane_r[source, part].astype(F32)
        line_s[part] = block.astype(BF16)
    line_r[z] = line_s[z_lo]
    line_copies = []
    for d in range(1, 16):
        to = (z + d) & 15
        copy = remote(line_s.at[to & 7], line_r.at[z], line_ss.at[d], line_rs.at[d], at(x, y, to, core))
        copy.start()
        line_copies.append(copy)
    sends += line_copies

    for copy in bline_copies:
        copy.wait_recv()
    part_sum = bline_r[0].astype(F32)
    for part in range(1, ZLO):
        part_sum = part_sum + bline_r[part].astype(F32)
    brow_r[y] = part_sum
    brow_copies = []
    for d in range(1, 4):
        to = (y + d) & 3
        copy = remote(brow_r.at[y], brow_r.at[y], brow_ss.at[d], brow_rs.at[d], at(x, to, z, core))
        copy.start()
        brow_copies.append(copy)
    sends += brow_copies

    for copy in brow_copies:
        copy.wait_recv()
    bias_part = (brow_r[0] + brow_r[1]) + (brow_r[2] + brow_r[3])
    for copy in line_copies:
        copy.wait_recv()
    piece = line_r[0].astype(F32)
    for source in range(1, 16):
        piece = piece + line_r[source].astype(F32)
    square = 0.5 * jnp.sum(piece * piece) + 0.25 * jnp.sum(bias_part * bias_part)
    squares_z[z] = jnp.full((1, LANES), square, F32)
    sz_copies = []
    for d in range(1, 16):
        to = (z + d) & 15
        copy = remote(squares_z.at[z], squares_z.at[z], sz_ss.at[d], sz_rs.at[d], at(x, y, to, core))
        copy.start()
        sz_copies.append(copy)
    sends += sz_copies
    mine = core * 4 + x
    share[mine] = piece
    share_copies = []
    for dx, dcore in ((1, 0), (2, 0), (3, 0), (0, 1), (1, 1), (2, 1), (3, 1)):
        d = dcore * 4 + dx
        copy = remote(
            share.at[mine],
            share.at[mine],
            share_ss.at[d],
            share_rs.at[d],
            at((x + dx) & 3, y, z, core + dcore * (1 - 2 * core)),
        )
        copy.start()
        share_copies.append(copy)
    sends += share_copies
    ball[core, z_lo] = bias_part
    ball_copies = []
    for d in range(1, ZLO):
        to = (z_lo + d) & 7
        copy = remote(
            ball.at[core, z_lo], ball.at[core, z_lo], ball_ss.at[d], ball_rs.at[d], at(x, y, z_hi * ZLO + to, core)
        )
        copy.start()
        ball_copies.append(copy)
    sends += ball_copies

    for copy in sz_copies:
        copy.wait_recv()
    square = squares_z[0]
    for source in range(1, 16):
        square = square + squares_z[source]
    spot = core * 16 + x * 4 + y
    squares_y[spot] = square
    sy_copies = []
    for d in range(1, 32):
        target = at((x + (d >> 2 & 3)) & 3, (y + (d & 3)) & 3, z, core + (d >> 4) * (1 - 2 * core))
        copy = remote(squares_y.at[spot], squares_y.at[spot], sy_ss.at[d], sy_rs.at[d], target)
        copy.start()
        sy_copies.append(copy)
    sends += sy_copies
    for copy in ball_copies:
        copy.wait_recv()
    bpair = remote(ball.at[core], ball.at[core], bpair_ss, bpair_rs, at(x, y, z, other))
    bpair.start()
    sends.append(bpair)
    for copy in share_copies:
        copy.wait_recv()
    dense_out[...] = share[...]
    back_out[3] = back_s[0]
    for slot, copy in back_copies:
        copy.wait_recv()
        back_out[3 - slot] = back_r[3 - slot]
    for copy in sy_copies:
        copy.wait_recv()
    square = squares_y[0]
    for source in range(1, 32):
        square = square + squares_y[source]
    total_out[...] = square
    bpair.wait_recv()
    bias_out[...] = ball[...]
    for copy in sends:
        copy.wait_send()


def main(*operands):
    token = np.arange(TOK)
    slot, level, cell = token // PART, (token % PART) // CELLS, token % CELLS
    row, col = 3 * (slot // 2) + cell // 6, 6 * (slot % 2) + cell % 6
    order = np.zeros((TOK, TOK), np.float32)
    order[token, (row * WIN_LON + col) * 2 + level] = 1.0
    operands = operands[:6] + (jnp.asarray(order, BF16),) + operands[6:]
    vmem = pl.BlockSpec(memory_space=pltpu.VMEM)
    dma = pltpu.SemaphoreType.DMA
    return pl.pallas_call(
        main_kernel,
        out_shape=(
            jax.ShapeDtypeStruct((8, 16, LANES), F32),
            jax.ShapeDtypeStruct((2, ZLO, 16, LANES), F32),
            jax.ShapeDtypeStruct((4, 64, LANES), BF16),
            jax.ShapeDtypeStruct((1, LANES), F32),
        ),
        in_specs=[pl.BlockSpec(memory_space=pl.ANY)] * 13,
        out_specs=(vmem,) * 4,
        scratch_shapes=[pltpu.VMEM(v.shape, v.dtype) for v in operands] + [
            pltpu.VMEM((4, 24, 2 * C), F32),
            pltpu.VMEM((4, 8, LANES), F32),
            pltpu.VMEM((4, 40, 2 * C), F32),
            pltpu.VMEM((4, SENT, LANES), F32),
            pltpu.VMEM((4, SENT, LANES), F32),
            pltpu.VMEM((4, SENT, LANES), BF16),
            pltpu.VMEM((4, SENT, LANES), BF16),
            pltpu.VMEM((4, SENT, LANES), BF16),
            pltpu.VMEM((4, SENT, LANES), BF16),
            pltpu.VMEM((HEADS * 32, LANES), F32),
            pltpu.VMEM((HEADS * DENSE, LANES), F32),
            pltpu.VMEM((DENSE, LANES), F32),
            pltpu.VMEM((DENSE, LANES), F32),
            pltpu.VMEM((HEADS * TOK, TOK), F32),
            pltpu.VMEM((FF, FF), BF16),
            pltpu.VMEM((4, 40, 2 * C), F32),
            pltpu.VMEM((TOK, C), F32),
            pltpu.VMEM((TOK, C), F32),
            pltpu.VMEM((TOK, LANES), F32),
            pltpu.VMEM((C, LANES), F32),
            pltpu.VMEM((TOK, C), F32),
            pltpu.VMEM((4, SENT, LANES), F32),
            pltpu.VMEM((HEADS * TOK, TOK), F32),
            pltpu.VMEM((32, LANES), F32),
            pltpu.VMEM((4, 64, LANES), BF16),
            pltpu.VMEM((C, COLS), F32),
            pltpu.VMEM((2, 4, 304, LANES), F32),
            pltpu.VMEM((2, 4, 168, LANES), F32),
            pltpu.VMEM((2, 2, 4, 2, ZLO, 16, LANES), BF16),
            pltpu.VMEM((208, LANES), F32),
            pltpu.VMEM((2, ZLO, 16, LANES), F32),
            pltpu.VMEM((2, 4, 2, ZLO, 16, LANES), BF16),
            pltpu.VMEM((2, 4, 2, ZLO, 16, LANES), BF16),
            pltpu.VMEM((16, ZLO, 16, LANES), BF16),
            pltpu.VMEM((ZLO, 16, LANES), BF16),
            pltpu.VMEM((16, 16, LANES), BF16),
            pltpu.VMEM((8, 16, LANES), F32),
            pltpu.VMEM((ZLO, 16, LANES), F32),
            pltpu.VMEM((ZLO, 16, LANES), BF16),
            pltpu.VMEM((ZLO, 16, LANES), BF16),
            pltpu.VMEM((4, 16, LANES), F32),
            pltpu.VMEM((2, ZLO, 16, LANES), F32),
            pltpu.VMEM((4, 64, LANES), BF16),
            pltpu.VMEM((16, 1, LANES), F32),
            pltpu.VMEM((32, 1, LANES), F32),
            dma((13,)),
            dma((8,)), dma((8,)),
            dma((4,)), dma((4,)),
            dma((16,)), dma((16,)),
            dma((16,)), dma((16,)),
            dma((8,)), dma((8,)),
            dma, dma,
            dma((8,)), dma((8,)),
            dma((4,)), dma((4,)),
            dma((8,)), dma((8,)),
            dma, dma,
            dma((4,)), dma((4,)),
            dma((16,)), dma((16,)),
            dma((32,)), dma((32,)),
        ],
        compiler_params=pltpu.CompilerParams(collective_id=0, has_side_effects=True, vmem_limit_bytes=VMEM_LIMIT),
        name="window_and_sums",
    )(*operands)


def output_kernel(
    dense_ref, bias_ref, back_ref, total_ref,
    token_ref, mix_ref, out_ref, up_ref, down_ref, gain_ref, embed_ref, table_ref,
    dense_s, flat_s, bias_s, back_s, token_s,
):
    count = C * COLS + (KINDS + 2) * C + LAT * HEADS * PAIRS
    factor = lax.rsqrt(total_ref[...] / count + RMS_EPS)
    odd = lax.axis_index("lon") % 2 == 1
    for part in range(8):
        dense_s[part // 4, 16 * (part % 4) : 16 * (part % 4) + 16, :] = dense_ref[part] * factor
    for tile in range(TILES):
        if tile < 6:
            half, start, step = tile // 3, 36 + tile % 3, 3
        else:
            half, start, step = (tile - 6) // 6, tile % 6, 6
        even_rows = dense_s[half, pl.ds(start, 3, stride=step), :]
        odd_rows = dense_s[half, pl.ds(start + 3 * step, 3, stride=step), :]
        flat_s[0:3, tile * LANES : (tile + 1) * LANES] = jnp.where(odd, odd_rows, even_rows)
    flat = flat_s[0:3, :]
    mix_ref[...] = flat[:, 0 : 3 * C]
    out_ref[...] = flat[:, 3 * C : 4 * C]
    up_ref[...] = flat[:, 4 * C : 8 * C]
    for row in range(3):
        for part in range(4):
            down_ref[4 * row + part : 4 * row + part + 1, :] = flat[row : row + 1, (8 + part) * C : (9 + part) * C]
    extra = dense_s[0, 54:55, :]
    lane = lax.broadcasted_iota(jnp.int32, (24, LANES), 1)
    sub = lax.broadcasted_iota(jnp.int32, (24, LANES), 0)
    small = jnp.zeros((24, LANES), F32)
    wide = jnp.zeros((8, LANES), F32)
    sub8 = lax.broadcasted_iota(jnp.int32, (8, LANES), 0)
    line8 = jnp.broadcast_to(extra, (8, LANES))
    for row in range(3):
        turned = jnp.where(odd, pltpu.roll(line8, LANES - 18 * (3 + row), 1), pltpu.roll(line8, (LANES - 18 * row) % LANES, 1))
        wide = jnp.where(sub8 == row, turned, wide)
        start = jnp.where(odd, 18 * (3 + row), 18 * row)
        column = jnp.sum(jnp.where(lane == sub + start, extra, 0.0), axis=1, keepdims=True)
        small = small + jnp.where(lane == row, column, 0.0)
    embed_ref[...] = wide[0:3, 0:KINDS]
    gain_ref[...] = small[KINDS : KINDS + 2, 0:3]
    for block in range(16):
        bias_s[12 * block : 12 * block + 12, :] = bias_ref[block // 8, block % 8, 0:12, :] * factor
    for row in range(HI):
        width = min(LANES, PAIRS - row * LANES)
        line = bias_s[pl.ds(row, HEADS, stride=32), :][:, 0:width]
        for head in range(HEADS):
            table_ref[head, :, row * LANES : row * LANES + width] = line[head : head + 1]
    for quarter in range(4):
        packed = back_ref[quarter].astype(F32)
        for tile in range(3):
            back_s[quarter, 0:CELLS, tile * LANES : (tile + 1) * LANES] = packed[CELLS * tile : CELLS * tile + CELLS]
        for i in range(3):
            row, half = 3 * (quarter // 2) + i, quarter % 2
            token_s[row, 6 * half : 6 * half + 6, :] = back_s[quarter, 6 * i : 6 * i + 6, :]
    for row in range(WIN_LAT):
        token_ref[row] = token_s[row, 0:WIN_LON, :].astype(BF16)


def outputs(dense, bias, back, total):
    vmem = pl.BlockSpec(memory_space=pltpu.VMEM)
    return pl.pallas_call(
        output_kernel,
        out_shape=(
            jax.ShapeDtypeStruct((WIN_LAT, WIN_LON, 2 * C), BF16),
            jax.ShapeDtypeStruct((3, 3 * C), F32),
            jax.ShapeDtypeStruct((3, C), F32),
            jax.ShapeDtypeStruct((3, FF), F32),
            jax.ShapeDtypeStruct((12, C), F32),
            jax.ShapeDtypeStruct((2, 3), F32),
            jax.ShapeDtypeStruct((3, KINDS), F32),
            jax.ShapeDtypeStruct((HEADS, 1, PAIRS), F32),
        ),
        in_specs=[vmem] * 4,
        out_specs=(vmem,) * 8,
        scratch_shapes=[
            pltpu.VMEM((2, 64, LANES), F32),
            pltpu.VMEM((8, COLS), F32),
            pltpu.VMEM((HEADS * 32, LANES), F32),
            pltpu.VMEM((4, 32, 2 * C), F32),
            pltpu.VMEM((WIN_LAT, 16, 2 * C), F32),
        ],
        compiler_params=pltpu.CompilerParams(vmem_limit_bytes=VMEM_LIMIT),
        name="scaled_outputs",
    )(dense, bias, back, total)


def shards(
    tokens, kinds, kind_embed, pair_index, bias_table, attn_gain, mlp_gain,
    mix_weight, out_weight, up_weight, down_weight, cotangent,
):
    sums = main(
        tokens, kinds.transpose(0, 2, 1), kind_embed, cotangent, pair_index, bias_table.transpose(1, 0, 2),
        attn_gain.reshape(1, C), mlp_gain.reshape(1, C), mix_weight, out_weight, up_weight, down_weight.T,
    )
    token, mix, out, up, down, gain, embed, table = outputs(*sums)
    return token, mix, out, up, down, gain, embed.T, table.transpose(1, 0, 2)


def solution(mesh):
    return jax.shard_map(
        shards,
        mesh=mesh,
        in_specs=(
            P("lat", "lon", None),
            P("lat", "lon", None),
            P(),
            P(),
            P("lat", None, None),
            P(),
            P(),
            P(),
            P(),
            P(),
            P(),
            P("lat", "lon", None),
        ),
        out_specs=(
            P("lat", "lon", None),
            P("lon", None),
            P("lon", None),
            P("lon", None),
            P("lon", None),
            P(None, "lon"),
            P(None, "lon"),
            P("lat", None, None),
        ),
        check_vma=False,
    )
```

```python
import jax
import jax.numpy as jnp
import numpy as np
from jax import lax
from jax.experimental import pallas as pl
from jax.experimental.pallas import tpu as pltpu
from jax.sharding import PartitionSpec as P

F32 = jnp.float32
BF16 = jnp.bfloat16
MESH = pl.DeviceIdType.MESH

C = 192
HEADS = 6
HEAD = 32
FF = 768
WIN_LAT = 6
WIN_LON = 12
KINDS = 16
PAIRS = 3312
TOK = 144
CELLS = 18
PART = 36
LANES = 128
HI = 26
COLS = 2304
TILES = 18
NORM_EPS = 1e-05
RMS_EPS = 1e-06
GELU_SQRT = 0.7978845608028654
GELU_CUBE = 0.044715
LON, LAT = 64, 8
FIXED = 8191.0
ZLO = 8
VMEM_LIMIT = 56 * 1024 * 1024


def coords(lat, lon):
    return lat >> 1, lon >> 4, ((lat & 1) << 3) + ((lon >> 1) & 7), lon & 1


def at(x, y, z, core):
    return {"lon": (y << 4) + ((z & 7) << 1) + core, "lat": (x << 1) + (z >> 3)}


def beside(lat, lon, rows, columns):
    return {"lon": (lon + columns) & (LON - 1), "lat": (lat + rows) & (LAT - 1)}


def dot(a, b):
    return lax.dot_general(a, b, (((1,), (0,)), ((), ())), preferred_element_type=F32)


def dot_nt(a, b):
    return lax.dot_general(a, b, (((1,), (1,)), ((), ())), preferred_element_type=F32)


def dot_tn(a, b):
    return lax.dot_general(a, b, (((0,), (0,)), ((), ())), preferred_element_type=F32)


def two_terms(v):
    high = v.astype(BF16)
    return high, (v - high.astype(F32)).astype(BF16)


def dense_rows(ref, values, base):
    ref[base : base + TOK, :] = values[:, 0:LANES]
    tail = values[:, LANES:TOK]
    tail = jnp.concatenate([tail, jnp.zeros((TOK, LANES - 16), tail.dtype)], axis=1)
    row = tail[0:16]
    for group in range(1, 8):
        row = row + pltpu.roll(tail[16 * group : 16 * group + 16], 16 * group, 1)
    ref[base + TOK : base + TOK + 16, :] = row
    ref[base + TOK + 16 : base + TOK + 32, :] = tail[LANES:TOK]


DENSE = TOK + 32
FLAT = 3 * PART
SENT = FLAT + 4


def layer_norm(values, gain):
    centred = values - jnp.mean(values, axis=-1, keepdims=True)
    inverse = lax.rsqrt(jnp.mean(centred * centred, axis=-1, keepdims=True) + NORM_EPS)
    normed = centred * inverse
    return normed * gain, normed, inverse


def norm_backward(upstream, normed, inverse, gain):
    scaled = upstream * gain
    return inverse * (
        scaled
        - jnp.mean(scaled, axis=-1, keepdims=True)
        - normed * jnp.mean(scaled * normed, axis=-1, keepdims=True)
    )


def main_kernel(
    tok_in, kind_in, embed_in, cot_in, index_in, table_in, order_in,
    gain1_in, gain2_in, mix_in, outw_in, up_in, down_in,
    dense_out, bias_out, back_out, total_out,
    tok_ref, kind_ref, embed_ref, cot_ref, index_ref, table_ref, order_ref,
    gain1_ref, gain2_ref, mix_ref, outw_ref, up_ref, down_ref,
    tok_s, kind_s, flat_s, pack_s, send, recv, table_s, pairs_s, dense_s, high_s, low_s, bias_s, spread_s,
    grid_s, x_s, g_s, hot_s, ge_s, moved_s, unpack_s, score_s, extra_s, back_s,
    grad_s, rows_s, grads, acc_s, parts_s,
    core_r, plane_s, plane_r, line_s, line_r, share, bcore_r, bline_s, bline_r, brow_r, ball, back_r, squares_z, squares_y,
    in_sems, halo_ss, halo_rs,
    core_ss, core_rs, plane_ss, plane_rs, line_ss, line_rs, share_ss, share_rs, bcore_ss, bcore_rs, bline_ss, bline_rs,
    brow_ss, brow_rs, ball_ss, ball_rs, bpair_ss, bpair_rs, back_ss, back_rs, sz_ss, sz_rs, sy_ss, sy_rs,
):
    lon, lat = lax.axis_index("lon"), lax.axis_index("lat")
    x, y, z, core = coords(lat, lon)
    z_lo, z_hi = z & 7, z >> 3
    other = 1 - core

    def remote(src, dst, send_sem, recv_sem, target):
        return pltpu.make_async_remote_copy(
            src_ref=src, dst_ref=dst, send_sem=send_sem, recv_sem=recv_sem, device_id=target, device_id_type=MESH
        )

    sources = (
        tok_in, kind_in, embed_in, cot_in, index_in, table_in, order_in,
        gain1_in, gain2_in, mix_in, outw_in, up_in, down_in,
    )
    targets = (
        tok_ref, kind_ref, embed_ref, cot_ref, index_ref, table_ref, order_ref,
        gain1_ref, gain2_ref, mix_ref, outw_ref, up_ref, down_ref,
    )
    fetches = [pltpu.make_async_copy(s, t, in_sems.at[i]) for i, (s, t) in enumerate(zip(sources, targets))]
    for fetch in fetches[:4]:
        fetch.start()

    barrier = pltpu.get_barrier_semaphore()
    peers = []
    for dr, dc in ((1, 0), (0, 1), (1, 1)):
        peers += [beside(lat, lon, -dr, -dc), beside(lat, lon, dr, dc)]
    peers += [at(x, y, (z + d) & 15, core) for d in range(1, 16)]
    peers += [at((x + d // 4) & 3, (y + d % 4) & 3, z, core) for d in range(1, 16)]
    peers += [at((x + d // 4) & 3, (y + d % 4) & 3, z, other) for d in range(16)]
    for peer in peers:
        pl.semaphore_signal(barrier, inc=1, device_id=peer, device_id_type=MESH)

    for fetch in fetches[4:]:
        fetch.start()
    for fetch in fetches[:4]:
        fetch.wait()
    embed = embed_ref[...].astype(F32)
    blank = jnp.zeros((KINDS, C), F32)
    wide = jnp.concatenate(
        [jnp.concatenate([embed, blank], axis=1), jnp.concatenate([blank, embed], axis=1)], axis=0
    ).astype(BF16)
    kind_s[...] = jnp.zeros((4, 8, LANES), F32)
    for row in range(WIN_LAT):
        tok = tok_ref[row].astype(F32)
        cot = cot_ref[row].astype(F32)
        kind = kind_ref[row].astype(F32)
        for half in range(2):
            quarter = 2 * (row // 3) + half
            start = 6 * (row % 3)
            cells = slice(6 * half, 6 * half + 6)
            tok_s[quarter, start : start + 6, :] = tok[cells]
            flat_s[quarter, CELLS + start : CELLS + start + 6, :] = cot[cells]
            kind_s[quarter, 0:2, start : start + 6] = kind[:, cells]
    sub = lax.broadcasted_iota(jnp.int32, (2 * KINDS, LANES), 0).astype(F32)
    for quarter in range(4):
        kinds = kind_s[quarter]
        hot = (sub == kinds[0:1]) | (sub - KINDS == kinds[1:2])
        hot = jnp.where(hot, 1.0, 0.0).astype(BF16)[:, 0:24]
        stored = tok_s[quarter] + dot_tn(hot, wide)
        flat_s[quarter, 0:CELLS, :] = stored[0:CELLS]
        for tile in range(3):
            pack_s[quarter, PART * tile : PART * tile + PART, :] = flat_s[
                quarter, 0:PART, tile * LANES : (tile + 1) * LANES
            ]
        pack_s[quarter, FLAT:SENT, :] = jnp.zeros((4, LANES), F32)
        pack_s[quarter, FLAT : FLAT + 1, :] = kinds[0:1] + pltpu.roll(kinds, CELLS, 1)[1:2]
        send[quarter] = pack_s[quarter].astype(BF16)
    pl.semaphore_wait(barrier, len(peers))
    halo_copies = []
    for slot in (3, 2, 1):
        copy = remote(
            send.at[3 - slot], recv.at[slot], halo_ss.at[slot], halo_rs.at[slot], beside(lat, lon, -(slot // 2), -(slot % 2))
        )
        copy.start()
        halo_copies.append(copy)
    sends = list(halo_copies)

    for fetch in fetches[4:7]:
        fetch.wait()
    order = order_ref[...]
    index = index_ref[...]
    high = (index >> 7).astype(F32).astype(BF16)
    low = (index & (LANES - 1)).astype(F32).astype(BF16)
    dense_rows(high_s, dot_nt(dot(order, high).astype(BF16), order), 0)
    dense_rows(low_s, dot_nt(dot(order, low).astype(BF16), order), 0)
    table_s[...] = jnp.zeros((HEADS * 32, LANES), F32)
    for row in range(HI):
        width = min(LANES, PAIRS - row * LANES)
        for head in range(HEADS):
            table_s[32 * head + row : 32 * head + row + 1, 0:width] = table_ref[
                head, :, row * LANES : row * LANES + width
            ]

    column = lax.broadcasted_iota(jnp.int32, (1, FF), 1)
    part = jnp.where(column >= C, 1, 0) + jnp.where(column >= 2 * C, 1, 0) + jnp.where(column >= 3 * C, 1, 0)
    unit = (4 * (column - C * part) + part).astype(F32)
    for block in range(6):
        place_at = (lax.broadcasted_iota(jnp.int32, (LANES, FF), 0) + LANES * block).astype(F32)
        spread_s[LANES * block : LANES * (block + 1), :] = jnp.where(place_at == unit, 1.0, 0.0).astype(BF16)

    for pair in range(3):
        fixed = [
            ((table_s[64 * pair + 32 * k : 64 * pair + 32 * k + 32, :] + 4.0) * FIXED + 0.5).astype(jnp.int32) for k in range(2)
        ]
        pairs_s[32 * pair : 32 * pair + 32, :] = (fixed[0] << 16) | fixed[1]

    def gather(step, carry):
        start = pl.multiple_of(step * 16, 16)
        lows = low_s[pl.ds(start, 16), :].astype(jnp.int32)
        highs = high_s[pl.ds(start, 16), :]
        totals = [jnp.zeros((16, LANES), jnp.int32) for _ in range(3)]
        for row in range(HI):
            chosen = highs == float(row)
            for pair in range(3):
                line = jnp.broadcast_to(pairs_s[32 * pair + row : 32 * pair + row + 1, :], (16, LANES))
                found = jnp.take_along_axis(line, lows, axis=1, mode="promise_in_bounds")
                totals[pair] = jnp.where(chosen, found, totals[pair])
        for head in range(HEADS):
            fixed = totals[head // 2]
            fixed = (fixed if head % 2 else fixed >> 16) & 0xFFFF
            dense_s[pl.ds(pl.multiple_of(head * DENSE + start, 16), 16), :] = fixed.astype(F32) * (1.0 / FIXED) - 4.0
        return carry

    lax.fori_loop(0, DENSE // 16, gather, 0)
    for head in range(HEADS):
        base = head * DENSE
        bias_s[head * TOK : head * TOK + TOK, 0:LANES] = dense_s[base : base + TOK, :]
        row = dense_s[base + TOK : base + TOK + 16, :]
        for group in range(8):
            turned = row if group == 0 else pltpu.roll(row, LANES - 16 * group, 1)
            bias_s[head * TOK + 16 * group : head * TOK + 16 * group + 16, LANES:TOK] = turned[:, 0:16]
        bias_s[head * TOK + LANES : head * TOK + TOK, LANES:TOK] = dense_s[base + TOK + 16 : base + TOK + 32, 0:16]

    for copy in halo_copies:
        copy.wait_recv()
    lane36 = lax.broadcasted_iota(jnp.int32, (PART, LANES), 1)
    sub36 = lax.broadcasted_iota(jnp.int32, (PART, LANES), 0)
    for slot in range(4):
        unpack_s[slot] = (send[3] if slot == 0 else recv[slot]).astype(F32)
        for tile in range(3):
            grid_s[slot, 0:PART, tile * LANES : (tile + 1) * LANES] = unpack_s[slot, PART * tile : PART * tile + PART, :]
        toks = grid_s[slot, 0:CELLS, :]
        cots = grid_s[slot, CELLS:PART, :]
        base = PART * slot
        x_s[base : base + CELLS, :] = toks[:, 0:C]
        x_s[base + CELLS : base + PART, :] = toks[:, C : 2 * C]
        g_s[base : base + CELLS, :] = cots[:, 0:C]
        g_s[base + CELLS : base + PART, :] = cots[:, C : 2 * C]
        kind_row = unpack_s[slot, FLAT : FLAT + 1, :]
        kind_col = jnp.sum(jnp.where(lane36 == sub36, kind_row, 0.0), axis=1, keepdims=True)
        hot_s[base : base + PART, :] = jnp.where(lane36.astype(F32) == kind_col, 1.0, 0.0)

    for fetch in fetches[7:]:
        fetch.wait()
    gain1, gain2 = gain1_ref[...], gain2_ref[...]
    mix_weight, out_weight = mix_ref[...], outw_ref[...]
    up_weight, down_weight = up_ref[...], down_ref[...]
    residual = x_s[...]
    upstream = g_s[...]
    upstream_low = upstream.astype(BF16)
    first, hat1, inv1 = layer_norm(residual, gain1)
    first_in = first.astype(BF16)
    mixed = dot(first_in, mix_weight)
    queries = mixed[:, 0:C].astype(BF16).astype(F32)
    keys = mixed[:, C : 2 * C].astype(BF16)
    values = mixed[:, 2 * C : 3 * C].astype(BF16)
    channel = lax.broadcasted_iota(jnp.int32, (TOK, C), 1)
    of_head = [(channel >= HEAD * n) & (channel < HEAD * n + HEAD) for n in range(HEADS)]
    q_stack = jnp.concatenate([jnp.where(m, queries, 0.0) for m in of_head], axis=0).astype(BF16)
    scores = dot_nt(q_stack, keys) * (HEAD**-0.5) + bias_s[...]
    last = lat == LAT - 1
    group_q = jnp.where(lax.broadcasted_iota(jnp.int32, (TOK, TOK), 0) >= 72, 1.0, 0.0)
    group_k = jnp.where(lax.broadcasted_iota(jnp.int32, (TOK, TOK), 1) >= 72, 1.0, 0.0)
    apart = jnp.abs(group_q - group_k) * jnp.where(last, 1.0, 0.0)
    allowed = jnp.concatenate([apart] * HEADS, axis=0) < 0.5
    expon = jnp.where(allowed, jnp.exp(scores), 0.0)
    attend = expon * (1.0 / jnp.sum(expon, axis=-1, keepdims=True))
    attend_low = attend.astype(BF16)
    context = jnp.zeros((TOK, C), F32)
    for n in range(HEADS):
        context += jnp.where(of_head[n], dot(attend_low[n * TOK : (n + 1) * TOK], values), 0.0)
    context = context.astype(BF16)
    mid = residual + dot(context, out_weight)
    second, hat2, inv2 = layer_norm(mid, gain2)
    second_in = second.astype(BF16)
    inner = dot(second_in, up_weight)
    tangent = jnp.tanh(GELU_SQRT * (inner + GELU_CUBE * inner * inner * inner))
    hidden_low = (0.5 * inner * (1.0 + tangent)).astype(BF16)
    slope = 0.5 * (1.0 + tangent) + 0.5 * inner * (1.0 - tangent * tangent) * GELU_SQRT * (
        1.0 + 3.0 * GELU_CUBE * inner * inner
    )
    hidden_grad = (dot(upstream_low, down_weight) * slope).astype(BF16)
    second_grad = dot_nt(hidden_grad, up_weight)
    mid_grad = upstream + norm_backward(second_grad, hat2, inv2, gain2)
    mid_low = mid_grad.astype(BF16)
    context_grad = dot_nt(mid_low, out_weight).astype(BF16).astype(F32)
    c_stack = jnp.concatenate([jnp.where(m, context_grad, 0.0) for m in of_head], axis=0).astype(BF16)
    attend_grad = dot_nt(c_stack, values)
    value_grad = dot_tn(attend_low, c_stack).astype(BF16)
    score_grad = attend * (attend_grad - jnp.sum(attend * attend_grad, axis=-1, keepdims=True))
    score_s[...] = score_grad
    score_low = score_grad.astype(BF16)
    query_grad = jnp.zeros((TOK, C), F32)
    for n in range(HEADS):
        query_grad += jnp.where(of_head[n], dot(score_low[n * TOK : (n + 1) * TOK], keys), 0.0)
    query_grad = (query_grad * (HEAD**-0.5)).astype(BF16)
    key_grad = (dot_tn(score_low, q_stack) * (HEAD**-0.5)).astype(BF16)
    first_grad = (
        dot_nt(query_grad, mix_weight[:, 0:C])
        + dot_nt(key_grad, mix_weight[:, C : 2 * C])
        + dot_nt(value_grad, mix_weight[:, 2 * C : 3 * C])
    )
    moved = mid_grad + norm_backward(first_grad, hat1, inv1, gain1)

    lane = lax.broadcasted_iota(jnp.int32, (TOK, LANES), 1)
    small = jnp.zeros((C, LANES), F32)
    for left, right in (
        (moved, hot_s[...]),
        (first_grad * hat1, jnp.where(lane == KINDS, 1.0, 0.0)),
        (second_grad * hat2, jnp.where(lane == KINDS + 1, 1.0, 0.0)),
    ):
        for term in two_terms(left):
            small += dot_tn(term, right.astype(BF16))
    ge_s[...] = small
    extra = jnp.zeros((32, LANES), F32)
    for k in range(6):
        line = ge_s[pl.ds(k, 32, stride=6), :]
        extra += pltpu.roll(line, 18 * k, 1) if k else line
    extra_s[...] = extra

    grad_s[:, 0:C] = dot_tn(first_in, query_grad)
    grad_s[:, C : 2 * C] = dot_tn(first_in, key_grad)
    grad_s[:, 2 * C : 3 * C] = dot_tn(first_in, value_grad)
    grad_s[:, 3 * C : 4 * C] = dot_tn(context, mid_low)
    grad_s[:, 4 * C : 8 * C] = dot_tn(second_in, hidden_grad)
    spread = dot(hidden_low, spread_s[...]).astype(BF16)
    for part in range(4):
        grad_s[:, (8 + part) * C : (9 + part) * C] = dot_tn(spread[:, part * C : (part + 1) * C], upstream_low)
    for tile in range(TILES):
        for part in range(4):
            rows_s[tile // 9, part, pl.ds(tile % 9, 48, stride=9), :] = grad_s[
                48 * part : 48 * part + 48, tile * LANES : (tile + 1) * LANES
            ]
    sub64 = lax.broadcasted_iota(jnp.int32, (64, LANES), 0)

    def blocks(half, part):
        for block in range(ZLO):
            got = rows_s[half, part, 54 * block : 54 * block + 64, :]
            line = extra_s[pl.ds(part * ZLO + block, 1), :] * jnp.where(half == 0, 1.0, 0.0)
            got = jnp.where(sub64 < 54, got, jnp.where(sub64 == 54, line, 0.0)).astype(BF16)
            for quarter in range(4):
                grads[half, part, quarter, block] = got[16 * quarter : 16 * quarter + 16]

    core_copies = []
    for j in range(4):
        to = (y + 1 + j) & 3
        blocks(other, to)
        copy = remote(grads.at[other, to], core_r.at[to], core_ss.at[j], core_rs.at[j], at(x, y, z, other))
        copy.start()
        core_copies.append(copy)
    sends += core_copies
    moved_s[...] = moved
    for slot in range(4):
        base = PART * slot
        grid_s[slot, 0:CELLS, 0:C] = moved_s[base : base + CELLS, :]
        grid_s[slot, 0:CELLS, C : 2 * C] = moved_s[base + CELLS : base + PART, :]
        for tile in range(3):
            unpack_s[slot, CELLS * tile : CELLS * tile + CELLS, :] = grid_s[
                slot, 0:CELLS, tile * LANES : (tile + 1) * LANES
            ]
        back_s[slot] = unpack_s[slot, 0:64, :].astype(BF16)

    back_copies = []
    for slot in (3, 2, 1):
        copy = remote(
            back_s.at[slot], back_r.at[3 - slot], back_ss.at[slot], back_rs.at[slot], beside(lat, lon, slot // 2, slot % 2)
        )
        copy.start()
        back_copies.append((slot, copy))
    sends += [copy for _, copy in back_copies]

    plane_copies = {}
    for j in range(4):
        to_y = (y + 1 + j) & 3
        blocks(core, to_y)
        core_copies[j].wait_recv()
        for part in range(4):
            plane_s[to_y, part] = (grads[core, to_y, part].astype(F32) + core_r[to_y, part].astype(F32)).astype(BF16)
        for i in range(4):
            dx, dy = (i + 1) % 4, (j + 1) % 4
            d = dx * 4 + dy
            to_x = (x + dx) & 3
            if d == 0:
                plane_r[x * 4 + y] = plane_s[y, x]
                continue
            copy = remote(
                plane_s.at[to_y, to_x], plane_r.at[x * 4 + y], plane_ss.at[d], plane_rs.at[d], at(to_x, to_y, z, core)
            )
            copy.start()
            plane_copies[d] = copy
    sends += list(plane_copies.values())

    acc_s[...] = jnp.zeros((208, LANES), F32)
    for n in range(HEADS):
        dense_rows(dense_s, score_s[n * TOK : (n + 1) * TOK, :], n * DENSE)
    row32 = lax.broadcasted_iota(jnp.int32, (32, LANES), 0).astype(F32).astype(BF16)
    row128 = lax.broadcasted_iota(jnp.int32, (LANES, LANES), 0).astype(F32).astype(BF16)
    zero, one = jnp.zeros((), BF16), jnp.ones((), BF16)

    def low_rows(line, count):
        return jnp.concatenate([jnp.broadcast_to(line, (16, LANES)).astype(BF16)] * (count // 16), axis=0)

    def scatter(step, carry):
        left, right = [], []
        start = pl.multiple_of(step * 16, 16)
        highs, lows = high_s[pl.ds(start, 16), :], low_s[pl.ds(start, 16), :]
        scores = [dense_s[pl.ds(pl.multiple_of(n * DENSE + start, 16), 16), :] for n in range(HEADS)]
        for row in range(16):
            chosen = row32 == low_rows(highs[row : row + 1], 32)
            right.append(jnp.where(row128 == low_rows(lows[row : row + 1], LANES), one, zero))
            left.append(
                jnp.concatenate([jnp.where(chosen, low_rows(scores[n][row : row + 1], 32), zero) for n in range(HEADS)], axis=0)
            )
        acc_s[0 : 32 * HEADS, :] += dot_nt(jnp.concatenate(left, axis=1), jnp.concatenate(right, axis=1))
        return carry

    lax.fori_loop(0, DENSE // 16, scatter, 0)
    sub16 = lax.broadcasted_iota(jnp.int32, (16, LANES), 0)
    for block in range(16):
        parts_s[block // 8, block % 8] = jnp.where(sub16 < 12, acc_s[12 * block : 12 * block + 16, :], 0.0)

    bcore = remote(parts_s.at[other], bcore_r, bcore_ss, bcore_rs, at(x, y, z, other))
    bcore.start()
    sends.append(bcore)
    bcore.wait_recv()
    for part in range(ZLO):
        bline_s[part] = (parts_s[core, part] + bcore_r[part]).astype(BF16)
    bline_r[z_lo] = bline_s[z_lo]
    bline_copies = []
    for d in range(1, ZLO):
        to = (z_lo + d) & 7
        copy = remote(
            bline_s.at[to], bline_r.at[z_lo], bline_ss.at[d], bline_rs.at[d], at(x, y, z_hi * ZLO + to, core)
        )
        copy.start()
        bline_copies.append(copy)
    sends += bline_copies

    for copy in plane_copies.values():
        copy.wait_recv()
    for part in range(ZLO):
        block = plane_r[0, part].astype(F32)
        for source in range(1, 16):
            block = block + plane_r[source, part].astype(F32)
        line_s[part] = block.astype(BF16)
    line_r[z] = line_s[z_lo]
    line_copies = []
    for d in range(1, 16):
        to = (z + d) & 15
        copy = remote(line_s.at[to & 7], line_r.at[z], line_ss.at[d], line_rs.at[d], at(x, y, to, core))
        copy.start()
        line_copies.append(copy)
    sends += line_copies

    for copy in bline_copies:
        copy.wait_recv()
    part_sum = bline_r[0].astype(F32)
    for part in range(1, ZLO):
        part_sum = part_sum + bline_r[part].astype(F32)
    brow_r[y] = part_sum
    brow_copies = []
    for d in range(1, 4):
        to = (y + d) & 3
        copy = remote(brow_r.at[y], brow_r.at[y], brow_ss.at[d], brow_rs.at[d], at(x, to, z, core))
        copy.start()
        brow_copies.append(copy)
    sends += brow_copies

    for copy in brow_copies:
        copy.wait_recv()
    bias_part = (brow_r[0] + brow_r[1]) + (brow_r[2] + brow_r[3])
    for copy in line_copies:
        copy.wait_recv()
    piece = line_r[0].astype(F32)
    for source in range(1, 16):
        piece = piece + line_r[source].astype(F32)
    square = 0.5 * jnp.sum(piece * piece) + 0.25 * jnp.sum(bias_part * bias_part)
    squares_z[z] = jnp.full((1, LANES), square, F32)
    sz_copies = []
    for d in range(1, 16):
        to = (z + d) & 15
        copy = remote(squares_z.at[z], squares_z.at[z], sz_ss.at[d], sz_rs.at[d], at(x, y, to, core))
        copy.start()
        sz_copies.append(copy)
    sends += sz_copies
    mine = core * 4 + x
    share[mine] = piece
    share_copies = []
    for dx, dcore in ((1, 0), (2, 0), (3, 0), (0, 1), (1, 1), (2, 1), (3, 1)):
        d = dcore * 4 + dx
        copy = remote(
            share.at[mine],
            share.at[mine],
            share_ss.at[d],
            share_rs.at[d],
            at((x + dx) & 3, y, z, core + dcore * (1 - 2 * core)),
        )
        copy.start()
        share_copies.append(copy)
    sends += share_copies
    ball[core, z_lo] = bias_part
    ball_copies = []
    for d in range(1, ZLO):
        to = (z_lo + d) & 7
        copy = remote(
            ball.at[core, z_lo], ball.at[core, z_lo], ball_ss.at[d], ball_rs.at[d], at(x, y, z_hi * ZLO + to, core)
        )
        copy.start()
        ball_copies.append(copy)
    sends += ball_copies

    for copy in sz_copies:
        copy.wait_recv()
    square = squares_z[0]
    for source in range(1, 16):
        square = square + squares_z[source]
    spot = core * 16 + x * 4 + y
    squares_y[spot] = square
    sy_copies = []
    for d in range(1, 32):
        target = at((x + (d >> 2 & 3)) & 3, (y + (d & 3)) & 3, z, core + (d >> 4) * (1 - 2 * core))
        copy = remote(squares_y.at[spot], squares_y.at[spot], sy_ss.at[d], sy_rs.at[d], target)
        copy.start()
        sy_copies.append(copy)
    sends += sy_copies
    for copy in ball_copies:
        copy.wait_recv()
    bpair = remote(ball.at[core], ball.at[core], bpair_ss, bpair_rs, at(x, y, z, other))
    bpair.start()
    sends.append(bpair)
    for copy in share_copies:
        copy.wait_recv()
    dense_out[...] = share[...]
    back_out[3] = back_s[0]
    for slot, copy in back_copies:
        copy.wait_recv()
        back_out[3 - slot] = back_r[3 - slot]
    for copy in sy_copies:
        copy.wait_recv()
    square = squares_y[0]
    for source in range(1, 32):
        square = square + squares_y[source]
    total_out[...] = square
    bpair.wait_recv()
    bias_out[...] = ball[...]
    for copy in sends:
        copy.wait_send()


def main(*operands):
    token = np.arange(TOK)
    slot, level, cell = token // PART, (token % PART) // CELLS, token % CELLS
    row, col = 3 * (slot // 2) + cell // 6, 6 * (slot % 2) + cell % 6
    order = np.zeros((TOK, TOK), np.float32)
    order[token, (row * WIN_LON + col) * 2 + level] = 1.0
    operands = operands[:6] + (jnp.asarray(order, BF16),) + operands[6:]
    vmem = pl.BlockSpec(memory_space=pltpu.VMEM)
    dma = pltpu.SemaphoreType.DMA
    return pl.pallas_call(
        main_kernel,
        out_shape=(
            jax.ShapeDtypeStruct((8, 16, LANES), F32),
            jax.ShapeDtypeStruct((2, ZLO, 16, LANES), F32),
            jax.ShapeDtypeStruct((4, 64, LANES), BF16),
            jax.ShapeDtypeStruct((1, LANES), F32),
        ),
        in_specs=[pl.BlockSpec(memory_space=pl.ANY)] * 13,
        out_specs=(vmem,) * 4,
        scratch_shapes=[pltpu.VMEM(v.shape, v.dtype) for v in operands] + [
            pltpu.VMEM((4, 24, 2 * C), F32),
            pltpu.VMEM((4, 8, LANES), F32),
            pltpu.VMEM((4, 40, 2 * C), F32),
            pltpu.VMEM((4, SENT, LANES), F32),
            pltpu.VMEM((4, SENT, LANES), BF16),
            pltpu.VMEM((4, SENT, LANES), BF16),
            pltpu.VMEM((HEADS * 32, LANES), F32),
            pltpu.VMEM((3 * 32, LANES), jnp.int32),
            pltpu.VMEM((HEADS * DENSE, LANES), F32),
            pltpu.VMEM((DENSE, LANES), F32),
            pltpu.VMEM((DENSE, LANES), F32),
            pltpu.VMEM((HEADS * TOK, TOK), F32),
            pltpu.VMEM((FF, FF), BF16),
            pltpu.VMEM((4, 40, 2 * C), F32),
            pltpu.VMEM((TOK, C), F32),
            pltpu.VMEM((TOK, C), F32),
            pltpu.VMEM((TOK, LANES), F32),
            pltpu.VMEM((C, LANES), F32),
            pltpu.VMEM((TOK, C), F32),
            pltpu.VMEM((4, SENT, LANES), F32),
            pltpu.VMEM((HEADS * TOK, TOK), F32),
            pltpu.VMEM((32, LANES), F32),
            pltpu.VMEM((4, 64, LANES), BF16),
            pltpu.VMEM((C, COLS), F32),
            pltpu.VMEM((2, 4, 448, LANES), F32),
            pltpu.VMEM((2, 4, 4, ZLO, 16, LANES), BF16),
            pltpu.VMEM((208, LANES), F32),
            pltpu.VMEM((2, ZLO, 16, LANES), F32),
            pltpu.VMEM((4, 4, ZLO, 16, LANES), BF16),
            pltpu.VMEM((4, 4, ZLO, 16, LANES), BF16),
            pltpu.VMEM((16, ZLO, 16, LANES), BF16),
            pltpu.VMEM((ZLO, 16, LANES), BF16),
            pltpu.VMEM((16, 16, LANES), BF16),
            pltpu.VMEM((8, 16, LANES), F32),
            pltpu.VMEM((ZLO, 16, LANES), F32),
            pltpu.VMEM((ZLO, 16, LANES), BF16),
            pltpu.VMEM((ZLO, 16, LANES), BF16),
            pltpu.VMEM((4, 16, LANES), F32),
            pltpu.VMEM((2, ZLO, 16, LANES), F32),
            pltpu.VMEM((4, 64, LANES), BF16),
            pltpu.VMEM((16, 1, LANES), F32),
            pltpu.VMEM((32, 1, LANES), F32),
            dma((13,)),
            dma((4,)), dma((4,)),
            dma((4,)), dma((4,)),
            dma((16,)), dma((16,)),
            dma((16,)), dma((16,)),
            dma((8,)), dma((8,)),
            dma, dma,
            dma((8,)), dma((8,)),
            dma((4,)), dma((4,)),
            dma((8,)), dma((8,)),
            dma, dma,
            dma((4,)), dma((4,)),
            dma((16,)), dma((16,)),
            dma((32,)), dma((32,)),
        ],
        compiler_params=pltpu.CompilerParams(collective_id=0, has_side_effects=True, vmem_limit_bytes=VMEM_LIMIT),
        name="window_and_sums",
    )(*operands)


def output_kernel(
    dense_ref, bias_ref, back_ref, total_ref,
    token_ref, mix_ref, out_ref, up_ref, down_ref, gain_ref, embed_ref, table_ref,
    dense_s, flat_s, bias_s, back_s, token_s,
):
    count = C * COLS + (KINDS + 2) * C + LAT * HEADS * PAIRS
    factor = lax.rsqrt(total_ref[...] / count + RMS_EPS)
    odd = lax.axis_index("lon") % 2 == 1
    for part in range(8):
        dense_s[part // 4, 16 * (part % 4) : 16 * (part % 4) + 16, :] = dense_ref[part] * factor
    for tile in range(TILES):
        half, t = tile // 9, tile % 9
        even_rows = dense_s[half, pl.ds(t, 3, stride=9), :]
        odd_rows = dense_s[half, pl.ds(27 + t, 3, stride=9), :]
        flat_s[0:3, tile * LANES : (tile + 1) * LANES] = jnp.where(odd, odd_rows, even_rows)
    flat = flat_s[0:3, :]
    mix_ref[...] = flat[:, 0 : 3 * C]
    out_ref[...] = flat[:, 3 * C : 4 * C]
    up_ref[...] = flat[:, 4 * C : 8 * C]
    for row in range(3):
        for part in range(4):
            down_ref[4 * row + part : 4 * row + part + 1, :] = flat[row : row + 1, (8 + part) * C : (9 + part) * C]
    extra = dense_s[0, 54:55, :]
    lane = lax.broadcasted_iota(jnp.int32, (24, LANES), 1)
    sub = lax.broadcasted_iota(jnp.int32, (24, LANES), 0)
    small = jnp.zeros((24, LANES), F32)
    wide = jnp.zeros((8, LANES), F32)
    sub8 = lax.broadcasted_iota(jnp.int32, (8, LANES), 0)
    line8 = jnp.broadcast_to(extra, (8, LANES))
    for row in range(3):
        turned = jnp.where(odd, pltpu.roll(line8, LANES - 18 * (3 + row), 1), pltpu.roll(line8, (LANES - 18 * row) % LANES, 1))
        wide = jnp.where(sub8 == row, turned, wide)
        start = jnp.where(odd, 18 * (3 + row), 18 * row)
        column = jnp.sum(jnp.where(lane == sub + start, extra, 0.0), axis=1, keepdims=True)
        small = small + jnp.where(lane == row, column, 0.0)
    embed_ref[...] = wide[0:3, 0:KINDS]
    gain_ref[...] = small[KINDS : KINDS + 2, 0:3]
    for block in range(16):
        bias_s[12 * block : 12 * block + 12, :] = bias_ref[block // 8, block % 8, 0:12, :] * factor
    for row in range(HI):
        width = min(LANES, PAIRS - row * LANES)
        line = bias_s[pl.ds(row, HEADS, stride=32), :][:, 0:width]
        for head in range(HEADS):
            table_ref[head, :, row * LANES : row * LANES + width] = line[head : head + 1]
    for quarter in range(4):
        packed = back_ref[quarter].astype(F32)
        for tile in range(3):
            back_s[quarter, 0:CELLS, tile * LANES : (tile + 1) * LANES] = packed[CELLS * tile : CELLS * tile + CELLS]
        for i in range(3):
            row, half = 3 * (quarter // 2) + i, quarter % 2
            token_s[row, 6 * half : 6 * half + 6, :] = back_s[quarter, 6 * i : 6 * i + 6, :]
    for row in range(WIN_LAT):
        token_ref[row] = token_s[row, 0:WIN_LON, :].astype(BF16)


def outputs(dense, bias, back, total):
    vmem = pl.BlockSpec(memory_space=pltpu.VMEM)
    return pl.pallas_call(
        output_kernel,
        out_shape=(
            jax.ShapeDtypeStruct((WIN_LAT, WIN_LON, 2 * C), BF16),
            jax.ShapeDtypeStruct((3, 3 * C), F32),
            jax.ShapeDtypeStruct((3, C), F32),
            jax.ShapeDtypeStruct((3, FF), F32),
            jax.ShapeDtypeStruct((12, C), F32),
            jax.ShapeDtypeStruct((2, 3), F32),
            jax.ShapeDtypeStruct((3, KINDS), F32),
            jax.ShapeDtypeStruct((HEADS, 1, PAIRS), F32),
        ),
        in_specs=[vmem] * 4,
        out_specs=(vmem,) * 8,
        scratch_shapes=[
            pltpu.VMEM((2, 64, LANES), F32),
            pltpu.VMEM((8, COLS), F32),
            pltpu.VMEM((HEADS * 32, LANES), F32),
            pltpu.VMEM((4, 32, 2 * C), F32),
            pltpu.VMEM((WIN_LAT, 16, 2 * C), F32),
        ],
        compiler_params=pltpu.CompilerParams(vmem_limit_bytes=VMEM_LIMIT),
        name="scaled_outputs",
    )(dense, bias, back, total)


def shards(
    tokens, kinds, kind_embed, pair_index, bias_table, attn_gain, mlp_gain,
    mix_weight, out_weight, up_weight, down_weight, cotangent,
):
    sums = main(
        tokens, kinds.transpose(0, 2, 1), kind_embed, cotangent, pair_index, bias_table.transpose(1, 0, 2),
        attn_gain.reshape(1, C), mlp_gain.reshape(1, C), mix_weight, out_weight, up_weight, down_weight.T,
    )
    token, mix, out, up, down, gain, embed, table = outputs(*sums)
    return token, mix, out, up, down, gain, embed.T, table.transpose(1, 0, 2)


def solution(mesh):
    return jax.shard_map(
        shards,
        mesh=mesh,
        in_specs=(
            P("lat", "lon", None),
            P("lat", "lon", None),
            P(),
            P(),
            P("lat", None, None),
            P(),
            P(),
            P(),
            P(),
            P(),
            P(),
            P("lat", "lon", None),
        ),
        out_specs=(
            P("lat", "lon", None),
            P("lon", None),
            P("lon", None),
            P("lon", None),
            P("lon", None),
            P(None, "lon"),
            P(None, "lon"),
            P("lat", None, None),
        ),
        check_vma=False,
    )
```

```python
import jax
import jax.numpy as jnp
import numpy as np
from jax import lax
from jax.experimental import pallas as pl
from jax.experimental.pallas import tpu as pltpu
from jax.sharding import PartitionSpec as P

F32 = jnp.float32
BF16 = jnp.bfloat16
MESH = pl.DeviceIdType.MESH

C = 192
HEADS = 6
HEAD = 32
FF = 768
WIN_LAT = 6
WIN_LON = 12
KINDS = 16
PAIRS = 3312
TOK = 144
CELLS = 18
PART = 36
LANES = 128
HI = 26
COLS = 2304
TILES = 18
NORM_EPS = 1e-05
RMS_EPS = 1e-06
GELU_SQRT = 0.7978845608028654
GELU_CUBE = 0.044715
LON, LAT = 64, 8
FIXED = 8191.0
ZLO = 8
VMEM_LIMIT = 56 * 1024 * 1024


def coords(lat, lon):
    return lat >> 1, lon >> 4, ((lat & 1) << 3) + ((lon >> 1) & 7), lon & 1


def at(x, y, z, core):
    return {"lon": (y << 4) + ((z & 7) << 1) + core, "lat": (x << 1) + (z >> 3)}


def beside(lat, lon, rows, columns):
    return {"lon": (lon + columns) & (LON - 1), "lat": (lat + rows) & (LAT - 1)}


def dot(a, b):
    return lax.dot_general(a, b, (((1,), (0,)), ((), ())), preferred_element_type=F32)


def dot_nt(a, b):
    return lax.dot_general(a, b, (((1,), (1,)), ((), ())), preferred_element_type=F32)


def dot_tn(a, b):
    return lax.dot_general(a, b, (((0,), (0,)), ((), ())), preferred_element_type=F32)


def two_terms(v):
    high = v.astype(BF16)
    return high, (v - high.astype(F32)).astype(BF16)


def dense_rows(ref, values, base):
    ref[base : base + TOK, :] = values[:, 0:LANES]
    tail = values[:, LANES:TOK]
    tail = jnp.concatenate([tail, jnp.zeros((TOK, LANES - 16), tail.dtype)], axis=1)
    row = tail[0:16]
    for group in range(1, 8):
        row = row + pltpu.roll(tail[16 * group : 16 * group + 16], 16 * group, 1)
    ref[base + TOK : base + TOK + 16, :] = row
    ref[base + TOK + 16 : base + TOK + 32, :] = tail[LANES:TOK]


DENSE = TOK + 32
FLAT = 3 * PART
SENT = FLAT + 4


def layer_norm(values, gain):
    centred = values - jnp.mean(values, axis=-1, keepdims=True)
    inverse = lax.rsqrt(jnp.mean(centred * centred, axis=-1, keepdims=True) + NORM_EPS)
    normed = centred * inverse
    return normed * gain, normed, inverse


def norm_backward(upstream, normed, inverse, gain):
    scaled = upstream * gain
    return inverse * (
        scaled
        - jnp.mean(scaled, axis=-1, keepdims=True)
        - normed * jnp.mean(scaled * normed, axis=-1, keepdims=True)
    )


def main_kernel(
    tok_in, kind_in, embed_in, cot_in, index_in, table_in, order_in,
    gain1_in, gain2_in, mix_in, outw_in, up_in, down_in,
    dense_out, bias_out, back_out, total_out,
    tok_ref, kind_ref, embed_ref, cot_ref, index_ref, table_ref, order_ref,
    gain1_ref, gain2_ref, mix_ref, outw_ref, up_ref, down_ref,
    tok_s, kind_s, flat_s, pack_s, send, recv, table_s, pairs_s, dense_s, high_s, low_s, bias_s, spread_s,
    grid_s, x_s, g_s, hot_s, ge_s, moved_s, unpack_s, score_s, extra_s, back_s,
    grad_s, rows_s, grads, acc_s, parts_s,
    core_r, plane_s, plane_r, line_s, line_r, share, bline_s, bline_r, brow_r, ball, back_r, squares_z, squares_y,
    in_sems, halo_ss, halo_rs,
    core_ss, core_rs, plane_ss, plane_rs, line_ss, line_rs, share_ss, share_rs, bline_ss, bline_rs,
    brow_ss, brow_rs, ball_ss, ball_rs, bpair_ss, bpair_rs, back_ss, back_rs, sz_ss, sz_rs, sy_ss, sy_rs,
):
    lon, lat = lax.axis_index("lon"), lax.axis_index("lat")
    x, y, z, core = coords(lat, lon)
    z_lo, z_hi = z & 7, z >> 3
    other = 1 - core

    def remote(src, dst, send_sem, recv_sem, target):
        return pltpu.make_async_remote_copy(
            src_ref=src, dst_ref=dst, send_sem=send_sem, recv_sem=recv_sem, device_id=target, device_id_type=MESH
        )

    sources = (
        tok_in, kind_in, embed_in, cot_in, index_in, table_in, order_in,
        gain1_in, gain2_in, mix_in, outw_in, up_in, down_in,
    )
    targets = (
        tok_ref, kind_ref, embed_ref, cot_ref, index_ref, table_ref, order_ref,
        gain1_ref, gain2_ref, mix_ref, outw_ref, up_ref, down_ref,
    )
    fetches = [pltpu.make_async_copy(s, t, in_sems.at[i]) for i, (s, t) in enumerate(zip(sources, targets))]
    for fetch in fetches[:4]:
        fetch.start()

    barrier = pltpu.get_barrier_semaphore()
    peers = []
    for dr, dc in ((1, 0), (0, 1), (1, 1)):
        peers += [beside(lat, lon, -dr, -dc), beside(lat, lon, dr, dc)]
    peers += [at(x, y, (z + d) & 15, core) for d in range(1, 16)]
    peers += [at((x + d // 4) & 3, (y + d % 4) & 3, z, core) for d in range(1, 16)]
    peers += [at((x + d // 4) & 3, (y + d % 4) & 3, z, other) for d in range(16)]
    peers += [at(x, y, z_hi * ZLO + ((z_lo + d) & 7), other) for d in range(1, ZLO)]
    for peer in peers:
        pl.semaphore_signal(barrier, inc=1, device_id=peer, device_id_type=MESH)

    for fetch in fetches[4:]:
        fetch.start()
    for fetch in fetches[:4]:
        fetch.wait()
    embed = embed_ref[...].astype(F32)
    blank = jnp.zeros((KINDS, C), F32)
    wide = jnp.concatenate(
        [jnp.concatenate([embed, blank], axis=1), jnp.concatenate([blank, embed], axis=1)], axis=0
    ).astype(BF16)
    kind_s[...] = jnp.zeros((4, 8, LANES), F32)
    for row in range(WIN_LAT):
        tok = tok_ref[row].astype(F32)
        cot = cot_ref[row].astype(F32)
        kind = kind_ref[row].astype(F32)
        for half in range(2):
            quarter = 2 * (row // 3) + half
            start = 6 * (row % 3)
            cells = slice(6 * half, 6 * half + 6)
            tok_s[quarter, start : start + 6, :] = tok[cells]
            flat_s[quarter, CELLS + start : CELLS + start + 6, :] = cot[cells]
            kind_s[quarter, 0:2, start : start + 6] = kind[:, cells]
    sub = lax.broadcasted_iota(jnp.int32, (2 * KINDS, LANES), 0).astype(F32)
    for quarter in range(4):
        kinds = kind_s[quarter]
        hot = (sub == kinds[0:1]) | (sub - KINDS == kinds[1:2])
        hot = jnp.where(hot, 1.0, 0.0).astype(BF16)[:, 0:24]
        stored = tok_s[quarter] + dot_tn(hot, wide)
        flat_s[quarter, 0:CELLS, :] = stored[0:CELLS]
        for tile in range(3):
            pack_s[quarter, PART * tile : PART * tile + PART, :] = flat_s[
                quarter, 0:PART, tile * LANES : (tile + 1) * LANES
            ]
        pack_s[quarter, FLAT:SENT, :] = jnp.zeros((4, LANES), F32)
        pack_s[quarter, FLAT : FLAT + 1, :] = kinds[0:1] + pltpu.roll(kinds, CELLS, 1)[1:2]
        send[quarter] = pack_s[quarter].astype(BF16)
    pl.semaphore_wait(barrier, len(peers))
    halo_copies = []
    for slot in (3, 2, 1):
        copy = remote(
            send.at[3 - slot], recv.at[slot], halo_ss.at[slot], halo_rs.at[slot], beside(lat, lon, -(slot // 2), -(slot % 2))
        )
        copy.start()
        halo_copies.append(copy)
    sends = list(halo_copies)

    for fetch in fetches[4:7]:
        fetch.wait()
    order = order_ref[...]
    index = index_ref[...]
    high = (index >> 7).astype(F32).astype(BF16)
    low = (index & (LANES - 1)).astype(F32).astype(BF16)
    dense_rows(high_s, dot_nt(dot(order, high).astype(BF16), order), 0)
    dense_rows(low_s, dot_nt(dot(order, low).astype(BF16), order), 0)
    table_s[...] = jnp.zeros((HEADS * 32, LANES), F32)
    for row in range(HI):
        width = min(LANES, PAIRS - row * LANES)
        for head in range(HEADS):
            table_s[32 * head + row : 32 * head + row + 1, 0:width] = table_ref[
                head, :, row * LANES : row * LANES + width
            ]

    column = lax.broadcasted_iota(jnp.int32, (1, FF), 1)
    part = jnp.where(column >= C, 1, 0) + jnp.where(column >= 2 * C, 1, 0) + jnp.where(column >= 3 * C, 1, 0)
    unit = (4 * (column - C * part) + part).astype(F32)
    for block in range(6):
        place_at = (lax.broadcasted_iota(jnp.int32, (LANES, FF), 0) + LANES * block).astype(F32)
        spread_s[LANES * block : LANES * (block + 1), :] = jnp.where(place_at == unit, 1.0, 0.0).astype(BF16)

    for pair in range(3):
        fixed = [
            ((table_s[64 * pair + 32 * k : 64 * pair + 32 * k + 32, :] + 4.0) * FIXED + 0.5).astype(jnp.int32) for k in range(2)
        ]
        pairs_s[32 * pair : 32 * pair + 32, :] = (fixed[0] << 16) | fixed[1]

    def gather(step, carry):
        start = pl.multiple_of(step * 16, 16)
        lows = low_s[pl.ds(start, 16), :].astype(jnp.int32)
        highs = high_s[pl.ds(start, 16), :]
        totals = [jnp.zeros((16, LANES), jnp.int32) for _ in range(3)]
        for row in range(HI):
            chosen = highs == float(row)
            for pair in range(3):
                line = jnp.broadcast_to(pairs_s[32 * pair + row : 32 * pair + row + 1, :], (16, LANES))
                found = jnp.take_along_axis(line, lows, axis=1, mode="promise_in_bounds")
                totals[pair] = jnp.where(chosen, found, totals[pair])
        for head in range(HEADS):
            fixed = totals[head // 2]
            fixed = (fixed if head % 2 else fixed >> 16) & 0xFFFF
            dense_s[pl.ds(pl.multiple_of(head * DENSE + start, 16), 16), :] = fixed.astype(F32) * (1.0 / FIXED) - 4.0
        return carry

    lax.fori_loop(0, DENSE // 16, gather, 0)
    for head in range(HEADS):
        base = head * DENSE
        bias_s[head * TOK : head * TOK + TOK, 0:LANES] = dense_s[base : base + TOK, :]
        row = dense_s[base + TOK : base + TOK + 16, :]
        for group in range(8):
            turned = row if group == 0 else pltpu.roll(row, LANES - 16 * group, 1)
            bias_s[head * TOK + 16 * group : head * TOK + 16 * group + 16, LANES:TOK] = turned[:, 0:16]
        bias_s[head * TOK + LANES : head * TOK + TOK, LANES:TOK] = dense_s[base + TOK + 16 : base + TOK + 32, 0:16]

    for copy in halo_copies:
        copy.wait_recv()
    lane36 = lax.broadcasted_iota(jnp.int32, (PART, LANES), 1)
    sub36 = lax.broadcasted_iota(jnp.int32, (PART, LANES), 0)
    for slot in range(4):
        unpack_s[slot] = (send[3] if slot == 0 else recv[slot]).astype(F32)
        for tile in range(3):
            grid_s[slot, 0:PART, tile * LANES : (tile + 1) * LANES] = unpack_s[slot, PART * tile : PART * tile + PART, :]
        toks = grid_s[slot, 0:CELLS, :]
        cots = grid_s[slot, CELLS:PART, :]
        base = PART * slot
        x_s[base : base + CELLS, :] = toks[:, 0:C]
        x_s[base + CELLS : base + PART, :] = toks[:, C : 2 * C]
        g_s[base : base + CELLS, :] = cots[:, 0:C]
        g_s[base + CELLS : base + PART, :] = cots[:, C : 2 * C]
        kind_row = unpack_s[slot, FLAT : FLAT + 1, :]
        kind_col = jnp.sum(jnp.where(lane36 == sub36, kind_row, 0.0), axis=1, keepdims=True)
        hot_s[base : base + PART, :] = jnp.where(lane36.astype(F32) == kind_col, 1.0, 0.0)

    for fetch in fetches[7:]:
        fetch.wait()
    gain1, gain2 = gain1_ref[...], gain2_ref[...]
    mix_weight, out_weight = mix_ref[...], outw_ref[...]
    up_weight, down_weight = up_ref[...], down_ref[...]
    residual = x_s[...]
    upstream = g_s[...]
    upstream_low = upstream.astype(BF16)
    first, hat1, inv1 = layer_norm(residual, gain1)
    first_in = first.astype(BF16)
    mixed = dot(first_in, mix_weight)
    queries = mixed[:, 0:C].astype(BF16).astype(F32)
    keys = mixed[:, C : 2 * C].astype(BF16)
    values = mixed[:, 2 * C : 3 * C].astype(BF16)
    channel = lax.broadcasted_iota(jnp.int32, (TOK, C), 1)
    of_head = [(channel >= HEAD * n) & (channel < HEAD * n + HEAD) for n in range(HEADS)]
    q_stack = jnp.concatenate([jnp.where(m, queries, 0.0) for m in of_head], axis=0).astype(BF16)
    scores = dot_nt(q_stack, keys) * (HEAD**-0.5) + bias_s[...]
    last = lat == LAT - 1
    group_q = jnp.where(lax.broadcasted_iota(jnp.int32, (TOK, TOK), 0) >= 72, 1.0, 0.0)
    group_k = jnp.where(lax.broadcasted_iota(jnp.int32, (TOK, TOK), 1) >= 72, 1.0, 0.0)
    apart = jnp.abs(group_q - group_k) * jnp.where(last, 1.0, 0.0)
    allowed = jnp.concatenate([apart] * HEADS, axis=0) < 0.5
    expon = jnp.where(allowed, jnp.exp(scores), 0.0)
    attend = expon * (1.0 / jnp.sum(expon, axis=-1, keepdims=True))
    attend_low = attend.astype(BF16)
    context = jnp.zeros((TOK, C), F32)
    for n in range(HEADS):
        context += jnp.where(of_head[n], dot(attend_low[n * TOK : (n + 1) * TOK], values), 0.0)
    context = context.astype(BF16)
    mid = residual + dot(context, out_weight)
    second, hat2, inv2 = layer_norm(mid, gain2)
    second_in = second.astype(BF16)
    inner = dot(second_in, up_weight)
    tangent = jnp.tanh(GELU_SQRT * (inner + GELU_CUBE * inner * inner * inner))
    hidden_low = (0.5 * inner * (1.0 + tangent)).astype(BF16)
    slope = 0.5 * (1.0 + tangent) + 0.5 * inner * (1.0 - tangent * tangent) * GELU_SQRT * (
        1.0 + 3.0 * GELU_CUBE * inner * inner
    )
    hidden_grad = (dot(upstream_low, down_weight) * slope).astype(BF16)
    second_grad = dot_nt(hidden_grad, up_weight)
    mid_grad = upstream + norm_backward(second_grad, hat2, inv2, gain2)
    mid_low = mid_grad.astype(BF16)
    context_grad = dot_nt(mid_low, out_weight).astype(BF16).astype(F32)
    c_stack = jnp.concatenate([jnp.where(m, context_grad, 0.0) for m in of_head], axis=0).astype(BF16)
    attend_grad = dot_nt(c_stack, values)
    value_grad = dot_tn(attend_low, c_stack).astype(BF16)
    score_grad = attend * (attend_grad - jnp.sum(attend * attend_grad, axis=-1, keepdims=True))
    score_s[...] = score_grad
    score_low = score_grad.astype(BF16)
    query_grad = jnp.zeros((TOK, C), F32)
    for n in range(HEADS):
        query_grad += jnp.where(of_head[n], dot(score_low[n * TOK : (n + 1) * TOK], keys), 0.0)
    query_grad = (query_grad * (HEAD**-0.5)).astype(BF16)
    key_grad = (dot_tn(score_low, q_stack) * (HEAD**-0.5)).astype(BF16)
    first_grad = (
        dot_nt(query_grad, mix_weight[:, 0:C])
        + dot_nt(key_grad, mix_weight[:, C : 2 * C])
        + dot_nt(value_grad, mix_weight[:, 2 * C : 3 * C])
    )
    moved = mid_grad + norm_backward(first_grad, hat1, inv1, gain1)

    lane = lax.broadcasted_iota(jnp.int32, (TOK, LANES), 1)
    small = jnp.zeros((C, LANES), F32)
    for left, right in (
        (moved, hot_s[...]),
        (first_grad * hat1, jnp.where(lane == KINDS, 1.0, 0.0)),
        (second_grad * hat2, jnp.where(lane == KINDS + 1, 1.0, 0.0)),
    ):
        for term in two_terms(left):
            small += dot_tn(term, right.astype(BF16))
    ge_s[...] = small
    extra = jnp.zeros((32, LANES), F32)
    for k in range(6):
        line = ge_s[pl.ds(k, 32, stride=6), :]
        extra += pltpu.roll(line, 18 * k, 1) if k else line
    extra_s[...] = extra

    grad_s[:, 0:C] = dot_tn(first_in, query_grad)
    grad_s[:, C : 2 * C] = dot_tn(first_in, key_grad)
    grad_s[:, 2 * C : 3 * C] = dot_tn(first_in, value_grad)
    grad_s[:, 3 * C : 4 * C] = dot_tn(context, mid_low)
    grad_s[:, 4 * C : 8 * C] = dot_tn(second_in, hidden_grad)
    spread = dot(hidden_low, spread_s[...]).astype(BF16)
    for part in range(4):
        grad_s[:, (8 + part) * C : (9 + part) * C] = dot_tn(spread[:, part * C : (part + 1) * C], upstream_low)
    for tile in range(TILES):
        for part in range(4):
            rows_s[tile // 9, part, pl.ds(tile % 9, 48, stride=9), :] = grad_s[
                48 * part : 48 * part + 48, tile * LANES : (tile + 1) * LANES
            ]
    sub64 = lax.broadcasted_iota(jnp.int32, (64, LANES), 0)

    def blocks(half, part):
        for block in range(ZLO):
            got = rows_s[half, part, 54 * block : 54 * block + 64, :]
            line = extra_s[pl.ds(part * ZLO + block, 1), :] * jnp.where(half == 0, 1.0, 0.0)
            got = jnp.where(sub64 < 54, got, jnp.where(sub64 == 54, line, 0.0)).astype(BF16)
            for quarter in range(4):
                grads[half, part, quarter, block] = got[16 * quarter : 16 * quarter + 16]

    core_copies = []
    for j in range(4):
        to = (y + 1 + j) & 3
        blocks(other, to)
        copy = remote(grads.at[other, to], core_r.at[to], core_ss.at[j], core_rs.at[j], at(x, y, z, other))
        copy.start()
        core_copies.append(copy)
    sends += core_copies
    moved_s[...] = moved
    for slot in range(4):
        base = PART * slot
        grid_s[slot, 0:CELLS, 0:C] = moved_s[base : base + CELLS, :]
        grid_s[slot, 0:CELLS, C : 2 * C] = moved_s[base + CELLS : base + PART, :]
        for tile in range(3):
            unpack_s[slot, CELLS * tile : CELLS * tile + CELLS, :] = grid_s[
                slot, 0:CELLS, tile * LANES : (tile + 1) * LANES
            ]
        back_s[slot] = unpack_s[slot, 0:64, :].astype(BF16)

    back_copies = []
    for slot in (3, 2, 1):
        copy = remote(
            back_s.at[slot], back_r.at[3 - slot], back_ss.at[slot], back_rs.at[slot], beside(lat, lon, slot // 2, slot % 2)
        )
        copy.start()
        back_copies.append((slot, copy))
    sends += [copy for _, copy in back_copies]

    acc_s[...] = jnp.zeros((208, LANES), F32)
    for n in range(HEADS):
        dense_rows(dense_s, score_s[n * TOK : (n + 1) * TOK, :], n * DENSE)
    row32 = lax.broadcasted_iota(jnp.int32, (32, LANES), 0).astype(F32).astype(BF16)
    row128 = lax.broadcasted_iota(jnp.int32, (LANES, LANES), 0).astype(F32).astype(BF16)
    zero, one = jnp.zeros((), BF16), jnp.ones((), BF16)

    def low_rows(line, count):
        return jnp.concatenate([jnp.broadcast_to(line, (16, LANES)).astype(BF16)] * (count // 16), axis=0)

    def scatter(step, carry):
        left, right = [], []
        start = pl.multiple_of(step * 16, 16)
        highs, lows = high_s[pl.ds(start, 16), :], low_s[pl.ds(start, 16), :]
        scores = [dense_s[pl.ds(pl.multiple_of(n * DENSE + start, 16), 16), :] for n in range(HEADS)]
        for row in range(16):
            chosen = row32 == low_rows(highs[row : row + 1], 32)
            right.append(jnp.where(row128 == low_rows(lows[row : row + 1], LANES), one, zero))
            left.append(
                jnp.concatenate([jnp.where(chosen, low_rows(scores[n][row : row + 1], 32), zero) for n in range(HEADS)], axis=0)
            )
        acc_s[0 : 32 * HEADS, :] += dot_nt(jnp.concatenate(left, axis=1), jnp.concatenate(right, axis=1))
        return carry

    lax.fori_loop(0, 4, scatter, 0)

    plane_copies = {}
    for j in range(4):
        to_y = (y + 1 + j) & 3
        blocks(core, to_y)
        core_copies[j].wait_recv()
        for part in range(4):
            plane_s[to_y, part] = (grads[core, to_y, part].astype(F32) + core_r[to_y, part].astype(F32)).astype(BF16)
        for i in range(4):
            dx, dy = (i + 1) % 4, (j + 1) % 4
            d = dx * 4 + dy
            to_x = (x + dx) & 3
            if d == 0:
                plane_r[x * 4 + y] = plane_s[y, x]
                continue
            copy = remote(
                plane_s.at[to_y, to_x], plane_r.at[x * 4 + y], plane_ss.at[d], plane_rs.at[d], at(to_x, to_y, z, core)
            )
            copy.start()
            plane_copies[d] = copy
    sends += list(plane_copies.values())

    lax.fori_loop(4, DENSE // 16, scatter, 0)
    sub16 = lax.broadcasted_iota(jnp.int32, (16, LANES), 0)
    for block in range(16):
        parts_s[block // 8, block % 8] = jnp.where(sub16 < 12, acc_s[12 * block : 12 * block + 16, :], 0.0)

    bline_s[...] = parts_s[...].astype(BF16)
    bline_r[core, z_lo] = bline_s[core, z_lo]
    bline_copies = []
    for d in range(1, 16):
        to_core, to = core + (d >> 3) * (1 - 2 * core), (z_lo + d) & 7
        copy = remote(
            bline_s.at[to_core, to],
            bline_r.at[core, z_lo],
            bline_ss.at[d],
            bline_rs.at[d],
            at(x, y, z_hi * ZLO + to, to_core),
        )
        copy.start()
        bline_copies.append(copy)
    sends += bline_copies

    for copy in plane_copies.values():
        copy.wait_recv()
    for part in range(ZLO):
        block = plane_r[0, part].astype(F32)
        for source in range(1, 16):
            block = block + plane_r[source, part].astype(F32)
        line_s[part] = block.astype(BF16)
    line_r[z] = line_s[z_lo]
    line_copies = []
    for d in range(1, 16):
        to = (z + d) & 15
        copy = remote(line_s.at[to & 7], line_r.at[z], line_ss.at[d], line_rs.at[d], at(x, y, to, core))
        copy.start()
        line_copies.append(copy)
    sends += line_copies

    for copy in bline_copies:
        copy.wait_recv()
    part_sum = bline_r[0, 0].astype(F32)
    for part in range(1, 16):
        part_sum = part_sum + bline_r[part // ZLO, part % ZLO].astype(F32)
    brow_r[y] = part_sum
    brow_copies = []
    for d in range(1, 4):
        to = (y + d) & 3
        copy = remote(brow_r.at[y], brow_r.at[y], brow_ss.at[d], brow_rs.at[d], at(x, to, z, core))
        copy.start()
        brow_copies.append(copy)
    sends += brow_copies

    for copy in brow_copies:
        copy.wait_recv()
    bias_part = (brow_r[0] + brow_r[1]) + (brow_r[2] + brow_r[3])
    for copy in line_copies:
        copy.wait_recv()
    piece = line_r[0].astype(F32)
    for source in range(1, 16):
        piece = piece + line_r[source].astype(F32)
    square = 0.5 * jnp.sum(piece * piece) + 0.25 * jnp.sum(bias_part * bias_part)
    squares_z[z] = jnp.full((1, LANES), square, F32)
    sz_copies = []
    for d in range(1, 16):
        to = (z + d) & 15
        copy = remote(squares_z.at[z], squares_z.at[z], sz_ss.at[d], sz_rs.at[d], at(x, y, to, core))
        copy.start()
        sz_copies.append(copy)
    sends += sz_copies
    mine = core * 4 + x
    share[mine] = piece
    share_copies = []
    for dx, dcore in ((1, 0), (2, 0), (3, 0), (0, 1), (1, 1), (2, 1), (3, 1)):
        d = dcore * 4 + dx
        copy = remote(
            share.at[mine],
            share.at[mine],
            share_ss.at[d],
            share_rs.at[d],
            at((x + dx) & 3, y, z, core + dcore * (1 - 2 * core)),
        )
        copy.start()
        share_copies.append(copy)
    sends += share_copies
    ball[core, z_lo] = bias_part
    ball_copies = []
    for d in range(1, ZLO):
        to = (z_lo + d) & 7
        copy = remote(
            ball.at[core, z_lo], ball.at[core, z_lo], ball_ss.at[d], ball_rs.at[d], at(x, y, z_hi * ZLO + to, core)
        )
        copy.start()
        ball_copies.append(copy)
    sends += ball_copies

    for copy in sz_copies:
        copy.wait_recv()
    square = squares_z[0]
    for source in range(1, 16):
        square = square + squares_z[source]
    spot = core * 16 + x * 4 + y
    squares_y[spot] = square
    sy_copies = []
    for d in range(1, 32):
        target = at((x + (d >> 2 & 3)) & 3, (y + (d & 3)) & 3, z, core + (d >> 4) * (1 - 2 * core))
        copy = remote(squares_y.at[spot], squares_y.at[spot], sy_ss.at[d], sy_rs.at[d], target)
        copy.start()
        sy_copies.append(copy)
    sends += sy_copies
    for copy in ball_copies:
        copy.wait_recv()
    bpair = remote(ball.at[core], ball.at[core], bpair_ss, bpair_rs, at(x, y, z, other))
    bpair.start()
    sends.append(bpair)
    for copy in share_copies:
        copy.wait_recv()
    dense_out[...] = share[...]
    back_out[3] = back_s[0]
    for slot, copy in back_copies:
        copy.wait_recv()
        back_out[3 - slot] = back_r[3 - slot]
    for copy in sy_copies:
        copy.wait_recv()
    square = squares_y[0]
    for source in range(1, 32):
        square = square + squares_y[source]
    total_out[...] = square
    bpair.wait_recv()
    bias_out[...] = ball[...]
    for copy in sends:
        copy.wait_send()


def main(*operands):
    token = np.arange(TOK)
    slot, level, cell = token // PART, (token % PART) // CELLS, token % CELLS
    row, col = 3 * (slot // 2) + cell // 6, 6 * (slot % 2) + cell % 6
    order = np.zeros((TOK, TOK), np.float32)
    order[token, (row * WIN_LON + col) * 2 + level] = 1.0
    operands = operands[:6] + (jnp.asarray(order, BF16),) + operands[6:]
    vmem = pl.BlockSpec(memory_space=pltpu.VMEM)
    dma = pltpu.SemaphoreType.DMA
    return pl.pallas_call(
        main_kernel,
        out_shape=(
            jax.ShapeDtypeStruct((8, 16, LANES), F32),
            jax.ShapeDtypeStruct((2, ZLO, 16, LANES), F32),
            jax.ShapeDtypeStruct((4, 64, LANES), BF16),
            jax.ShapeDtypeStruct((1, LANES), F32),
        ),
        in_specs=[pl.BlockSpec(memory_space=pl.ANY)] * 13,
        out_specs=(vmem,) * 4,
        scratch_shapes=[pltpu.VMEM(v.shape, v.dtype) for v in operands] + [
            pltpu.VMEM((4, 24, 2 * C), F32),
            pltpu.VMEM((4, 8, LANES), F32),
            pltpu.VMEM((4, 40, 2 * C), F32),
            pltpu.VMEM((4, SENT, LANES), F32),
            pltpu.VMEM((4, SENT, LANES), BF16),
            pltpu.VMEM((4, SENT, LANES), BF16),
            pltpu.VMEM((HEADS * 32, LANES), F32),
            pltpu.VMEM((3 * 32, LANES), jnp.int32),
            pltpu.VMEM((HEADS * DENSE, LANES), F32),
            pltpu.VMEM((DENSE, LANES), F32),
            pltpu.VMEM((DENSE, LANES), F32),
            pltpu.VMEM((HEADS * TOK, TOK), F32),
            pltpu.VMEM((FF, FF), BF16),
            pltpu.VMEM((4, 40, 2 * C), F32),
            pltpu.VMEM((TOK, C), F32),
            pltpu.VMEM((TOK, C), F32),
            pltpu.VMEM((TOK, LANES), F32),
            pltpu.VMEM((C, LANES), F32),
            pltpu.VMEM((TOK, C), F32),
            pltpu.VMEM((4, SENT, LANES), F32),
            pltpu.VMEM((HEADS * TOK, TOK), F32),
            pltpu.VMEM((32, LANES), F32),
            pltpu.VMEM((4, 64, LANES), BF16),
            pltpu.VMEM((C, COLS), F32),
            pltpu.VMEM((2, 4, 448, LANES), F32),
            pltpu.VMEM((2, 4, 4, ZLO, 16, LANES), BF16),
            pltpu.VMEM((208, LANES), F32),
            pltpu.VMEM((2, ZLO, 16, LANES), F32),
            pltpu.VMEM((4, 4, ZLO, 16, LANES), BF16),
            pltpu.VMEM((4, 4, ZLO, 16, LANES), BF16),
            pltpu.VMEM((16, ZLO, 16, LANES), BF16),
            pltpu.VMEM((ZLO, 16, LANES), BF16),
            pltpu.VMEM((16, 16, LANES), BF16),
            pltpu.VMEM((8, 16, LANES), F32),
            pltpu.VMEM((2, ZLO, 16, LANES), BF16),
            pltpu.VMEM((2, ZLO, 16, LANES), BF16),
            pltpu.VMEM((4, 16, LANES), F32),
            pltpu.VMEM((2, ZLO, 16, LANES), F32),
            pltpu.VMEM((4, 64, LANES), BF16),
            pltpu.VMEM((16, 1, LANES), F32),
            pltpu.VMEM((32, 1, LANES), F32),
            dma((13,)),
            dma((4,)), dma((4,)),
            dma((4,)), dma((4,)),
            dma((16,)), dma((16,)),
            dma((16,)), dma((16,)),
            dma((8,)), dma((8,)),
            dma((16,)), dma((16,)),
            dma((4,)), dma((4,)),
            dma((8,)), dma((8,)),
            dma, dma,
            dma((4,)), dma((4,)),
            dma((16,)), dma((16,)),
            dma((32,)), dma((32,)),
        ],
        compiler_params=pltpu.CompilerParams(collective_id=0, has_side_effects=True, vmem_limit_bytes=VMEM_LIMIT),
        name="window_and_sums",
    )(*operands)


def output_kernel(
    dense_ref, bias_ref, back_ref, total_ref,
    token_ref, mix_ref, out_ref, up_ref, down_ref, gain_ref, embed_ref, table_ref,
    dense_s, flat_s, bias_s, back_s, token_s,
):
    count = C * COLS + (KINDS + 2) * C + LAT * HEADS * PAIRS
    factor = lax.rsqrt(total_ref[...] / count + RMS_EPS)
    odd = lax.axis_index("lon") % 2 == 1
    for part in range(8):
        dense_s[part // 4, 16 * (part % 4) : 16 * (part % 4) + 16, :] = dense_ref[part] * factor
    for tile in range(TILES):
        half, t = tile // 9, tile % 9
        even_rows = dense_s[half, pl.ds(t, 3, stride=9), :]
        odd_rows = dense_s[half, pl.ds(27 + t, 3, stride=9), :]
        flat_s[0:3, tile * LANES : (tile + 1) * LANES] = jnp.where(odd, odd_rows, even_rows)
    flat = flat_s[0:3, :]
    mix_ref[...] = flat[:, 0 : 3 * C]
    out_ref[...] = flat[:, 3 * C : 4 * C]
    up_ref[...] = flat[:, 4 * C : 8 * C]
    for row in range(3):
        for part in range(4):
            down_ref[4 * row + part : 4 * row + part + 1, :] = flat[row : row + 1, (8 + part) * C : (9 + part) * C]
    extra = dense_s[0, 54:55, :]
    lane = lax.broadcasted_iota(jnp.int32, (24, LANES), 1)
    sub = lax.broadcasted_iota(jnp.int32, (24, LANES), 0)
    small = jnp.zeros((24, LANES), F32)
    wide = jnp.zeros((8, LANES), F32)
    sub8 = lax.broadcasted_iota(jnp.int32, (8, LANES), 0)
    line8 = jnp.broadcast_to(extra, (8, LANES))
    for row in range(3):
        turned = jnp.where(odd, pltpu.roll(line8, LANES - 18 * (3 + row), 1), pltpu.roll(line8, (LANES - 18 * row) % LANES, 1))
        wide = jnp.where(sub8 == row, turned, wide)
        start = jnp.where(odd, 18 * (3 + row), 18 * row)
        column = jnp.sum(jnp.where(lane == sub + start, extra, 0.0), axis=1, keepdims=True)
        small = small + jnp.where(lane == row, column, 0.0)
    embed_ref[...] = wide[0:3, 0:KINDS]
    gain_ref[...] = small[KINDS : KINDS + 2, 0:3]
    for block in range(16):
        bias_s[12 * block : 12 * block + 12, :] = bias_ref[block // 8, block % 8, 0:12, :] * factor
    for row in range(HI):
        width = min(LANES, PAIRS - row * LANES)
        line = bias_s[pl.ds(row, HEADS, stride=32), :][:, 0:width]
        for head in range(HEADS):
            table_ref[head, :, row * LANES : row * LANES + width] = line[head : head + 1]
    for quarter in range(4):
        packed = back_ref[quarter].astype(F32)
        for tile in range(3):
            back_s[quarter, 0:CELLS, tile * LANES : (tile + 1) * LANES] = packed[CELLS * tile : CELLS * tile + CELLS]
        for i in range(3):
            row, half = 3 * (quarter // 2) + i, quarter % 2
            token_s[row, 6 * half : 6 * half + 6, :] = back_s[quarter, 6 * i : 6 * i + 6, :]
    for row in range(WIN_LAT):
        token_ref[row] = token_s[row, 0:WIN_LON, :].astype(BF16)


def outputs(dense, bias, back, total):
    vmem = pl.BlockSpec(memory_space=pltpu.VMEM)
    return pl.pallas_call(
        output_kernel,
        out_shape=(
            jax.ShapeDtypeStruct((WIN_LAT, WIN_LON, 2 * C), BF16),
            jax.ShapeDtypeStruct((3, 3 * C), F32),
            jax.ShapeDtypeStruct((3, C), F32),
            jax.ShapeDtypeStruct((3, FF), F32),
            jax.ShapeDtypeStruct((12, C), F32),
            jax.ShapeDtypeStruct((2, 3), F32),
            jax.ShapeDtypeStruct((3, KINDS), F32),
            jax.ShapeDtypeStruct((HEADS, 1, PAIRS), F32),
        ),
        in_specs=[vmem] * 4,
        out_specs=(vmem,) * 8,
        scratch_shapes=[
            pltpu.VMEM((2, 64, LANES), F32),
            pltpu.VMEM((8, COLS), F32),
            pltpu.VMEM((HEADS * 32, LANES), F32),
            pltpu.VMEM((4, 32, 2 * C), F32),
            pltpu.VMEM((WIN_LAT, 16, 2 * C), F32),
        ],
        compiler_params=pltpu.CompilerParams(vmem_limit_bytes=VMEM_LIMIT),
        name="scaled_outputs",
    )(dense, bias, back, total)


def shards(
    tokens, kinds, kind_embed, pair_index, bias_table, attn_gain, mlp_gain,
    mix_weight, out_weight, up_weight, down_weight, cotangent,
):
    sums = main(
        tokens, kinds.transpose(0, 2, 1), kind_embed, cotangent, pair_index, bias_table.transpose(1, 0, 2),
        attn_gain.reshape(1, C), mlp_gain.reshape(1, C), mix_weight, out_weight, up_weight, down_weight.T,
    )
    token, mix, out, up, down, gain, embed, table = outputs(*sums)
    return token, mix, out, up, down, gain, embed.T, table.transpose(1, 0, 2)


def solution(mesh):
    return jax.shard_map(
        shards,
        mesh=mesh,
        in_specs=(
            P("lat", "lon", None),
            P("lat", "lon", None),
            P(),
            P(),
            P("lat", None, None),
            P(),
            P(),
            P(),
            P(),
            P(),
            P(),
            P("lat", "lon", None),
        ),
        out_specs=(
            P("lat", "lon", None),
            P("lon", None),
            P("lon", None),
            P("lon", None),
            P("lon", None),
            P(None, "lon"),
            P(None, "lon"),
            P("lat", None, None),
        ),
        check_vma=False,
    )
```
